512 devices in a mesh: dp: 32 (over x_hi, z), space: 16 (over x_lo, y, core).
Axes of the slice: x: 4 (x_hi: 2, x_lo: 2; x = x_hi * 2 + x_lo), y: 4, z: 16, core: 2. Of those that a mesh axis runs over, the one named last changes fastest.
Arguments:
- volume: bfloat16 [32, 96, 32, 2, 256], P('dp', None, 'space'), may hold values from -6 to 6
- first_weight: bfloat16 [27, 4, 24, 24], replicated, may hold values from -0.25 to 0.25
- second_weight: bfloat16 [27, 96, 192], replicated, may hold values from -0.125 to 0.125
- out_cotangent: bfloat16 [32, 192, 16, 1, 128], P('dp', None, 'space'), may hold values from -6 to 6
Outputs:
- features: bfloat16 [32, 192, 16, 1, 128], P('dp', None, 'space')
- volume_grad: bfloat16 [32, 96, 32, 2, 256], P('dp', None, 'space')
- first_grad: float32 [27, 4, 24, 24], replicated
- second_grad: float32 [27, 96, 192], replicated
The draws below stay inside these ranges and needn't reach their ends.
All inputs are finite; a program needn't handle non-finite values.
Results may differ from the reference program's by a relative error of at most 0.0049.
Values may be sent and summed in bfloat16 or wider, within the bound.
No kernel may reach another device: no remote copies, remote signals or barrier semaphores. Data moves between devices by JAX's collectives and lax.ppermute only.
A program may use at most 64 MiB of HBM per device.

```python
import math
import jax
import jax.numpy as jnp
from jax import lax

CH = 96
CH_OUT = 192
GROUPS = 4
NY = 2
NZ = 256
BATCH = 32
NX = 32


def steps_of(stream_key, shape, split, smallest, largest):
    level = 1.0
    for axis_at, shards_of in split:
        draws = jax.random.uniform(jax.random.fold_in(jax.random.fold_in(stream_key, 6), axis_at), (shards_of,), jnp.float32, smallest / len(split), largest / len(split))
        level = level * jnp.repeat(jnp.exp(draws), shape[axis_at] // shards_of).reshape((-1,) + (1,) * (len(shape) - 1 - axis_at))
    return level


def noise(key, shape, deviation, limit, cuts=(), dtype=jnp.bfloat16):
    values = jax.random.normal(key, shape, jnp.float32) * deviation
    if len(cuts) > 0:
        values = steps_of(key, shape, cuts, -0.22, 0.18) * values
    return jnp.clip(values, min=-limit, max=limit).astype(dtype)


def setup_inputs(seed: int = 0) -> dict:
    splits = jax.random.split(jax.random.key(seed), 5)
    volume = noise(splits[0], (BATCH, CH, NX, NY, NZ), 1.0, 6.0, ((0, 32), (2, 16)))
    first_weight = noise(splits[1], (27, GROUPS, CH // GROUPS, CH // GROUPS), (27 * CH // GROUPS) ** -0.5, 0.25)
    second_weight = noise(splits[2], (27, CH, CH_OUT), (27 * CH) ** -0.5, 0.125)
    out_cotangent = noise(splits[3], (BATCH, CH_OUT, NX // 2, NY // 2, NZ // 2), 1.0, 6.0, ((0, 32), (2, 16)))
    return {"volume": volume, "first_weight": first_weight, "second_weight": second_weight, "out_cotangent": out_cotangent}


offsets = [(off_x, off_y, off_z) for off_x in range(3) for off_y in range(3) for off_z in range(3)]

def silu_slope(values):
    sigma = jax.nn.sigmoid(values)
    return sigma * (1.0 + values * (1.0 - sigma))

def grouped(block, groups):
    return block.reshape(groups, block.shape[0] // groups, -1)

def strided(padded, off_x, off_y, off_z, out_x, out_y, out_z):
    channels = padded.shape[0]
    return lax.slice(padded, (0, off_x, off_y, off_z), (channels, off_x + 2 * out_x - 1, off_y + 2 * out_y - 1, off_z + 2 * out_z - 1), (1, 2, 2, 2))

def alternate(parity):
    layers = []
    for bit_x in (0, 1):
        rows = []
        for bit_y in (0, 1):
            rows.append(jnp.stack([parity[bit_x, bit_y, 0], parity[bit_x, bit_y, 1]], axis=4))
        layers.append(jnp.stack(rows, axis=3))
    merged = jnp.stack(layers, axis=2)
    extent = merged.shape
    return merged.reshape(extent[0], 2 * extent[1], 2 * extent[3], 2 * extent[5])

def first_layer(padded, weight, planes, cells_y, cells_z):
    channels = padded.shape[0]
    groups = weight.shape[1]
    summed = jnp.zeros((groups, channels // groups, planes * cells_y * cells_z), jnp.float32)
    for tap_index, (off_x, off_y, off_z) in enumerate(offsets):
        window = grouped(padded[:, off_x:off_x + planes, off_y:off_y + cells_y, off_z:off_z + cells_z], groups)
        summed = summed + jnp.einsum('gio,gin->gon', weight[tap_index].astype(jnp.float32), window.astype(jnp.float32))
    return summed.reshape(channels, planes, cells_y, cells_z)

def second_layer(hid_pad, weight, out_x, out_y, out_z):
    summed = jnp.zeros((weight.shape[2], out_x * out_y * out_z), jnp.float32)
    for tap_index, (off_x, off_y, off_z) in enumerate(offsets):
        window = strided(hid_pad, off_x, off_y, off_z, out_x, out_y, out_z).reshape(hid_pad.shape[0], -1)
        summed = summed + jnp.einsum('co,cn->on', weight[tap_index].astype(jnp.float32), window.astype(jnp.float32))
    return summed.reshape(weight.shape[2], out_x, out_y, out_z)

def second_backward(hid_pad, weight, cotangent):
    channels = hid_pad.shape[0]
    out_x, out_y, out_z = (cotangent.shape[1], cotangent.shape[2], cotangent.shape[3])
    flat_cot = cotangent.reshape(cotangent.shape[0], -1).astype(jnp.float32)
    grads = []
    parity = {}
    for tap_index, (off_x, off_y, off_z) in enumerate(offsets):
        window = strided(hid_pad, off_x, off_y, off_z, out_x, out_y, out_z).reshape(channels, -1)
        grads.append(jnp.einsum('cn,on->co', window.astype(jnp.float32), flat_cot))
        spread = jnp.einsum('co,on->cn', weight[tap_index].astype(jnp.float32), flat_cot).reshape(channels, out_x, out_y, out_z)
        spread = jnp.pad(spread, ((0, 0), (off_x // 2, 1 - off_x // 2), (off_y // 2, 1 - off_y // 2), (off_z // 2, 1 - off_z // 2)))
        bucket = (off_x % 2, off_y % 2, off_z % 2)
        parity[bucket] = parity[bucket] + spread if bucket in parity else spread
    return (jnp.stack(grads), alternate(parity))

def first_backward(padded, grad_pad, weight, planes, cells_y, cells_z):
    channels = padded.shape[0]
    groups = weight.shape[1]
    grads = []
    back = jnp.zeros((groups, channels // groups, planes * cells_y * cells_z), jnp.float32)
    centre = grouped(grad_pad[:, 1:1 + planes, 1:1 + cells_y, 1:1 + cells_z], groups).astype(jnp.float32)
    for tap_index, (off_x, off_y, off_z) in enumerate(offsets):
        window_x = grouped(padded[:, off_x:off_x + planes, off_y:off_y + cells_y, off_z:off_z + cells_z], groups).astype(jnp.float32)
        window_g = grouped(grad_pad[:, 2 - off_x:2 - off_x + planes, 2 - off_y:2 - off_y + cells_y, 2 - off_z:2 - off_z + cells_z], groups).astype(jnp.float32)
        grads.append(jnp.einsum('gin,gon->gio', window_x, centre))
        back = back + jnp.einsum('gio,gon->gin', weight[tap_index].astype(jnp.float32), window_g)
    return (jnp.stack(grads), back.reshape(channels, planes, cells_y, cells_z))

def one_sample(sample, cotangent, first_weight, second_weight):
    planes, cells_y, cells_z = (sample.shape[1], sample.shape[2], sample.shape[3])
    padded = jnp.pad(sample, ((0, 0), (1, 1), (1, 1), (1, 1)))
    pre = first_layer(padded, first_weight, planes, cells_y, cells_z)
    hidden = jax.nn.silu(pre).astype(jnp.bfloat16)
    hid_pad = jnp.pad(hidden, ((0, 0), (1, 0), (1, 1), (1, 1)))
    features = second_layer(hid_pad, second_weight, planes // 2, cells_y // 2, cells_z // 2).astype(jnp.bfloat16)
    second_grad, spread = second_backward(hid_pad, second_weight, cotangent)
    hidden_grad = spread[:, 1:planes + 1, 1:cells_y + 1, 1:cells_z + 1]
    pre_grad = (hidden_grad * silu_slope(pre)).astype(jnp.bfloat16)
    grad_pad = jnp.pad(pre_grad, ((0, 0), (1, 1), (1, 1), (1, 1)))
    first_grad, volume_grad = first_backward(padded, grad_pad, first_weight, planes, cells_y, cells_z)
    return (features, volume_grad.astype(jnp.bfloat16), first_grad, second_grad)

def reference(volume, first_weight, second_weight, out_cotangent):

    def visit(carry, items):
        features, volume_grad, first_grad, second_grad = one_sample(items[0], items[1], first_weight, second_weight)
        return ((carry[0] + first_grad, carry[1] + second_grad), (features, volume_grad))
    zeros_pair = (jnp.zeros(first_weight.shape, jnp.float32), jnp.zeros(second_weight.shape, jnp.float32))
    totals, stacked = lax.scan(visit, zeros_pair, (volume, out_cotangent))
    factor = 1.0 / math.sqrt(BATCH * (NX // 2) * (NY // 2) * (NZ // 2))
    return (stacked[0], stacked[1], totals[0] * factor, totals[1] * factor)
```

```python
import math

import jax
import jax.numpy as jnp
import numpy as np
from jax import lax
from jax.experimental import pallas as pl
from jax.experimental.pallas import tpu as pltpu
from jax.sharding import Mesh
from jax.sharding import PartitionSpec as P

SPACE = ("xl", "y", "core")
DP = ("xh", "z")
NEAR = ("xh", "xl", "y", "core")
F32 = jnp.float32
BF16 = jnp.bfloat16

CH = 96
PG = 24
WIN = 9 * CH
LANES = 128
PIECES = 32
S_ROWS = 4096
F_ROWS = 768
S_PIECE = S_ROWS // PIECES
F_PIECE = F_ROWS // PIECES


def dot(a, b):
    return lax.dot_general(a, b, (((1,), (0,)), ((), ())), preferred_element_type=F32)


def dot_nt(a, b):
    return lax.dot_general(a, b, (((1,), (1,)), ((), ())), preferred_element_type=F32)


def dot_tn(a, b):
    return lax.dot_general(a, b, (((0,), (0,)), ((), ())), preferred_element_type=F32)


def later(tile):
    lane = lax.broadcasted_iota(jnp.int32, tile.shape, 1)
    return jnp.where(lane == 0, 0.0, pltpu.roll(tile, 1, 1))


def earlier(tile):
    lane = lax.broadcasted_iota(jnp.int32, tile.shape, 1)
    return jnp.where(lane == LANES - 1, 0.0, pltpu.roll(tile, LANES - 1, 1))


def fill_windows(ref, tiles):
    zero = jnp.zeros((CH, LANES), BF16)
    for b in range(3):
        for c in range(3):
            rows = pl.ds((b * 3 + c) * CH, CH)
            for y in range(2):
                source = y + b - 1
                if source in (0, 1):
                    even, odd, odd_later, even_earlier = tiles[source]
                    pair = ((odd_later, even), (even, odd), (odd, even_earlier))[c]
                else:
                    pair = (zero, zero)
                for parity in range(2):
                    ref[rows, pl.ds((2 * y + parity) * LANES, LANES)] = pair[parity]


def split_matrix():
    z = lax.broadcasted_iota(jnp.int32, (256, LANES), 0)
    k2 = 2 * lax.broadcasted_iota(jnp.int32, (256, LANES), 1)
    return jnp.concatenate(
        [jnp.where(z == k2 + off, 1.0, 0.0).astype(BF16) for off in (0, 1, -1, 2)], axis=1
    )


def merge_matrix():
    lane = lax.broadcasted_iota(jnp.int32, (LANES, 256), 0)
    z = lax.broadcasted_iota(jnp.int32, (LANES, 256), 1)
    return jnp.concatenate(
        [jnp.where(z == 2 * lane + bit, 1.0, 0.0).astype(BF16) for bit in (0, 1)], axis=0
    )


def expand(narrow, fold, mask):
    return (dot(narrow, fold) * mask).astype(BF16)


def forward_kernel(
    inner_ref, low_ref, own_ref, high_ref, fw_ref, fold_ref, mask_ref, cot_ref,
    sg_ref, pre_ref, xc_ref, wn_ref, xs, w1,
):
    inner = inner_ref[0]
    split = split_matrix()
    mask = mask_ref[...].astype(F32)
    for a in range(3):
        w1[pl.ds(a * CH, CH), :] = expand(fw_ref[pl.ds(a * CH, CH), :], fold_ref[...], mask)
    for e in range(6):
        plane_ref = (low_ref, own_ref, high_ref)[e // 2].at[e % 2]
        tiles = []
        for y in range(2):
            parts = dot(plane_ref[:, pl.ds(y * 256, 256)], split).astype(BF16)
            tiles.append([parts[:, q * LANES : (q + 1) * LANES] for q in range(4)])
            if 1 <= e <= 4:
                xc_ref[e - 1, :, pl.ds(y * 256, 256)] = parts[:, :256]
        fill_windows(xs.at[e], tiles)
    for e in range(6):
        first, last = max(0, e - 3), min(2, e)
        terms = dot(w1[pl.ds(first * CH, (last - first + 1) * CH), :], xs[e])
        for a in range(first, last + 1):
            term = terms[(a - first) * CH : (a - first + 1) * CH]
            j = e - a
            if a == 0:
                pre_ref[j] = term
            else:
                pre_ref[j] += term
    zero = jnp.zeros((CH, LANES), BF16)
    for a in range(3):
        for c in range(3):
            wn_ref[pl.ds((9 * a + c) * CH, CH), :] = zero
        for y in range(2):
            value = pre_ref[a, :, pl.ds(y * 256, 256)]
            hidden = value * jax.nn.sigmoid(value)
            if a == 0:
                hidden = hidden * inner
            even, odd = hidden[:, :LANES], hidden[:, LANES:]
            base = (9 * a + 3 * (y + 1)) * CH
            wn_ref[pl.ds(base, CH), :] = later(odd).astype(BF16)
            wn_ref[pl.ds(base + CH, CH), :] = even.astype(BF16)
            wn_ref[pl.ds(base + 2 * CH, CH), :] = odd.astype(BF16)
    cot = cot_ref[...]
    rows = 27 * CH
    half = rows // 2
    sg_ref[pl.ds(0, rows), :] = dot_nt(wn_ref[...], cot[:LANES]).astype(BF16)
    rest = cot[LANES:]
    none = jnp.zeros_like(rest)
    both = jnp.concatenate(
        [jnp.concatenate([rest, none], axis=1), jnp.concatenate([none, rest], axis=1)], axis=0
    )
    pairs = jnp.concatenate([wn_ref[pl.ds(0, half), :], wn_ref[pl.ds(half, half), :]], axis=1)
    sg_ref[pl.ds(rows, half), :] = dot_nt(pairs, both).astype(BF16)
    sg_ref[pl.ds(rows + half, S_ROWS - rows - half), :] = jnp.zeros(
        (S_ROWS - rows - half, LANES), BF16
    )


def backward_kernel(
    inner_ref, pre_ref, xc_ref, wn_ref, w2_ref, below_ref, cot_ref, above_ref, fw_ref, fold_ref,
    flip_ref, mask_ref, feat_ref, vg_ref, fg_ref, gs, w1, acc,
):
    inner = inner_ref[0]
    mask = mask_ref[...].astype(F32)
    for a in range(3):
        w1[pl.ds(a * CH, CH), :] = expand(fw_ref[pl.ds(a * CH, CH), :], fold_ref[...], mask)
    feat_ref[...] = dot_tn(w2_ref[...], wn_ref[...]).astype(BF16)
    cot = cot_ref[...]
    with_above = jnp.concatenate([cot, above_ref[...]], axis=1)
    with_below = jnp.concatenate([cot, below_ref[...]], axis=1)
    spread = [
        dot(w2_ref[pl.ds((9 * a + 3) * CH, 6 * CH), :], with_below if a == 2 else with_above)
        for a in range(3)
    ]
    for j in range(4):
        sources = {0: ((0, 0), (2, 1)), 1: ((1, 0),), 2: ((2, 0), (0, 1)), 3: ((1, 1),)}[j]
        tiles = []
        for y in range(2):
            got = []
            for c in range(3):
                total = None
                for a, part in sources:
                    tile = spread[a][
                        (3 * y + c) * CH : (3 * y + c + 1) * CH, part * LANES : (part + 1) * LANES
                    ]
                    total = tile if total is None else total + tile
                got.append(total)
            even = got[1]
            odd = got[2] + earlier(got[0])
            value = pre_ref[j, :, pl.ds(y * 256, 256)]
            sigma = jax.nn.sigmoid(value)
            slope = sigma * (1.0 + value * (1.0 - sigma))
            if j == 0:
                slope = slope * inner
            even = even * slope[:, :LANES]
            odd = odd * slope[:, LANES:]
            tiles.append(
                [t.astype(BF16) for t in (even, odd, later(odd), earlier(even))]
            )
        fill_windows(gs.at[j], tiles)
    for j in range(4):
        first, last = max(0, j - 1), min(2, j)
        terms = dot(w1[pl.ds(first * CH, (last - first + 1) * CH), :], gs[j])
        for a in range(first, last + 1):
            term = terms[(a - first) * CH : (a - first + 1) * CH]
            out = j - a
            if a == 0:
                acc[out] = term
            else:
                acc[out] += term
    merge = merge_matrix()
    for out in range(2):
        for y in range(2):
            cut = pl.ds(y * 256, 256)
            vg_ref[out, :, cut] = dot(acc[out, :, cut].astype(BF16), merge).astype(BF16)
    taps = None
    for j in (1, 2):
        planes = jnp.concatenate([xc_ref[j - 1], xc_ref[j], xc_ref[j + 1]], axis=0)
        term = dot_nt(planes, gs[j])
        taps = term if taps is None else taps + term
    for a in range(3):
        kept = (taps[a * CH : (a + 1) * CH] * mask).astype(BF16)
        narrow = dot_nt(kept, flip_ref[...]).astype(BF16)
        fg_ref[pl.ds(a * CH, CH), :] = narrow[:, :LANES]
        fg_ref[pl.ds((3 + a) * CH, CH), :] = narrow[:, LANES:]
    fg_ref[pl.ds(6 * CH, F_ROWS - 6 * CH), :] = jnp.zeros((F_ROWS - 6 * CH, LANES), BF16)


def finish_kernel(factor, all_ref, out_ref):
    rows = 27 * CH
    half = rows // 2
    flat = all_ref[:, pl.ds(0, S_PIECE), :].reshape(S_ROWS, LANES).astype(F32) * factor
    out_ref[:, pl.ds(0, LANES)] = flat[:rows]
    rest = flat[rows : rows + half]
    out_ref[pl.ds(0, half), pl.ds(LANES, 64)] = rest[:, :64]
    out_ref[pl.ds(half, half), pl.ds(LANES, 64)] = rest[:, 64:]


def constants():
    narrow = np.arange(9 * PG)
    wide = np.arange(WIN)
    same = (narrow[:, None] % PG) == (wide[None, :] % PG)
    fold = same & ((narrow[:, None] // PG) == (wide[None, :] // CH))
    flip = same & ((8 - narrow[:, None] // PG) == (wide[None, :] // CH))
    flip = np.pad(flip, ((0, 256 - 9 * PG), (0, 0)))
    mask = (np.arange(CH)[:, None] // PG) == ((wide[None, :] % CH) // PG)
    return [jnp.asarray(m.astype(np.float32), BF16) for m in (fold, flip, mask)]


def sum_pieces(parts):
    return jnp.sum(parts.astype(F32), axis=0).astype(BF16)


def to_all(piece, axes, count):
    copies = jnp.broadcast_to(piece[None], (count,) + piece.shape)
    return lax.all_to_all(copies, axes, 0, 0, tiled=True)


def shards(volume, first_weight, second_weight, out_cotangent):
    vmem = pl.BlockSpec(memory_space=pltpu.VMEM)
    smem = pl.BlockSpec(memory_space=pltpu.SMEM)
    params = pltpu.CompilerParams(vmem_limit_bytes=56 * 1024 * 1024)
    count = lax.axis_size(SPACE)
    up = [(i, i + 1) for i in range(count - 1)]
    down = [(i + 1, i) for i in range(count - 1)]
    own = volume[0].transpose(1, 0, 2, 3).reshape(2, CH, 512)
    cot = out_cotangent.reshape(192, LANES)
    low = lax.ppermute(own, SPACE, up)
    high = lax.ppermute(own, SPACE, down)
    below = lax.ppermute(cot, SPACE, up)
    above = lax.ppermute(cot, SPACE, down)
    inner = jnp.where(lax.axis_index(SPACE) > 0, 1.0, 0.0).astype(F32).reshape(1)
    fold, flip, mask = constants()
    forward_weight = (
        first_weight.reshape(3, 9, 4, PG, PG).transpose(0, 2, 4, 1, 3).reshape(3 * CH, 9 * PG)
    )
    backward_weight = (
        first_weight[::-1].reshape(3, 9, 4, PG, PG).transpose(0, 2, 3, 1, 4).reshape(3 * CH, 9 * PG)
    )
    w2 = second_weight.reshape(27 * CH, 192)
    sg, pre, centre, windows = pl.pallas_call(
        forward_kernel,
        out_shape=(
            jax.ShapeDtypeStruct((S_ROWS, LANES), BF16),
            jax.ShapeDtypeStruct((4, CH, 512), F32),
            jax.ShapeDtypeStruct((4, CH, 512), BF16),
            jax.ShapeDtypeStruct((27 * CH, LANES), BF16),
        ),
        in_specs=[smem] + [vmem] * 7,
        out_specs=(vmem,) * 4,
        scratch_shapes=[pltpu.VMEM((6, WIN, 512), BF16), pltpu.VMEM((3 * CH, WIN), BF16)],
        compiler_params=params,
        name="forward",
    )(inner, low, own, high, forward_weight, fold, mask, cot)
    s_parts = lax.all_to_all(sg.reshape(PIECES, S_PIECE, LANES), NEAR, 0, 0, tiled=True)
    feat, vgrad, fg = pl.pallas_call(
        backward_kernel,
        out_shape=(
            jax.ShapeDtypeStruct((192, LANES), BF16),
            jax.ShapeDtypeStruct((2, CH, 512), BF16),
            jax.ShapeDtypeStruct((F_ROWS, LANES), BF16),
        ),
        in_specs=[smem] + [vmem] * 11,
        out_specs=(vmem,) * 3,
        scratch_shapes=[
            pltpu.VMEM((4, WIN, 512), BF16),
            pltpu.VMEM((3 * CH, WIN), BF16),
            pltpu.VMEM((2, CH, 512), F32),
        ],
        compiler_params=params,
        cost_estimate=pl.CostEstimate(flops=2 * 10**9, bytes_accessed=4 * 10**6, transcendentals=200000),
        name="backward",
    )(inner, pre, centre, windows, w2, below, cot, above, backward_weight, fold, flip, mask)
    f_parts = lax.all_to_all(fg.reshape(PIECES, F_PIECE, LANES), NEAR, 0, 0, tiled=True)
    piece = jnp.concatenate([sum_pieces(s_parts), sum_pieces(f_parts)], axis=0)
    piece = sum_pieces(to_all(piece, "z", lax.axis_size("z")))
    every = to_all(piece, NEAR, PIECES)
    factor = 1.0 / math.sqrt(lax.axis_size(DP) * lax.axis_size(SPACE) * LANES)
    second_grad = pl.pallas_call(
        lambda a, b: finish_kernel(factor, a, b),
        out_shape=jax.ShapeDtypeStruct((27 * CH, 192), F32),
        in_specs=[vmem],
        out_specs=vmem,
        compiler_params=params,
        name="finish",
    )(every)
    narrow = every[:, S_PIECE:].reshape(F_ROWS, LANES)[: 6 * CH].astype(F32) * factor
    narrow = jnp.concatenate([narrow[: 3 * CH], narrow[3 * CH :]], axis=1)[:, : 9 * PG]
    first_grad = (
        narrow.reshape(3, 4, PG, 9, PG).transpose(0, 3, 1, 2, 4).reshape(first_weight.shape)
    )
    features = feat.reshape(out_cotangent.shape)
    volume_grad = vgrad.reshape(2, CH, 2, 256).transpose(1, 0, 2, 3)[None]
    return (features, volume_grad, first_grad, second_grad.reshape(second_weight.shape))


def solution(mesh):
    fine = Mesh(mesh.devices.reshape(2, 16, 2, 4, 2), ("xh", "z", "xl", "y", "core"))
    split = P(DP, None, SPACE, None, None)
    return jax.shard_map(
        shards,
        mesh=fine,
        in_specs=(split, P(), P(), split),
        out_specs=(split, split, P(), P()),
        check_vma=False,
    )
```

```python
import math

import jax
import jax.numpy as jnp
import numpy as np
from jax import lax
from jax.experimental import pallas as pl
from jax.experimental.pallas import tpu as pltpu
from jax.sharding import Mesh
from jax.sharding import PartitionSpec as P

SPACE = ("xl", "y", "core")
DP = ("xh", "zh", "zl")
NEAR = ("xh", "xl", "y", "core", "zl")
F32 = jnp.float32
BF16 = jnp.bfloat16

CH = 96
PG = 24
WIN = 9 * CH
LANES = 128
PIECES = 64
ROWS = 4608
S_ROWS = 3 * (WIN + WIN // 2)
PIECE = ROWS // PIECES


def dot(a, b):
    return lax.dot_general(a, b, (((1,), (0,)), ((), ())), preferred_element_type=F32)


def dot_nt(a, b):
    return lax.dot_general(a, b, (((1,), (1,)), ((), ())), preferred_element_type=F32)


def dot_tn(a, b):
    return lax.dot_general(a, b, (((0,), (0,)), ((), ())), preferred_element_type=F32)


def later(tile):
    lane = lax.broadcasted_iota(jnp.int32, tile.shape, 1)
    return jnp.where(lane == 0, 0.0, pltpu.roll(tile, 1, 1))


def earlier(tile):
    lane = lax.broadcasted_iota(jnp.int32, tile.shape, 1)
    return jnp.where(lane == LANES - 1, 0.0, pltpu.roll(tile, LANES - 1, 1))


def fill_windows(ref, tiles):
    zero = jnp.zeros((CH, LANES), BF16)
    for b in range(3):
        for c in range(3):
            rows = pl.ds((b * 3 + c) * CH, CH)
            for y in range(2):
                source = y + b - 1
                if source in (0, 1):
                    even, odd, odd_later, even_earlier = tiles[source]
                    pair = ((odd_later, even), (even, odd), (odd, even_earlier))[c]
                else:
                    pair = (zero, zero)
                for parity in range(2):
                    ref[rows, pl.ds((2 * y + parity) * LANES, LANES)] = pair[parity]


def split_matrix():
    z = lax.broadcasted_iota(jnp.int32, (256, LANES), 0)
    k2 = 2 * lax.broadcasted_iota(jnp.int32, (256, LANES), 1)
    return jnp.concatenate(
        [jnp.where(z == k2 + off, 1.0, 0.0).astype(BF16) for off in (0, 1, -1, 2)], axis=1
    )


def merge_matrix():
    lane = lax.broadcasted_iota(jnp.int32, (LANES, 256), 0)
    z = lax.broadcasted_iota(jnp.int32, (LANES, 256), 1)
    return jnp.concatenate(
        [jnp.where(z == 2 * lane + bit, 1.0, 0.0).astype(BF16) for bit in (0, 1)], axis=0
    )


def expand(narrow, fold, mask):
    return (dot(narrow, fold) * mask).astype(BF16)


def main_kernel(
    inner_ref, low_ref, own_ref, high_ref, fw_ref, fold_ref, mask_ref, order_ref, w2_ref,
    comm_ref, wn_ref, g_ref, xs, w1, pre_ref, xc_ref, gs,
):
    inner = inner_ref[0]
    split = split_matrix()
    mask = mask_ref[...].astype(F32)
    for a in range(3):
        w1[pl.ds(a * CH, CH), :] = expand(fw_ref[pl.ds(a * CH, CH), :], fold_ref[...], mask)
    for e in range(6):
        slab = (low_ref, own_ref, high_ref)[e // 2]
        tiles = []
        for y in range(2):
            at = 4 * (e % 2) + 2 * y
            parts = dot(jnp.concatenate([slab[at], slab[at + 1]], axis=1), split).astype(BF16)
            tiles.append([parts[:, q * LANES : (q + 1) * LANES] for q in range(4)])
            if 1 <= e <= 4:
                xc_ref[e - 1, :, pl.ds(y * 256, 256)] = parts[:, :256]
        fill_windows(xs.at[e], tiles)
    for e in range(6):
        first, last = max(0, e - 3), min(2, e)
        terms = dot(w1[pl.ds(first * CH, (last - first + 1) * CH), :], xs[e])
        for a in range(first, last + 1):
            term = terms[(a - first) * CH : (a - first + 1) * CH]
            j = e - a
            if a == 0:
                pre_ref[j] = term
            else:
                pre_ref[j] += term
    zero = jnp.zeros((CH, LANES), BF16)
    for a in range(3):
        for c in range(3):
            wn_ref[pl.ds((9 * a + c) * CH, CH), :] = zero
        for y in range(2):
            value = pre_ref[a, :, pl.ds(y * 256, 256)]
            hidden = value * jax.nn.sigmoid(value)
            if a == 0:
                hidden = hidden * inner
            even, odd = hidden[:, :LANES], hidden[:, LANES:]
            base = (9 * a + 3 * (y + 1)) * CH
            wn_ref[pl.ds(base, CH), :] = later(odd).astype(BF16)
            wn_ref[pl.ds(base + CH, CH), :] = even.astype(BF16)
            wn_ref[pl.ds(base + 2 * CH, CH), :] = odd.astype(BF16)
    cot = jnp.concatenate([own_ref[8], own_ref[9]], axis=0)
    rest = cot[LANES:]
    none = jnp.zeros_like(rest)
    both = jnp.concatenate(
        [jnp.concatenate([rest, none], axis=1), jnp.concatenate([none, rest], axis=1)], axis=0
    )
    half = WIN // 2
    for a in range(3):
        at = a * (WIN + half)
        comm_ref[pl.ds(at, WIN), :] = dot_nt(wn_ref[pl.ds(a * WIN, WIN), :], cot[:LANES]).astype(
            BF16
        )
        pairs = jnp.concatenate(
            [wn_ref[pl.ds(a * WIN, half), :], wn_ref[pl.ds(a * WIN + half, half), :]], axis=1
        )
        comm_ref[pl.ds(at + WIN, half), :] = dot_nt(pairs, both).astype(BF16)
    above = jnp.concatenate([high_ref[8], high_ref[9]], axis=0)
    below = jnp.concatenate([low_ref[8], low_ref[9]], axis=0)
    with_above = jnp.concatenate([cot, above], axis=1)
    with_below = jnp.concatenate([cot, below], axis=1)
    spread = [
        dot(w2_ref[pl.ds((9 * a + 3) * CH, 6 * CH), :], with_below if a == 2 else with_above)
        for a in range(3)
    ]
    for j in range(4):
        sources = {0: ((0, 0), (2, 1)), 1: ((1, 0),), 2: ((2, 0), (0, 1)), 3: ((1, 1),)}[j]
        tiles = []
        for y in range(2):
            got = []
            for c in range(3):
                total = None
                for a, part in sources:
                    tile = spread[a][
                        (3 * y + c) * CH : (3 * y + c + 1) * CH, part * LANES : (part + 1) * LANES
                    ]
                    total = tile if total is None else total + tile
                got.append(total)
            even = got[1]
            odd = got[2] + earlier(got[0])
            value = pre_ref[j, :, pl.ds(y * 256, 256)]
            sigma = jax.nn.sigmoid(value)
            slope = sigma * (1.0 + value * (1.0 - sigma))
            if j == 0:
                slope = slope * inner
            even = even * slope[:, :LANES]
            odd = odd * slope[:, LANES:]
            tiles.append([t.astype(BF16) for t in (even, odd, later(odd), earlier(even))])
            for q in range(4):
                g_ref[j, :, pl.ds((4 * y + q) * LANES, LANES)] = tiles[y][q]
        if j in (1, 2):
            fill_windows(gs.at[j - 1], tiles)
    taps = None
    for j in (1, 2):
        planes = jnp.concatenate([xc_ref[j - 1], xc_ref[j], xc_ref[j + 1]], axis=0)
        term = dot_nt(planes, gs[j - 1])
        taps = term if taps is None else taps + term
    narrow = [
        dot_nt((taps[a * CH : (a + 1) * CH] * mask).astype(BF16), fold_ref[...]).astype(BF16)
        for a in range(3)
    ]
    ordered = dot(jnp.concatenate(narrow, axis=1), order_ref[...]).astype(BF16)
    for k in range(6):
        comm_ref[pl.ds(S_ROWS + k * CH, CH), :] = ordered[:, k * LANES : (k + 1) * LANES]
    left = ROWS - S_ROWS - 6 * CH
    comm_ref[pl.ds(ROWS - left, left), :] = jnp.zeros((left, LANES), BF16)


def tail_kernel(g_ref, wn_ref, w2_ref, fw_ref, fold_ref, mask_ref, feat_ref, vg_ref, gs, w1, acc):
    mask = mask_ref[...].astype(F32)
    for a in range(3):
        w1[pl.ds(a * CH, CH), :] = expand(fw_ref[pl.ds(a * CH, CH), :], fold_ref[...], mask)
    feat_ref[...] = dot_tn(w2_ref[...], wn_ref[...]).astype(BF16)
    for j in range(4):
        tiles = [
            [g_ref[j, :, pl.ds((4 * y + q) * LANES, LANES)] for q in range(4)] for y in range(2)
        ]
        fill_windows(gs.at[j], tiles)
    for j in range(4):
        first, last = max(0, j - 1), min(2, j)
        terms = dot(w1[pl.ds(first * CH, (last - first + 1) * CH), :], gs[j])
        for a in range(first, last + 1):
            term = terms[(a - first) * CH : (a - first + 1) * CH]
            out = j - a
            if a == 0:
                acc[out] = term
            else:
                acc[out] += term
    merge = merge_matrix()
    for out in range(2):
        for y in range(2):
            cut = pl.ds(y * 256, 256)
            vg_ref[out, :, cut] = dot(acc[out, :, cut].astype(BF16), merge).astype(BF16)


def finish_kernel(factor, all_ref, out_ref):
    half = WIN // 2
    out_ref[:, pl.ds(0, LANES)] = all_ref[pl.ds(0, WIN), :].astype(F32) * factor
    rest = all_ref[pl.ds(WIN, half), :].astype(F32) * factor
    out_ref[pl.ds(0, half), pl.ds(LANES, 64)] = rest[:, :64]
    out_ref[pl.ds(half, half), pl.ds(LANES, 64)] = rest[:, 64:]


def constants():
    narrow = np.arange(9 * PG)
    wide = np.arange(WIN)
    fold = ((narrow[:, None] % PG) == (wide[None, :] % PG)) & (
        (narrow[:, None] // PG) == (wide[None, :] // CH)
    )
    fold = np.pad(fold, ((0, 256 - 9 * PG), (0, 0)))
    mask = (np.arange(CH)[:, None] // PG) == ((wide[None, :] % CH) // PG)
    order = np.zeros((3 * 256, 6 * LANES))
    for a in range(3):
        for back in range(9):
            for o in range(PG):
                order[a * 256 + back * PG + o, o * 27 + 9 * a + 8 - back] = 1
    return [jnp.asarray(m.astype(np.float32), BF16) for m in (fold, mask, order)]


def sum_pieces(parts):
    return jnp.sum(parts.astype(F32), axis=0).astype(BF16)


def to_all(piece, axes, count):
    copies = jnp.broadcast_to(piece[None], (count,) + piece.shape)
    return lax.all_to_all(copies, axes, 0, 0, tiled=True)


def shards(volume, first_weight, second_weight, out_cotangent):
    vmem = pl.BlockSpec(memory_space=pltpu.VMEM)
    smem = pl.BlockSpec(memory_space=pltpu.SMEM)
    params = pltpu.CompilerParams(vmem_limit_bytes=56 * 1024 * 1024)
    count = lax.axis_size(SPACE)
    up = [(i, i + 1) for i in range(count - 1)]
    down = [(i + 1, i) for i in range(count - 1)]
    planes = volume.reshape(CH, 2, 2, 2, LANES).transpose(1, 2, 3, 0, 4).reshape(8, CH, LANES)
    own = jnp.concatenate([planes, out_cotangent.reshape(2, CH, LANES)], axis=0)
    low = lax.ppermute(own, SPACE, up)
    high = lax.ppermute(own, SPACE, down)
    inner = jnp.where(lax.axis_index(SPACE) > 0, 1.0, 0.0).astype(F32).reshape(1)
    fold, mask, order = constants()
    wide = ((0, 0), (0, 256 - 9 * PG))
    forward_weight = jnp.pad(
        first_weight.reshape(3, 9, 4, PG, PG).transpose(0, 2, 4, 1, 3).reshape(3 * CH, 9 * PG), wide
    )
    w2 = second_weight.reshape(27 * CH, 192)
    comm, windows, grads = pl.pallas_call(
        main_kernel,
        out_shape=(
            jax.ShapeDtypeStruct((ROWS, LANES), BF16),
            jax.ShapeDtypeStruct((27 * CH, LANES), BF16),
            jax.ShapeDtypeStruct((4, CH, 8 * LANES), BF16),
        ),
        in_specs=[smem] + [vmem] * 8,
        out_specs=(vmem,) * 3,
        scratch_shapes=[
            pltpu.VMEM((6, WIN, 512), BF16),
            pltpu.VMEM((3 * CH, WIN), BF16),
            pltpu.VMEM((4, CH, 512), F32),
            pltpu.VMEM((4, CH, 512), BF16),
            pltpu.VMEM((2, WIN, 512), BF16),
        ],
        compiler_params=params,
        name="main",
    )(inner, low, own, high, forward_weight, fold, mask, order, w2)
    parts = lax.all_to_all(comm.reshape(PIECES, PIECE, LANES), NEAR, 0, 0, tiled=True)
    late_weight = lax.optimization_barrier((first_weight, comm))[0]
    backward_weight = jnp.pad(
        late_weight[::-1].reshape(3, 9, 4, PG, PG).transpose(0, 2, 3, 1, 4).reshape(3 * CH, 9 * PG),
        wide,
    )
    feat, vgrad = pl.pallas_call(
        tail_kernel,
        out_shape=(
            jax.ShapeDtypeStruct((192, LANES), BF16),
            jax.ShapeDtypeStruct((2, CH, 512), BF16),
        ),
        in_specs=[vmem] * 6,
        out_specs=(vmem,) * 2,
        scratch_shapes=[
            pltpu.VMEM((4, WIN, 512), BF16),
            pltpu.VMEM((3 * CH, WIN), BF16),
            pltpu.VMEM((2, CH, 512), F32),
        ],
        compiler_params=params,
        cost_estimate=pl.CostEstimate(flops=10**9, bytes_accessed=4 * 10**6, transcendentals=0),
        name="tail",
    )(grads, windows, w2, backward_weight, fold, mask)
    piece = sum_pieces(to_all(sum_pieces(parts), "zh", lax.axis_size("zh")))
    every = to_all(piece, NEAR, PIECES).reshape(ROWS, LANES)
    factor = 1.0 / math.sqrt(lax.axis_size(DP) * lax.axis_size(SPACE) * LANES)
    block = WIN + WIN // 2
    second_grad = pl.pallas_call(
        lambda a, b: finish_kernel(factor, a, b),
        out_shape=jax.ShapeDtypeStruct((27 * CH, 192), F32),
        grid=(3,),
        in_specs=[pl.BlockSpec((block, LANES), lambda k: (k, 0))],
        out_specs=pl.BlockSpec((WIN, 192), lambda k: (k, 0)),
        compiler_params=params,
        name="finish",
    )(every)
    narrow = every[S_ROWS : S_ROWS + 6 * CH].reshape(6, CH, LANES).transpose(1, 0, 2)
    narrow = narrow.reshape(CH, 6 * LANES)[:, : 27 * PG].astype(F32) * factor
    first_grad = narrow.reshape(4, PG, PG, 27).transpose(3, 0, 1, 2)
    features = feat.reshape(out_cotangent.shape)
    volume_grad = vgrad.reshape(2, CH, 2, 256).transpose(1, 0, 2, 3)[None]
    return (features, volume_grad, first_grad, second_grad.reshape(second_weight.shape))


def solution(mesh):
    fine = Mesh(mesh.devices.reshape(2, 8, 2, 2, 4, 2), ("xh", "zh", "zl", "xl", "y", "core"))
    split = P(DP, None, SPACE, None, None)
    return jax.shard_map(
        shards,
        mesh=fine,
        in_specs=(split, P(), P(), split),
        out_specs=(split, split, P(), P()),
        check_vma=False,
    )
```

```python
import functools
import math

import jax
import jax.numpy as jnp
import numpy as np
from jax import lax
from jax.experimental import pallas as pl
from jax.experimental.pallas import tpu as pltpu
from jax.sharding import Mesh
from jax.sharding import PartitionSpec as P

SPACE = ("xl", "y", "core")
DP = ("xh", "zh", "zl")
NEAR = ("xh", "xl", "y", "zl")
F32 = jnp.float32
BF16 = jnp.bfloat16

CH = 96
PG = 24
WIN = 9 * CH
LANES = 128
HALF = 27 * CH // 2
LEFT, RIGHT = 656, HALF - 656
S_ROWS = HALF + LEFT
F_ROWS = 3 * CH
PIECES = 32
PIECE = 72
ROWS = PIECES * PIECE


def dot(a, b):
    return lax.dot_general(a, b, (((1,), (0,)), ((), ())), preferred_element_type=F32)


def dot_nt(a, b):
    return lax.dot_general(a, b, (((1,), (1,)), ((), ())), preferred_element_type=F32)


def dot_tn(a, b):
    return lax.dot_general(a, b, (((0,), (0,)), ((), ())), preferred_element_type=F32)


def later(tile):
    lane = lax.broadcasted_iota(jnp.int32, tile.shape, 1)
    return jnp.where(lane == 0, 0.0, pltpu.roll(tile, 1, 1))


def earlier(tile):
    lane = lax.broadcasted_iota(jnp.int32, tile.shape, 1)
    return jnp.where(lane == LANES - 1, 0.0, pltpu.roll(tile, LANES - 1, 1))


def fill_windows(ref, tiles):
    zero = jnp.zeros((CH, LANES), BF16)
    for b in range(3):
        for c in range(3):
            rows = pl.ds((b * 3 + c) * CH, CH)
            for y in range(2):
                source = y + b - 1
                if source in (0, 1):
                    even, odd, odd_later, even_earlier = tiles[source]
                    pair = ((odd_later, even), (even, odd), (odd, even_earlier))[c]
                else:
                    pair = (zero, zero)
                for parity in range(2):
                    ref[rows, pl.ds((2 * y + parity) * LANES, LANES)] = pair[parity]


def split_matrix():
    z = lax.broadcasted_iota(jnp.int32, (256, LANES), 0)
    k2 = 2 * lax.broadcasted_iota(jnp.int32, (256, LANES), 1)
    return jnp.concatenate(
        [jnp.where(z == k2 + off, 1.0, 0.0).astype(BF16) for off in (0, 1, -1, 2)], axis=1
    )


def merge_matrix():
    lane = lax.broadcasted_iota(jnp.int32, (LANES, 256), 0)
    z = lax.broadcasted_iota(jnp.int32, (LANES, 256), 1)
    return jnp.concatenate(
        [jnp.where(z == 2 * lane + bit, 1.0, 0.0).astype(BF16) for bit in (0, 1)], axis=0
    )


def expand(narrow, fold, mask):
    return (dot(narrow, fold[: 9 * PG]) * mask).astype(BF16)


def main_kernel(
    inner_ref, core_ref, low_hbm, own_ref, high_hbm, fw_ref, fold_ref, mask_ref, order_ref, w2_ref,
    mine_ref, other_ref, wn_ref, g_ref, xs, w1, pre_ref, xc_ref, gs, low_ref, high_ref, fg, sems,
):
    inner = inner_ref[0]
    core = core_ref[0]
    fetch_low = pltpu.make_async_copy(low_hbm, low_ref, sems.at[0])
    fetch_high = pltpu.make_async_copy(high_hbm, high_ref, sems.at[1])
    fetch_low.start()
    fetch_high.start()
    split = split_matrix()
    mask = mask_ref[...].astype(F32)
    for a in range(3):
        w1[pl.ds(a * CH, CH), :] = expand(fw_ref[pl.ds(a * CH, CH), :], fold_ref[...], mask)
    for e in (2, 3, 0, 1, 4, 5):
        slab = (low_ref, own_ref, high_ref)[e // 2]
        if e == 0:
            fetch_low.wait()
            fetch_high.wait()
        tiles = []
        for y in range(2):
            at = 4 * (e % 2) + 2 * y
            parts = dot(jnp.concatenate([slab[at], slab[at + 1]], axis=1), split).astype(BF16)
            tiles.append([parts[:, q * LANES : (q + 1) * LANES] for q in range(4)])
            if 1 <= e <= 4:
                xc_ref[e - 1, :, pl.ds(y * 256, 256)] = parts[:, :256]
        fill_windows(xs.at[e], tiles)
    for e in range(6):
        first, last = max(0, e - 3), min(2, e)
        terms = dot(w1[pl.ds(first * CH, (last - first + 1) * CH), :], xs[e])
        for a in range(first, last + 1):
            term = terms[(a - first) * CH : (a - first + 1) * CH]
            j = e - a
            if a == 0:
                pre_ref[j] = term
            else:
                pre_ref[j] += term
    zero = jnp.zeros((CH, LANES), BF16)
    for a in range(3):
        for c in range(3):
            wn_ref[pl.ds((9 * a + c) * CH, CH), :] = zero
        for y in range(2):
            value = pre_ref[a, :, pl.ds(y * 256, 256)]
            hidden = value * jax.nn.sigmoid(value)
            if a == 0:
                hidden = hidden * inner
            even, odd = hidden[:, :LANES], hidden[:, LANES:]
            base = (9 * a + 3 * (y + 1)) * CH
            wn_ref[pl.ds(base, CH), :] = later(odd).astype(BF16)
            wn_ref[pl.ds(base + CH, CH), :] = even.astype(BF16)
            wn_ref[pl.ds(base + 2 * CH, CH), :] = odd.astype(BF16)
    cot = jnp.concatenate([own_ref[8], own_ref[9]], axis=0)
    rest = cot[LANES:]
    none = jnp.zeros_like(rest)
    both = jnp.concatenate(
        [jnp.concatenate([rest, none], axis=1), jnp.concatenate([none, rest], axis=1)], axis=0
    )
    for out_ref, half in ((mine_ref, core), (other_ref, 1 - core)):
        base = pl.multiple_of(half * HALF, 16)
        out_ref[pl.ds(0, HALF), :] = dot_nt(wn_ref[pl.ds(base, HALF), :], cot[:LANES]).astype(BF16)
        left = wn_ref[pl.ds(base, LEFT), :]
        right = wn_ref[pl.ds(base + LEFT, RIGHT), :]
        right = jnp.concatenate([right, jnp.zeros((LEFT - RIGHT, LANES), BF16)], axis=0)
        pairs = jnp.concatenate([left, right], axis=1)
        out_ref[pl.ds(HALF, LEFT), :] = dot_nt(pairs, both).astype(BF16)
    above = jnp.concatenate([high_ref[8], high_ref[9]], axis=0)
    below = jnp.concatenate([low_ref[8], low_ref[9]], axis=0)
    with_above = jnp.concatenate([cot, above], axis=1)
    with_below = jnp.concatenate([cot, below], axis=1)
    spread = [
        dot(w2_ref[pl.ds((9 * a + 3) * CH, 6 * CH), :], with_below if a == 2 else with_above)
        for a in range(3)
    ]
    for j in range(4):
        sources = {0: ((0, 0), (2, 1)), 1: ((1, 0),), 2: ((2, 0), (0, 1)), 3: ((1, 1),)}[j]
        tiles = []
        for y in range(2):
            got = []
            for c in range(3):
                total = None
                for a, part in sources:
                    tile = spread[a][
                        (3 * y + c) * CH : (3 * y + c + 1) * CH, part * LANES : (part + 1) * LANES
                    ]
                    total = tile if total is None else total + tile
                got.append(total)
            even = got[1]
            odd = got[2] + earlier(got[0])
            value = pre_ref[j, :, pl.ds(y * 256, 256)]
            sigma = jax.nn.sigmoid(value)
            slope = sigma * (1.0 + value * (1.0 - sigma))
            if j == 0:
                slope = slope * inner
            even = even * slope[:, :LANES]
            odd = odd * slope[:, LANES:]
            tiles.append([t.astype(BF16) for t in (even, odd, later(odd), earlier(even))])
            for q in range(4):
                g_ref[j, :, pl.ds((4 * y + q) * LANES, LANES)] = tiles[y][q]
        if j in (1, 2):
            fill_windows(gs.at[j - 1], tiles)
    taps = None
    for j in (1, 2):
        planes = jnp.concatenate([xc_ref[j - 1], xc_ref[j], xc_ref[j + 1]], axis=0)
        term = dot_nt(planes, gs[j - 1])
        taps = term if taps is None else taps + term
    narrow = [
        dot_nt((taps[a * CH : (a + 1) * CH] * mask).astype(BF16), fold_ref[...]).astype(BF16)
        for a in range(3)
    ]
    ordered = dot(jnp.concatenate(narrow, axis=1), order_ref[...]).astype(BF16)
    for k in range(6):
        fg[pl.ds(k * CH, CH), :] = ordered[:, k * LANES : (k + 1) * LANES]
    for out_ref, half in ((mine_ref, core), (other_ref, 1 - core)):
        base = pl.multiple_of(half * F_ROWS, 16)
        out_ref[pl.ds(S_ROWS, F_ROWS), :] = fg[pl.ds(base, F_ROWS), :]
        left = ROWS - S_ROWS - F_ROWS
        out_ref[pl.ds(ROWS - left, left), :] = jnp.zeros((left, LANES), BF16)


def tail_kernel(
    after_ref, g_ref, wn_ref, w2_ref, fw_ref, fold_ref, mask_ref, feat_ref, vg_ref, done_ref, gs, w1, acc,
):
    done_ref[...] = jnp.zeros((1, LANES), F32)
    mask = mask_ref[...].astype(F32)
    for a in range(3):
        w1[pl.ds(a * CH, CH), :] = expand(fw_ref[pl.ds(a * CH, CH), :], fold_ref[...], mask)
    feat_ref[...] = dot_tn(w2_ref[...], wn_ref[...]).astype(BF16)
    for j in range(4):
        tiles = [
            [g_ref[j, :, pl.ds((4 * y + q) * LANES, LANES)] for q in range(4)] for y in range(2)
        ]
        fill_windows(gs.at[j], tiles)
    for j in range(4):
        first, last = max(0, j - 1), min(2, j)
        terms = dot(w1[pl.ds(first * CH, (last - first + 1) * CH), :], gs[j])
        for a in range(first, last + 1):
            term = terms[(a - first) * CH : (a - first + 1) * CH]
            out = j - a
            if a == 0:
                acc[out] = term
            else:
                acc[out] += term
    merge = merge_matrix()
    for out in range(2):
        for y in range(2):
            cut = pl.ds(y * 256, 256)
            vg_ref[out, :, cut] = dot(acc[out, :, cut].astype(BF16), merge).astype(BF16)


def finish_kernel(factor, half_ref, all_ref, *refs):
    out_ref = refs[-1]
    out_ref[:, pl.ds(0, LANES)] = all_ref[pl.ds(0, HALF), :].astype(F32) * factor
    rest = all_ref[pl.ds(HALF, LEFT), :].astype(F32) * factor
    out_ref[pl.ds(0, LEFT), pl.ds(LANES, 64)] = rest[:, :64]
    out_ref[pl.ds(LEFT, RIGHT), pl.ds(LANES, 64)] = rest[:RIGHT, 64:]


def finish(factor, half, rows, params, before=None):
    return pl.pallas_call(
        functools.partial(finish_kernel, factor),
        out_shape=jax.ShapeDtypeStruct((27 * CH, 192), F32),
        grid_spec=pltpu.PrefetchScalarGridSpec(
            num_scalar_prefetch=1,
            grid=(1,),
            in_specs=[pl.BlockSpec((ROWS, LANES), lambda k, half: (0, 0))]
            + ([] if before is None else [pl.BlockSpec(memory_space=pl.ANY)]),
            out_specs=pl.BlockSpec((HALF, 192), lambda k, half: (half[0], 0)),
        ),
        input_output_aliases={} if before is None else {2: 0},
        compiler_params=params,
        name="finish",
    )(half, rows, *([] if before is None else [before]))


def constants():
    narrow = np.arange(9 * PG)
    wide = np.arange(WIN)
    fold = ((narrow[:, None] % PG) == (wide[None, :] % PG)) & (
        (narrow[:, None] // PG) == (wide[None, :] // CH)
    )
    fold = np.pad(fold, ((0, 256 - 9 * PG), (0, 0)))
    mask = (np.arange(CH)[:, None] // PG) == ((wide[None, :] % CH) // PG)
    order = np.zeros((3 * 256, 6 * LANES))
    for a in range(3):
        for back in range(9):
            for o in range(PG):
                order[a * 256 + back * PG + o, o * 27 + 9 * a + 8 - back] = 1
    return [jnp.asarray(m.astype(np.float32), BF16) for m in (fold, mask, order)]


def sum_pieces(parts):
    return jnp.sum(parts.astype(F32), axis=0).astype(BF16)


def to_all(piece, axes, count):
    copies = jnp.broadcast_to(piece[None], (count,) + piece.shape)
    return lax.all_to_all(copies, axes, 0, 0, tiled=True)


def shards(volume, first_weight, second_weight, out_cotangent):
    vmem = pl.BlockSpec(memory_space=pltpu.VMEM)
    smem = pl.BlockSpec(memory_space=pltpu.SMEM)
    anywhere = pl.BlockSpec(memory_space=pl.ANY)
    params = pltpu.CompilerParams(vmem_limit_bytes=56 * 1024 * 1024)
    count = lax.axis_size(SPACE)
    up = [(i, i + 1) for i in range(count - 1)]
    down = [(i + 1, i) for i in range(count - 1)]
    planes = volume.reshape(CH, 2, 2, 2, LANES).transpose(1, 2, 3, 0, 4).reshape(8, CH, LANES)
    own = jnp.concatenate([planes, out_cotangent.reshape(2, CH, LANES)], axis=0)
    low = lax.ppermute(own, SPACE, up)
    high = lax.ppermute(own, SPACE, down)
    core = lax.axis_index("core").astype(jnp.int32).reshape(1)
    inner = jnp.where(lax.axis_index(SPACE) > 0, 1.0, 0.0).astype(F32).reshape(1)
    fold, mask, order = constants()
    forward_weight = (
        first_weight.reshape(3, 9, 4, PG, PG).transpose(0, 2, 4, 1, 3).reshape(3 * CH, 9 * PG)
    )
    w2 = second_weight.reshape(27 * CH, 192)
    mine, other, windows, grads = pl.pallas_call(
        main_kernel,
        out_shape=(
            jax.ShapeDtypeStruct((ROWS, LANES), BF16),
            jax.ShapeDtypeStruct((ROWS, LANES), BF16),
            jax.ShapeDtypeStruct((27 * CH, LANES), BF16),
            jax.ShapeDtypeStruct((4, CH, 8 * LANES), BF16),
        ),
        in_specs=[smem, smem, anywhere, vmem, anywhere] + [vmem] * 5,
        out_specs=(vmem,) * 4,
        scratch_shapes=[
            pltpu.VMEM((6, WIN, 512), BF16),
            pltpu.VMEM((3 * CH, WIN), BF16),
            pltpu.VMEM((4, CH, 512), F32),
            pltpu.VMEM((4, CH, 512), BF16),
            pltpu.VMEM((2, WIN, 512), BF16),
            pltpu.VMEM((10, CH, LANES), BF16),
            pltpu.VMEM((10, CH, LANES), BF16),
            pltpu.VMEM((6 * CH, LANES), BF16),
            pltpu.SemaphoreType.DMA((2,)),
        ],
        compiler_params=params,
        name="main",
    )(inner, core, low, own, high, forward_weight, fold, mask, order, w2)
    swap = [(0, 1), (1, 0)]
    got = lax.ppermute(other, "core", swap)
    chip = (mine.astype(F32) + got.astype(F32)).astype(BF16)
    parts = lax.all_to_all(chip.reshape(PIECES, PIECE, LANES), NEAR, 0, 0, tiled=True)
    late_weight = lax.optimization_barrier((first_weight, windows))[0]
    backward_weight = (
        late_weight[::-1].reshape(3, 9, 4, PG, PG).transpose(0, 2, 3, 1, 4).reshape(3 * CH, 9 * PG)
    )
    feat, vgrad, done = pl.pallas_call(
        tail_kernel,
        out_shape=(
            jax.ShapeDtypeStruct((192, LANES), BF16),
            jax.ShapeDtypeStruct((2, CH, 512), BF16),
            jax.ShapeDtypeStruct((1, LANES), F32),
        ),
        in_specs=[anywhere] + [vmem] * 6,
        out_specs=(vmem,) * 3,
        scratch_shapes=[
            pltpu.VMEM((4, WIN, 512), BF16),
            pltpu.VMEM((3 * CH, WIN), BF16),
            pltpu.VMEM((2, CH, 512), F32),
        ],
        compiler_params=params,
        cost_estimate=pl.CostEstimate(flops=10**9, bytes_accessed=4 * 10**6, transcendentals=0),
        name="tail",
    )(chip, grads, windows, w2, backward_weight, fold, mask)
    piece = (jnp.sum(parts.astype(F32), axis=0) + done).astype(BF16)
    piece = sum_pieces(to_all(piece, "zh", lax.axis_size("zh")))
    own_half = to_all(piece, NEAR, PIECES).reshape(ROWS, LANES)
    other_half = lax.ppermute(own_half, "core", swap)
    factor = 1.0 / math.sqrt(lax.axis_size(DP) * lax.axis_size(SPACE) * LANES)
    second_grad = finish(factor, core, own_half, params)
    second_grad = finish(factor, 1 - core, other_half, params, second_grad)
    cut = slice(S_ROWS, S_ROWS + F_ROWS)
    halves = [jnp.where(core == h, own_half[cut], other_half[cut]) for h in (0, 1)]
    narrow = jnp.concatenate([t.reshape(3, CH, LANES) for t in halves]).transpose(1, 0, 2)
    narrow = narrow.reshape(CH, 6 * LANES)[:, : 27 * PG].astype(F32) * factor
    first_grad = narrow.reshape(4, PG, PG, 27).transpose(3, 0, 1, 2)
    features = feat.reshape(out_cotangent.shape)
    volume_grad = vgrad.reshape(2, CH, 2, 256).transpose(1, 0, 2, 3)[None]
    return (features, volume_grad, first_grad, second_grad.reshape(second_weight.shape))


def solution(mesh):
    fine = Mesh(mesh.devices.reshape(2, 8, 2, 2, 4, 2), ("xh", "zh", "zl", "xl", "y", "core"))
    split = P(DP, None, SPACE, None, None)
    return jax.shard_map(
        shards,
        mesh=fine,
        in_specs=(split, P(), P(), split),
        out_specs=(split, split, P(), P()),
        check_vma=False,
    )
```

```python
import functools
import math

import jax
import jax.numpy as jnp
from jax import lax
from jax.experimental import pallas as pl
from jax.experimental.pallas import tpu as pltpu
from jax.sharding import Mesh
from jax.sharding import PartitionSpec as P

SPACE = ("xl", "y", "core")
DP = ("xh", "zh", "zl")
NEAR = ("xh", "xl", "y", "zl")
F32 = jnp.float32
BF16 = jnp.bfloat16

CH = 96
PG = 24
TAPS = 27
WIN = 9 * CH
LANES = 128
HALF = TAPS * CH // 2
PART = HALF // 3
LEFT, RIGHT = 224, PART - 224
F_PART = CH // 2
CHUNK = PART + LEFT + 2 * F_PART
PIECES = 32
PIECE = 72
ROWS = PIECES * PIECE


def dot(a, b):
    return lax.dot_general(a, b, (((1,), (0,)), ((), ())), preferred_element_type=F32)


def dot_nt(a, b):
    return lax.dot_general(a, b, (((1,), (1,)), ((), ())), preferred_element_type=F32)


def dot_tn(a, b):
    return lax.dot_general(a, b, (((0,), (0,)), ((), ())), preferred_element_type=F32)


def later(tile):
    lane = lax.broadcasted_iota(jnp.int32, tile.shape, 1)
    return jnp.where(lane == 0, 0.0, pltpu.roll(tile, 1, 1))


def earlier(tile):
    lane = lax.broadcasted_iota(jnp.int32, tile.shape, 1)
    return jnp.where(lane == LANES - 1, 0.0, pltpu.roll(tile, LANES - 1, 1))


def fill_windows(ref, tiles):
    zero = jnp.zeros((CH, LANES), BF16)
    for b in range(3):
        for c in range(3):
            rows = pl.ds((b * 3 + c) * CH, CH)
            for y in range(2):
                source = y + b - 1
                if source in (0, 1):
                    even, odd, odd_later, even_earlier = tiles[source]
                    pair = ((odd_later, even), (even, odd), (odd, even_earlier))[c]
                else:
                    pair = (zero, zero)
                for parity in range(2):
                    ref[rows, pl.ds((2 * y + parity) * LANES, LANES)] = pair[parity]


def ones_where(condition):
    return jnp.where(condition, 1.0, 0.0).astype(BF16)


def split_matrix():
    z = lax.broadcasted_iota(jnp.int32, (256, LANES), 0)
    k2 = 2 * lax.broadcasted_iota(jnp.int32, (256, LANES), 1)
    return jnp.concatenate([ones_where(z == k2 + off) for off in (0, 1, -1, 2)], axis=1)


def merge_matrix():
    lane = lax.broadcasted_iota(jnp.int32, (LANES, 256), 0)
    z = lax.broadcasted_iota(jnp.int32, (LANES, 256), 1)
    return jnp.concatenate([ones_where(z == 2 * lane + bit) for bit in (0, 1)], axis=0)


def quotient(value, divisor, bits):
    return (value * (2**bits // divisor + 1)) >> bits


def fold_matrix(rows):
    row = lax.broadcasted_iota(jnp.int32, (rows, WIN), 0)
    column = lax.broadcasted_iota(jnp.int32, (1, WIN), 1)
    target = quotient(column, CH, 16) * PG + column - PG * quotient(column, PG, 16)
    return ones_where(row == target)


def group_mask():
    row = lax.broadcasted_iota(jnp.int32, (CH, WIN), 0)
    column = lax.broadcasted_iota(jnp.int32, (1, WIN), 1)
    offset = row - PG * quotient(column - CH * quotient(column, CH, 16), PG, 16)
    return (offset >= 0) & (offset < PG)


def order_matrix():
    row = lax.broadcasted_iota(jnp.int32, (3 * 256, 6 * LANES), 0)
    column = lax.broadcasted_iota(jnp.int32, (1, 6 * LANES), 1)
    channel = quotient(column, TAPS, 16)
    tap = column - TAPS * channel
    plane = quotient(tap, 9, 16)
    target = plane * 256 + (8 - tap + 9 * plane) * PG + channel
    return ones_where((row == target) & (column < PG * TAPS))


def expand(narrow, fold, mask):
    return jnp.where(mask, dot(narrow, fold), 0.0).astype(BF16)


def main_kernel(
    stage, inner_ref, core_ref, low_hbm, own_hbm, high_hbm, fw_ref, w2_hbm,
    mine_hbm, other_hbm, wn_hbm, g_hbm,
    low_ref, own_ref, high_ref, w2_ref, mine_ref, other_ref, wn_ref, g_ref,
    xs, w1, pre_ref, xc_ref, gs, order_ref, fg, sems,
):
    inner = inner_ref[0]
    core = core_ref[0]
    fetches = [
        pltpu.make_async_copy(source, target, sems.at[i])
        for i, (source, target) in enumerate(
            ((own_hbm, own_ref), (low_hbm, low_ref), (high_hbm, high_ref), (w2_hbm, w2_ref))
        )
    ]
    for fetch in fetches:
        fetch.start()
    split = split_matrix()
    mask = group_mask()
    fold = fold_matrix(9 * PG)
    for a in range(3):
        w1[pl.ds(a * CH, CH), :] = expand(fw_ref[pl.ds(a * CH, CH), :], fold, mask)
    fetches[0].wait()
    for e in (2, 3, 0, 1, 4, 5):
        slab = (low_ref, own_ref, high_ref)[e // 2]
        if e == 0:
            fetches[1].wait()
            fetches[2].wait()
        tiles = []
        for y in range(2):
            at = 4 * (e % 2) + 2 * y
            parts = dot(jnp.concatenate([slab[at], slab[at + 1]], axis=1), split).astype(BF16)
            tiles.append([parts[:, q * LANES : (q + 1) * LANES] for q in range(4)])
            if 1 <= e <= 4:
                xc_ref[e - 1, :, pl.ds(y * 256, 256)] = parts[:, :256]
        fill_windows(xs.at[e], tiles)
    for e in range(6):
        first, last = max(0, e - 3), min(2, e)
        terms = dot(w1[pl.ds(first * CH, (last - first + 1) * CH), :], xs[e])
        for a in range(first, last + 1):
            term = terms[(a - first) * CH : (a - first + 1) * CH]
            j = e - a
            if a == 0:
                pre_ref[j] = term
            else:
                pre_ref[j] += term
    zero = jnp.zeros((CH, LANES), BF16)
    for a in range(3):
        for c in range(3):
            wn_ref[pl.ds((9 * a + c) * CH, CH), :] = zero
        for y in range(2):
            value = pre_ref[a, :, pl.ds(y * 256, 256)]
            hidden = value * jax.nn.sigmoid(value)
            if a == 0:
                hidden = hidden * inner
            even, odd = hidden[:, :LANES], hidden[:, LANES:]
            base = (9 * a + 3 * (y + 1)) * CH
            wn_ref[pl.ds(base, CH), :] = later(odd).astype(BF16)
            wn_ref[pl.ds(base + CH, CH), :] = even.astype(BF16)
            wn_ref[pl.ds(base + 2 * CH, CH), :] = odd.astype(BF16)
    send_wn = pltpu.make_async_copy(wn_ref, wn_hbm, sems.at[0])
    send_wn.start()
    cot = jnp.concatenate([own_ref[8], own_ref[9]], axis=0)
    rest = cot[LANES:]
    none = jnp.zeros_like(rest)
    both = jnp.concatenate(
        [jnp.concatenate([rest, none], axis=1), jnp.concatenate([none, rest], axis=1)], axis=0
    )
    fill = jnp.zeros((LEFT - RIGHT, LANES), BF16)
    for out_ref, half in ((other_ref, 1 - core), (mine_ref, core)):
        for k in range(3):
            base = pl.multiple_of(half * HALF + k * PART, 16)
            wide = dot_nt(wn_ref[pl.ds(base, PART), :], cot[:LANES])
            out_ref[pl.ds(k * CHUNK, PART), :] = wide.astype(BF16)
            left = wn_ref[pl.ds(base, LEFT), :]
            right = jnp.concatenate([wn_ref[pl.ds(base + LEFT, RIGHT), :], fill], axis=0)
            pairs = jnp.concatenate([left, right], axis=1)
            out_ref[pl.ds(k * CHUNK + PART, LEFT), :] = dot_nt(pairs, both).astype(BF16)
    above = jnp.concatenate([high_ref[8], high_ref[9]], axis=0)
    below = jnp.concatenate([low_ref[8], low_ref[9]], axis=0)
    with_above = jnp.concatenate([cot, above], axis=1)
    with_below = jnp.concatenate([cot, below], axis=1)
    order_ref[...] = order_matrix()
    fetches[3].wait()
    spread = [
        dot(w2_ref[pl.ds((9 * a + 3) * CH, 6 * CH), :], with_below if a == 2 else with_above)
        for a in range(3)
    ]
    for j in range(4):
        sources = {0: ((0, 0), (2, 1)), 1: ((1, 0),), 2: ((2, 0), (0, 1)), 3: ((1, 1),)}[j]
        tiles = []
        for y in range(2):
            got = []
            for c in range(3):
                total = None
                for a, part in sources:
                    tile = spread[a][
                        (3 * y + c) * CH : (3 * y + c + 1) * CH, part * LANES : (part + 1) * LANES
                    ]
                    total = tile if total is None else total + tile
                got.append(total)
            even = got[1]
            odd = got[2] + earlier(got[0])
            value = pre_ref[j, :, pl.ds(y * 256, 256)]
            sigma = jax.nn.sigmoid(value)
            slope = sigma * (1.0 + value * (1.0 - sigma))
            if j == 0:
                slope = slope * inner
            even = even * slope[:, :LANES]
            odd = odd * slope[:, LANES:]
            tiles.append([t.astype(BF16) for t in (even, odd, later(odd), earlier(even))])
            for q in range(4):
                g_ref[j, :, pl.ds((4 * y + q) * LANES, LANES)] = tiles[y][q]
        if j in (1, 2):
            fill_windows(gs.at[j - 1], tiles)
    send_g = pltpu.make_async_copy(g_ref, g_hbm, sems.at[1])
    send_g.start()
    taps = None
    for j in (1, 2):
        planes = jnp.concatenate([xc_ref[j - 1], xc_ref[j], xc_ref[j + 1]], axis=0)
        term = dot_nt(planes, gs[j - 1])
        taps = term if taps is None else taps + term
    fold = fold_matrix(256)
    kept = [jnp.where(mask, taps[a * CH : (a + 1) * CH], 0.0).astype(BF16) for a in range(3)]
    narrow = dot_nt(jnp.concatenate(kept, axis=0), fold).astype(BF16)
    ordered = dot(
        jnp.concatenate([narrow[a * CH : (a + 1) * CH] for a in range(3)], axis=1), order_ref[...]
    )
    fg[...] = ordered.astype(BF16)
    for out_ref, half in ((other_ref, 1 - core), (mine_ref, core)):
        base = pl.multiple_of(half * F_PART, 16)
        for k in range(6):
            at = (k // 2) * CHUNK + PART + LEFT + (k % 2) * F_PART
            out_ref[pl.ds(at, F_PART), :] = fg[pl.ds(base, F_PART), pl.ds(k * LANES, LANES)]
        out_ref[pl.ds(3 * CHUNK, ROWS - 3 * CHUNK), :] = jnp.zeros((ROWS - 3 * CHUNK, LANES), BF16)
    send_other = pltpu.make_async_copy(other_ref, other_hbm, sems.at[2])
    send_mine = pltpu.make_async_copy(mine_ref, mine_hbm, sems.at[3])
    send_other.start()
    send_mine.start()
    send_wn.wait()
    send_g.wait()
    send_other.wait()
    send_mine.wait()


def tail_kernel(
    after_hbm, g_hbm, wn_hbm, w2_hbm, fw_ref, feat_ref, vg_ref, done_ref,
    g_ref, wn_ref, w2_ref, gs, w1, acc, sems,
):
    fetches = [
        pltpu.make_async_copy(source, target, sems.at[i])
        for i, (source, target) in enumerate(
            ((g_hbm, g_ref), (wn_hbm, wn_ref), (w2_hbm, w2_ref))
        )
    ]
    for fetch in fetches:
        fetch.start()
    done_ref[...] = jnp.zeros((1, LANES), F32)
    mask = group_mask()
    fold = fold_matrix(9 * PG)
    for a in range(3):
        w1[pl.ds(a * CH, CH), :] = expand(fw_ref[pl.ds(a * CH, CH), :], fold, mask)
    fetches[0].wait()
    for j in range(4):
        tiles = [
            [g_ref[j, :, pl.ds((4 * y + q) * LANES, LANES)] for q in range(4)] for y in range(2)
        ]
        fill_windows(gs.at[j], tiles)
    for j in range(4):
        first, last = max(0, j - 1), min(2, j)
        terms = dot(w1[pl.ds(first * CH, (last - first + 1) * CH), :], gs[j])
        for a in range(first, last + 1):
            term = terms[(a - first) * CH : (a - first + 1) * CH]
            out = j - a
            if a == 0:
                acc[out] = term
            else:
                acc[out] += term
    merge = merge_matrix()
    for out in range(2):
        for y in range(2):
            cut = pl.ds(y * 256, 256)
            vg_ref[out, :, cut] = dot(acc[out, :, cut].astype(BF16), merge).astype(BF16)
    fetches[1].wait()
    fetches[2].wait()
    feat_ref[...] = dot_tn(w2_ref[...], wn_ref[...]).astype(BF16)


def add_kernel(mine_hbm, got_hbm, out_hbm, mine_ref, got_ref, sems):
    fetches = [
        pltpu.make_async_copy(mine_hbm, mine_ref, sems.at[0]),
        pltpu.make_async_copy(got_hbm, got_ref, sems.at[1]),
    ]
    for fetch in fetches:
        fetch.start()
    for fetch in fetches:
        fetch.wait()
    got_ref[...] = (mine_ref[...].astype(F32) + got_ref[...].astype(F32)).astype(BF16)
    send = pltpu.make_async_copy(got_ref, out_hbm, sems.at[0])
    send.start()
    send.wait()


def finish_kernel(factor, half_ref, rows_hbm, *refs):
    strided_hbm, grouped_hbm, rows_ref, strided_ref, grouped_ref, fetch_sems, send_sems = refs[-7:]
    half = half_ref[0]
    fetches = [
        pltpu.make_async_copy(
            rows_hbm.at[pl.ds(k * CHUNK, CHUNK)], rows_ref.at[pl.ds(k * CHUNK, CHUNK)], fetch_sems.at[k]
        )
        for k in range(3)
    ]
    for fetch in fetches:
        fetch.start()
    sends = []
    for k in range(3):
        fetches[k].wait()
        at = k * CHUNK
        here = pl.ds(k * PART, PART)
        strided_ref[here, pl.ds(0, LANES)] = rows_ref[pl.ds(at, PART), :].astype(F32) * factor
        rest = rows_ref[pl.ds(at + PART, LEFT), :].astype(F32) * factor
        strided_ref[pl.ds(k * PART, LEFT), pl.ds(LANES, 64)] = rest[:, :64]
        strided_ref[pl.ds(k * PART + LEFT, RIGHT), pl.ds(LANES, 64)] = rest[:RIGHT, 64:]
        there = pl.ds(pl.multiple_of(half * HALF + k * PART, 8), PART)
        sends.append(
            pltpu.make_async_copy(strided_ref.at[here], strided_hbm.at[there], send_sems.at[k])
        )
        sends[-1].start()
        for i in range(2):
            tile = rows_ref[pl.ds(at + PART + LEFT + i * F_PART, F_PART), :]
            grouped_ref[:, pl.ds((2 * k + i) * LANES, LANES)] = tile.astype(F32) * factor
    there = pl.ds(pl.multiple_of(half * F_PART, 8), F_PART)
    sends.append(pltpu.make_async_copy(grouped_ref, grouped_hbm.at[there], send_sems.at[3]))
    sends[-1].start()
    for send in sends:
        send.wait()


VMEM = pl.BlockSpec(memory_space=pltpu.VMEM)
SMEM = pl.BlockSpec(memory_space=pltpu.SMEM)
ANY = pl.BlockSpec(memory_space=pl.ANY)
MIB = 1024 * 1024


def main_call(inner, core, low, own, high, weight, w2, stage=9):
    return pl.pallas_call(
        functools.partial(main_kernel, stage),
        out_shape=(
            jax.ShapeDtypeStruct((ROWS, LANES), BF16),
            jax.ShapeDtypeStruct((ROWS, LANES), BF16),
            jax.ShapeDtypeStruct((TAPS * CH, LANES), BF16),
            jax.ShapeDtypeStruct((4, CH, 8 * LANES), BF16),
        ),
        in_specs=[SMEM, SMEM, ANY, ANY, ANY, VMEM, ANY],
        out_specs=(ANY,) * 4,
        scratch_shapes=[
            pltpu.VMEM((10, CH, LANES), BF16),
            pltpu.VMEM((10, CH, LANES), BF16),
            pltpu.VMEM((10, CH, LANES), BF16),
            pltpu.VMEM((TAPS * CH, 192), BF16),
            pltpu.VMEM((ROWS, LANES), BF16),
            pltpu.VMEM((ROWS, LANES), BF16),
            pltpu.VMEM((TAPS * CH, LANES), BF16),
            pltpu.VMEM((4, CH, 8 * LANES), BF16),
            pltpu.VMEM((6, WIN, 512), BF16),
            pltpu.VMEM((3 * CH, WIN), BF16),
            pltpu.VMEM((4, CH, 512), F32),
            pltpu.VMEM((4, CH, 512), BF16),
            pltpu.VMEM((2, WIN, 512), BF16),
            pltpu.VMEM((768, 768), BF16),
            pltpu.VMEM((CH, 6 * LANES), BF16),
            pltpu.SemaphoreType.DMA((4,)),
        ],
        compiler_params=pltpu.CompilerParams(vmem_limit_bytes=40 * MIB),
        name="main",
    )(inner, core, low, own, high, weight, w2)


def tail_call(chip, grads, windows, w2, weight):
    return pl.pallas_call(
        tail_kernel,
        out_shape=(
            jax.ShapeDtypeStruct((192, LANES), BF16),
            jax.ShapeDtypeStruct((2, CH, 512), BF16),
            jax.ShapeDtypeStruct((1, LANES), F32),
        ),
        in_specs=[ANY, ANY, ANY, ANY, VMEM],
        out_specs=(VMEM,) * 3,
        scratch_shapes=[
            pltpu.VMEM((4, CH, 8 * LANES), BF16),
            pltpu.VMEM((TAPS * CH, LANES), BF16),
            pltpu.VMEM((TAPS * CH, 192), BF16),
            pltpu.VMEM((4, WIN, 512), BF16),
            pltpu.VMEM((3 * CH, WIN), BF16),
            pltpu.VMEM((2, CH, 512), F32),
            pltpu.SemaphoreType.DMA((3,)),
        ],
        compiler_params=pltpu.CompilerParams(vmem_limit_bytes=40 * MIB),
        cost_estimate=pl.CostEstimate(flops=10**9, bytes_accessed=4 * 10**6, transcendentals=0),
        name="tail",
    )(chip, grads, windows, w2, weight)


def add_call(mine, got):
    return pl.pallas_call(
        add_kernel,
        out_shape=jax.ShapeDtypeStruct((ROWS, LANES), BF16),
        in_specs=[ANY, ANY],
        out_specs=ANY,
        scratch_shapes=[
            pltpu.VMEM((ROWS, LANES), BF16),
            pltpu.VMEM((ROWS, LANES), BF16),
            pltpu.SemaphoreType.DMA((2,)),
        ],
        compiler_params=pltpu.CompilerParams(vmem_limit_bytes=16 * MIB),
        name="add",
    )(mine, got)


def finish_call(factor, half, rows, before=()):
    return pl.pallas_call(
        functools.partial(finish_kernel, factor),
        out_shape=(
            jax.ShapeDtypeStruct((TAPS * CH, 192), F32),
            jax.ShapeDtypeStruct((CH, 6 * LANES), F32),
        ),
        in_specs=[SMEM, ANY] + [ANY] * len(before),
        out_specs=(ANY, ANY),
        scratch_shapes=[
            pltpu.VMEM((ROWS, LANES), BF16),
            pltpu.VMEM((HALF, 192), F32),
            pltpu.VMEM((F_PART, 6 * LANES), F32),
            pltpu.SemaphoreType.DMA((3,)),
            pltpu.SemaphoreType.DMA((4,)),
        ],
        input_output_aliases={2 + i: i for i in range(len(before))},
        compiler_params=pltpu.CompilerParams(vmem_limit_bytes=16 * MIB),
        name="finish",
    )(half, rows, *before)


def sum_pieces(parts):
    return jnp.sum(parts.astype(F32), axis=0).astype(BF16)


def to_all(piece, axes, count):
    copies = jnp.broadcast_to(piece[None], (count,) + piece.shape)
    return lax.all_to_all(copies, axes, 0, 0, tiled=True)


def shards(volume, first_weight, second_weight, out_cotangent):
    count = lax.axis_size(SPACE)
    up = [(i, i + 1) for i in range(count - 1)]
    down = [(i + 1, i) for i in range(count - 1)]
    planes = volume.reshape(CH, 2, 2, 2, LANES).transpose(1, 2, 3, 0, 4).reshape(8, CH, LANES)
    own = jnp.concatenate([planes, out_cotangent.reshape(2, CH, LANES)], axis=0)
    low = lax.ppermute(own, SPACE, up)
    high = lax.ppermute(own, SPACE, down)
    core = lax.axis_index("core").astype(jnp.int32).reshape(1)
    inner = jnp.where(lax.axis_index(SPACE) > 0, 1.0, 0.0).astype(F32).reshape(1)
    blocks = first_weight.reshape(3, 9, 4, PG, PG)
    forward_weight = blocks.transpose(0, 2, 4, 1, 3).reshape(3 * CH, 9 * PG)
    backward_weight = blocks[::-1, ::-1].transpose(0, 2, 3, 1, 4).reshape(3 * CH, 9 * PG)
    w2 = second_weight.reshape(TAPS * CH, 192)
    mine, other, windows, grads = main_call(inner, core, low, own, high, forward_weight, w2)
    swap = [(0, 1), (1, 0)]
    chip = add_call(mine, lax.ppermute(other, "core", swap))
    parts = lax.all_to_all(chip.reshape(PIECES, PIECE, LANES), NEAR, 0, 0, tiled=True)
    feat, vgrad, done = tail_call(chip, grads, windows, w2, backward_weight)
    piece = (jnp.sum(parts.astype(F32), axis=0) + done).astype(BF16)
    piece = sum_pieces(to_all(piece, "zh", lax.axis_size("zh")))
    own_half = to_all(piece, NEAR, PIECES).reshape(ROWS, LANES)
    other_half = lax.ppermute(own_half, "core", swap)
    factor = 1.0 / math.sqrt(lax.axis_size(DP) * lax.axis_size(SPACE) * LANES)
    halves = finish_call(factor, core, own_half)
    second_grad, narrow = finish_call(factor, 1 - core, other_half, halves)
    first_grad = narrow[:, : TAPS * PG].reshape(4, PG, PG, TAPS).transpose(3, 0, 1, 2)
    features = feat.reshape(out_cotangent.shape)
    volume_grad = vgrad.reshape(2, CH, 2, 256).transpose(1, 0, 2, 3)[None]
    return (features, volume_grad, first_grad, second_grad.reshape(second_weight.shape))


def solution(mesh):
    fine = Mesh(mesh.devices.reshape(2, 8, 2, 2, 4, 2), ("xh", "zh", "zl", "xl", "y", "core"))
    split = P(DP, None, SPACE, None, None)
    return jax.shard_map(
        shards,
        mesh=fine,
        in_specs=(split, P(), P(), split),
        out_specs=(split, split, P(), P()),
        check_vma=False,
    )
```

```python
import functools
import math

import jax
import jax.numpy as jnp
from jax import lax
from jax.experimental import pallas as pl
from jax.experimental.pallas import tpu as pltpu
from jax.sharding import Mesh
from jax.sharding import PartitionSpec as P

SPACE = ("xl", "y", "core")
DP = ("xh", "zh", "zl")
NEAR = ("xh", "xl", "y", "zl")
F32 = jnp.float32
BF16 = jnp.bfloat16

CH = 96
PG = 24
TAPS = 27
WIN = 9 * CH
LANES = 128
HALF = TAPS * CH // 2
PART = HALF // 3
LEFT, RIGHT = 224, PART - 224
F_PART = CH // 2
CHUNK = PART + LEFT + 2 * F_PART
PIECES = 32
PIECE = 72
ROWS = PIECES * PIECE


def dot(a, b):
    return lax.dot_general(a, b, (((1,), (0,)), ((), ())), preferred_element_type=F32)


def dot_nt(a, b):
    return lax.dot_general(a, b, (((1,), (1,)), ((), ())), preferred_element_type=F32)


def dot_tn(a, b):
    return lax.dot_general(a, b, (((0,), (0,)), ((), ())), preferred_element_type=F32)


def later(tile):
    lane = lax.broadcasted_iota(jnp.int32, tile.shape, 1)
    return jnp.where(lane == 0, 0.0, pltpu.roll(tile, 1, 1))


def earlier(tile):
    lane = lax.broadcasted_iota(jnp.int32, tile.shape, 1)
    return jnp.where(lane == LANES - 1, 0.0, pltpu.roll(tile, LANES - 1, 1))


def fill_windows(ref, tiles):
    zero = jnp.zeros((CH, LANES), BF16)
    for b in range(3):
        for c in range(3):
            rows = pl.ds((b * 3 + c) * CH, CH)
            for y in range(2):
                source = y + b - 1
                if source in (0, 1):
                    even, odd, odd_later, even_earlier = tiles[source]
                    pair = ((odd_later, even), (even, odd), (odd, even_earlier))[c]
                else:
                    pair = (zero, zero)
                for parity in range(2):
                    ref[rows, pl.ds((2 * y + parity) * LANES, LANES)] = pair[parity]


def ones_where(condition):
    return jnp.where(condition, 1.0, 0.0).astype(BF16)


def split_matrix():
    z = lax.broadcasted_iota(jnp.int32, (256, LANES), 0)
    k2 = 2 * lax.broadcasted_iota(jnp.int32, (256, LANES), 1)
    return jnp.concatenate([ones_where(z == k2 + off) for off in (0, 1, -1, 2)], axis=1)


def merge_matrix():
    lane = lax.broadcasted_iota(jnp.int32, (LANES, 256), 0)
    z = lax.broadcasted_iota(jnp.int32, (LANES, 256), 1)
    return jnp.concatenate([ones_where(z == 2 * lane + bit) for bit in (0, 1)], axis=0)


def quotient(value, divisor, bits):
    return (value * (2**bits // divisor + 1)) >> bits


def fold_matrix(rows):
    row = lax.broadcasted_iota(jnp.int32, (rows, WIN), 0)
    column = lax.broadcasted_iota(jnp.int32, (1, WIN), 1)
    target = quotient(column, CH, 16) * PG + column - PG * quotient(column, PG, 16)
    return ones_where(row == target)


def group_mask():
    row = lax.broadcasted_iota(jnp.int32, (CH, WIN), 0)
    column = lax.broadcasted_iota(jnp.int32, (1, WIN), 1)
    offset = row - PG * quotient(column - CH * quotient(column, CH, 16), PG, 16)
    return (offset >= 0) & (offset < PG)


def order_matrix():
    row = lax.broadcasted_iota(jnp.int32, (3 * 256, 6 * LANES), 0)
    column = lax.broadcasted_iota(jnp.int32, (1, 6 * LANES), 1)
    channel = quotient(column, TAPS, 16)
    tap = column - TAPS * channel
    plane = quotient(tap, 9, 16)
    target = plane * 256 + (8 - tap + 9 * plane) * PG + channel
    return ones_where((row == target) & (column < PG * TAPS))


def expand(narrow, fold, mask):
    return jnp.where(mask, dot(narrow, fold), 0.0).astype(BF16)


def cotangent_of(slab):
    return jnp.concatenate([slab[4, :, :LANES], slab[4, :, LANES:]], axis=0)


def main_kernel(
    inner_ref, core_ref, far_hbm, own_hbm, twin_hbm, fw_ref, w2_hbm,
    mine_hbm, other_hbm, wn_hbm, g_hbm,
    beside, own_ref, w2_ref, mine_ref, other_ref, wn_ref, g_ref,
    xs, w1, pre_ref, xc_ref, gs, order_ref, fg, sems,
):
    inner = inner_ref[0]
    core = core_ref[0]
    low_ref, high_ref = beside.at[0], beside.at[1]
    fetches = [
        pltpu.make_async_copy(own_hbm, own_ref, sems.at[0]),
        pltpu.make_async_copy(far_hbm, beside.at[core], sems.at[1]),
        pltpu.make_async_copy(twin_hbm, beside.at[1 - core], sems.at[2]),
        pltpu.make_async_copy(w2_hbm, w2_ref, sems.at[3]),
    ]
    for fetch in fetches:
        fetch.start()
    split = split_matrix()
    mask = group_mask()
    fold = fold_matrix(9 * PG)
    for a in range(3):
        w1[pl.ds(a * CH, CH), :] = expand(fw_ref[pl.ds(a * CH, CH), :], fold, mask)
    fetches[0].wait()
    for e in (2, 3, 0, 1, 4, 5):
        slab = (low_ref, own_ref, high_ref)[e // 2]
        if e == 0:
            fetches[1].wait()
            fetches[2].wait()
        tiles = []
        for y in range(2):
            parts = dot(slab[2 * (e % 2) + y], split).astype(BF16)
            tiles.append([parts[:, q * LANES : (q + 1) * LANES] for q in range(4)])
            if 1 <= e <= 4:
                xc_ref[e - 1, :, pl.ds(y * 256, 256)] = parts[:, :256]
        fill_windows(xs.at[e], tiles)
    for e in range(6):
        first, last = max(0, e - 3), min(2, e)
        terms = dot(w1[pl.ds(first * CH, (last - first + 1) * CH), :], xs[e])
        for a in range(first, last + 1):
            term = terms[(a - first) * CH : (a - first + 1) * CH]
            j = e - a
            if a == 0:
                pre_ref[j] = term
            else:
                pre_ref[j] += term
    zero = jnp.zeros((CH, LANES), BF16)
    for a in range(3):
        for c in range(3):
            wn_ref[pl.ds((9 * a + c) * CH, CH), :] = zero
        for y in range(2):
            value = pre_ref[a, :, pl.ds(y * 256, 256)]
            hidden = value * jax.nn.sigmoid(value)
            if a == 0:
                hidden = hidden * inner
            even, odd = hidden[:, :LANES], hidden[:, LANES:]
            base = (9 * a + 3 * (y + 1)) * CH
            wn_ref[pl.ds(base, CH), :] = later(odd).astype(BF16)
            wn_ref[pl.ds(base + CH, CH), :] = even.astype(BF16)
            wn_ref[pl.ds(base + 2 * CH, CH), :] = odd.astype(BF16)
    send_wn = pltpu.make_async_copy(wn_ref, wn_hbm, sems.at[0])
    send_wn.start()
    cot = cotangent_of(own_ref)
    rest = cot[LANES:]
    none = jnp.zeros_like(rest)
    both = jnp.concatenate(
        [jnp.concatenate([rest, none], axis=1), jnp.concatenate([none, rest], axis=1)], axis=0
    )
    fill = jnp.zeros((LEFT - RIGHT, LANES), BF16)
    for out_ref, half in ((other_ref, 1 - core), (mine_ref, core)):
        for k in range(3):
            base = pl.multiple_of(half * HALF + k * PART, 16)
            wide = dot_nt(wn_ref[pl.ds(base, PART), :], cot[:LANES])
            out_ref[pl.ds(k * CHUNK, PART), :] = wide.astype(BF16)
            left = wn_ref[pl.ds(base, LEFT), :]
            right = jnp.concatenate([wn_ref[pl.ds(base + LEFT, RIGHT), :], fill], axis=0)
            pairs = jnp.concatenate([left, right], axis=1)
            out_ref[pl.ds(k * CHUNK + PART, LEFT), :] = dot_nt(pairs, both).astype(BF16)
    with_above = jnp.concatenate([cot, cotangent_of(high_ref)], axis=1)
    with_below = jnp.concatenate([cot, cotangent_of(low_ref)], axis=1)
    order_ref[...] = order_matrix()
    fetches[3].wait()
    spread = [
        dot(w2_ref[pl.ds((9 * a + 3) * CH, 6 * CH), :], with_below if a == 2 else with_above)
        for a in range(3)
    ]
    for j in range(4):
        sources = {0: ((0, 0), (2, 1)), 1: ((1, 0),), 2: ((2, 0), (0, 1)), 3: ((1, 1),)}[j]
        tiles = []
        for y in range(2):
            got = []
            for c in range(3):
                total = None
                for a, part in sources:
                    tile = spread[a][
                        (3 * y + c) * CH : (3 * y + c + 1) * CH, part * LANES : (part + 1) * LANES
                    ]
                    total = tile if total is None else total + tile
                got.append(total)
            even = got[1]
            odd = got[2] + earlier(got[0])
            value = pre_ref[j, :, pl.ds(y * 256, 256)]
            sigma = jax.nn.sigmoid(value)
            slope = sigma * (1.0 + value * (1.0 - sigma))
            if j == 0:
                slope = slope * inner
            even = even * slope[:, :LANES]
            odd = odd * slope[:, LANES:]
            tiles.append([t.astype(BF16) for t in (even, odd, later(odd), earlier(even))])
            for q in range(4):
                g_ref[j, :, pl.ds((4 * y + q) * LANES, LANES)] = tiles[y][q]
        if j in (1, 2):
            fill_windows(gs.at[j - 1], tiles)
    send_g = pltpu.make_async_copy(g_ref, g_hbm, sems.at[1])
    send_g.start()
    taps = None
    for j in (1, 2):
        planes = jnp.concatenate([xc_ref[j - 1], xc_ref[j], xc_ref[j + 1]], axis=0)
        term = dot_nt(planes, gs[j - 1])
        taps = term if taps is None else taps + term
    fold = fold_matrix(256)
    kept = [jnp.where(mask, taps[a * CH : (a + 1) * CH], 0.0).astype(BF16) for a in range(3)]
    narrow = dot_nt(jnp.concatenate(kept, axis=0), fold).astype(BF16)
    ordered = dot(
        jnp.concatenate([narrow[a * CH : (a + 1) * CH] for a in range(3)], axis=1), order_ref[...]
    )
    fg[...] = ordered.astype(BF16)
    for out_ref, half in ((other_ref, 1 - core), (mine_ref, core)):
        base = pl.multiple_of(half * F_PART, 16)
        for k in range(6):
            at = (k // 2) * CHUNK + PART + LEFT + (k % 2) * F_PART
            out_ref[pl.ds(at, F_PART), :] = fg[pl.ds(base, F_PART), pl.ds(k * LANES, LANES)]
        out_ref[pl.ds(3 * CHUNK, ROWS - 3 * CHUNK), :] = jnp.zeros((ROWS - 3 * CHUNK, LANES), BF16)
    send_other = pltpu.make_async_copy(other_ref, other_hbm, sems.at[2])
    send_mine = pltpu.make_async_copy(mine_ref, mine_hbm, sems.at[3])
    send_other.start()
    send_mine.start()
    send_wn.wait()
    send_g.wait()
    send_other.wait()
    send_mine.wait()


def tail_kernel(
    after_hbm, g_hbm, wn_hbm, w2_hbm, fw_ref, feat_ref, vg_ref,
    g_ref, wn_ref, w2_ref, gs, w1, acc, sems,
):
    fetches = [
        pltpu.make_async_copy(source, target, sems.at[i])
        for i, (source, target) in enumerate(
            ((g_hbm, g_ref), (wn_hbm, wn_ref), (w2_hbm, w2_ref))
        )
    ]
    for fetch in fetches:
        fetch.start()
    mask = group_mask()
    fold = fold_matrix(9 * PG)
    for a in range(3):
        w1[pl.ds(a * CH, CH), :] = expand(fw_ref[pl.ds(a * CH, CH), :], fold, mask)
    fetches[0].wait()
    for j in range(4):
        tiles = [
            [g_ref[j, :, pl.ds((4 * y + q) * LANES, LANES)] for q in range(4)] for y in range(2)
        ]
        fill_windows(gs.at[j], tiles)
    for j in range(4):
        first, last = max(0, j - 1), min(2, j)
        terms = dot(w1[pl.ds(first * CH, (last - first + 1) * CH), :], gs[j])
        for a in range(first, last + 1):
            term = terms[(a - first) * CH : (a - first + 1) * CH]
            out = j - a
            if a == 0:
                acc[out] = term
            else:
                acc[out] += term
    merge = merge_matrix()
    for out in range(2):
        for y in range(2):
            cut = pl.ds(y * 256, 256)
            vg_ref[out, :, cut] = dot(acc[out, :, cut].astype(BF16), merge).astype(BF16)
    fetches[1].wait()
    fetches[2].wait()
    feat_ref[...] = dot_tn(w2_ref[...], wn_ref[...]).astype(BF16)


def add_kernel(mine_hbm, got_hbm, out_hbm, mine_ref, got_ref, sems):
    fetches = [
        pltpu.make_async_copy(mine_hbm, mine_ref, sems.at[0]),
        pltpu.make_async_copy(got_hbm, got_ref, sems.at[1]),
    ]
    for fetch in fetches:
        fetch.start()
    for fetch in fetches:
        fetch.wait()
    got_ref[...] = (mine_ref[...].astype(F32) + got_ref[...].astype(F32)).astype(BF16)
    send = pltpu.make_async_copy(got_ref, out_hbm, sems.at[0])
    send.start()
    send.wait()


def finish_kernel(factor, half_ref, rows_hbm, *refs):
    strided_hbm, grouped_hbm, rows_ref, strided_ref, grouped_ref, fetch_sems, send_sems = refs[-7:]
    half = half_ref[0]
    fetches = [
        pltpu.make_async_copy(
            rows_hbm.at[pl.ds(k * CHUNK, CHUNK)], rows_ref.at[pl.ds(k * CHUNK, CHUNK)], fetch_sems.at[k]
        )
        for k in range(3)
    ]
    for fetch in fetches:
        fetch.start()
    sends = []
    for k in range(3):
        fetches[k].wait()
        at = k * CHUNK
        here = pl.ds(k * PART, PART)
        strided_ref[here, pl.ds(0, LANES)] = rows_ref[pl.ds(at, PART), :].astype(F32) * factor
        rest = rows_ref[pl.ds(at + PART, LEFT), :].astype(F32) * factor
        strided_ref[pl.ds(k * PART, LEFT), pl.ds(LANES, 64)] = rest[:, :64]
        strided_ref[pl.ds(k * PART + LEFT, RIGHT), pl.ds(LANES, 64)] = rest[:RIGHT, 64:]
        there = pl.ds(pl.multiple_of(half * HALF + k * PART, 8), PART)
        sends.append(
            pltpu.make_async_copy(strided_ref.at[here], strided_hbm.at[there], send_sems.at[k])
        )
        sends[-1].start()
        for i in range(2):
            tile = rows_ref[pl.ds(at + PART + LEFT + i * F_PART, F_PART), :]
            grouped_ref[:, pl.ds((2 * k + i) * LANES, LANES)] = tile.astype(F32) * factor
    there = pl.ds(pl.multiple_of(half * F_PART, 8), F_PART)
    sends.append(pltpu.make_async_copy(grouped_ref, grouped_hbm.at[there], send_sems.at[3]))
    sends[-1].start()
    for send in sends:
        send.wait()


VMEM = pl.BlockSpec(memory_space=pltpu.VMEM)
SMEM = pl.BlockSpec(memory_space=pltpu.SMEM)
ANY = pl.BlockSpec(memory_space=pl.ANY)
MIB = 1024 * 1024


def main_call(inner, core, far, own, twin, weight, w2):
    return pl.pallas_call(
        main_kernel,
        out_shape=(
            jax.ShapeDtypeStruct((ROWS, LANES), BF16),
            jax.ShapeDtypeStruct((ROWS, LANES), BF16),
            jax.ShapeDtypeStruct((TAPS * CH, LANES), BF16),
            jax.ShapeDtypeStruct((4, CH, 8 * LANES), BF16),
        ),
        in_specs=[SMEM, SMEM, ANY, ANY, ANY, VMEM, ANY],
        out_specs=(ANY,) * 4,
        scratch_shapes=[
            pltpu.VMEM((2, 5, CH, 256), BF16),
            pltpu.VMEM((5, CH, 256), BF16),
            pltpu.VMEM((TAPS * CH, 192), BF16),
            pltpu.VMEM((ROWS, LANES), BF16),
            pltpu.VMEM((ROWS, LANES), BF16),
            pltpu.VMEM((TAPS * CH, LANES), BF16),
            pltpu.VMEM((4, CH, 8 * LANES), BF16),
            pltpu.VMEM((6, WIN, 512), BF16),
            pltpu.VMEM((3 * CH, WIN), BF16),
            pltpu.VMEM((4, CH, 512), F32),
            pltpu.VMEM((4, CH, 512), BF16),
            pltpu.VMEM((2, WIN, 512), BF16),
            pltpu.VMEM((768, 768), BF16),
            pltpu.VMEM((CH, 6 * LANES), BF16),
            pltpu.SemaphoreType.DMA((4,)),
        ],
        compiler_params=pltpu.CompilerParams(vmem_limit_bytes=40 * MIB),
        name="main",
    )(inner, core, far, own, twin, weight, w2)


def tail_call(after, grads, windows, w2, weight):
    return pl.pallas_call(
        tail_kernel,
        out_shape=(
            jax.ShapeDtypeStruct((192, LANES), BF16),
            jax.ShapeDtypeStruct((2, CH, 512), BF16),
        ),
        in_specs=[ANY, ANY, ANY, ANY, VMEM],
        out_specs=(VMEM,) * 2,
        scratch_shapes=[
            pltpu.VMEM((4, CH, 8 * LANES), BF16),
            pltpu.VMEM((TAPS * CH, LANES), BF16),
            pltpu.VMEM((TAPS * CH, 192), BF16),
            pltpu.VMEM((4, WIN, 512), BF16),
            pltpu.VMEM((3 * CH, WIN), BF16),
            pltpu.VMEM((2, CH, 512), F32),
            pltpu.SemaphoreType.DMA((3,)),
        ],
        compiler_params=pltpu.CompilerParams(vmem_limit_bytes=40 * MIB),
        cost_estimate=pl.CostEstimate(flops=10**9, bytes_accessed=4 * 10**6, transcendentals=0),
        name="tail",
    )(after, grads, windows, w2, weight)


def add_call(mine, got):
    return pl.pallas_call(
        add_kernel,
        out_shape=jax.ShapeDtypeStruct((ROWS, LANES), BF16),
        in_specs=[ANY, ANY],
        out_specs=ANY,
        scratch_shapes=[
            pltpu.VMEM((ROWS, LANES), BF16),
            pltpu.VMEM((ROWS, LANES), BF16),
            pltpu.SemaphoreType.DMA((2,)),
        ],
        compiler_params=pltpu.CompilerParams(vmem_limit_bytes=16 * MIB),
        name="add",
    )(mine, got)


def finish_call(factor, half, rows, before=()):
    return pl.pallas_call(
        functools.partial(finish_kernel, factor),
        out_shape=(
            jax.ShapeDtypeStruct((TAPS * CH, 192), F32),
            jax.ShapeDtypeStruct((CH, 6 * LANES), F32),
        ),
        in_specs=[SMEM, ANY] + [ANY] * len(before),
        out_specs=(ANY, ANY),
        scratch_shapes=[
            pltpu.VMEM((ROWS, LANES), BF16),
            pltpu.VMEM((HALF, 192), F32),
            pltpu.VMEM((F_PART, 6 * LANES), F32),
            pltpu.SemaphoreType.DMA((3,)),
            pltpu.SemaphoreType.DMA((4,)),
        ],
        input_output_aliases={2 + i: i for i in range(len(before))},
        compiler_params=pltpu.CompilerParams(vmem_limit_bytes=16 * MIB),
        name="finish",
    )(half, rows, *before)


def sum_kernel(parts_ref, after_hbm, out_ref):
    total = parts_ref[0].astype(F32)
    for k in range(1, parts_ref.shape[0]):
        total = total + parts_ref[k].astype(F32)
    out_ref[...] = total.astype(BF16)


def sum_call(parts, after):
    return pl.pallas_call(
        sum_kernel,
        out_shape=jax.ShapeDtypeStruct(parts.shape[1:], BF16),
        in_specs=[VMEM, ANY],
        out_specs=VMEM,
        name="sum",
    )(parts, after)


def sum_pieces(parts):
    return jnp.sum(parts.astype(F32), axis=0).astype(BF16)


def to_all(piece, axes, count):
    copies = jnp.broadcast_to(piece[None], (count,) + piece.shape)
    return lax.all_to_all(copies, axes, 0, 0, tiled=True)


def shards(volume, first_weight, second_weight, out_cotangent):
    count = lax.axis_size(SPACE)
    planes = volume[0].transpose(1, 2, 0, 3).reshape(4, CH, 256)
    cotangent = out_cotangent.reshape(2, CH, LANES).transpose(1, 0, 2).reshape(1, CH, 256)
    own = jnp.concatenate([planes, cotangent], axis=0)
    far = lax.ppermute(
        own,
        SPACE,
        [(i, i + 1) for i in range(1, count - 1, 2)] + [(i, i - 1) for i in range(2, count, 2)],
    )
    swap = [(0, 1), (1, 0)]
    twin = lax.ppermute(own, "core", swap)
    core = lax.axis_index("core").astype(jnp.int32).reshape(1)
    inner = jnp.where(lax.axis_index(SPACE) > 0, 1.0, 0.0).astype(F32).reshape(1)
    blocks = first_weight.reshape(3, 9, 4, PG, PG)
    forward_weight = blocks.transpose(0, 2, 4, 1, 3).reshape(3 * CH, 9 * PG)
    backward_weight = blocks[::-1, ::-1].transpose(0, 2, 3, 1, 4).reshape(3 * CH, 9 * PG)
    w2 = second_weight.reshape(TAPS * CH, 192)
    mine, other, windows, grads = main_call(inner, core, far, own, twin, forward_weight, w2)
    chip = add_call(mine, lax.ppermute(other, "core", swap))
    parts = lax.all_to_all(chip.reshape(PIECES, PIECE, LANES), NEAR, 0, 0, tiled=True)
    piece = sum_pieces(parts)
    feat, vgrad = tail_call(piece, grads, windows, w2, backward_weight)
    features = feat.reshape(out_cotangent.shape)
    volume_grad = vgrad.reshape(2, CH, 2, 256).transpose(1, 0, 2, 3)
    piece = sum_call(to_all(piece, "zh", lax.axis_size("zh")), volume_grad)
    own_half = to_all(piece, NEAR, PIECES).reshape(ROWS, LANES)
    other_half = lax.ppermute(own_half, "core", swap)
    factor = 1.0 / math.sqrt(lax.axis_size(DP) * lax.axis_size(SPACE) * LANES)
    halves = finish_call(factor, core, own_half)
    second_grad, narrow = finish_call(factor, 1 - core, other_half, halves)
    first_grad = narrow[:, : TAPS * PG].reshape(4, PG, PG, TAPS).transpose(3, 0, 1, 2)
    return (features, volume_grad[None], first_grad, second_grad.reshape(second_weight.shape))


def solution(mesh):
    fine = Mesh(mesh.devices.reshape(2, 8, 2, 2, 4, 2), ("xh", "zh", "zl", "xl", "y", "core"))
    split = P(DP, None, SPACE, None, None)
    return jax.shard_map(
        shards,
        mesh=fine,
        in_specs=(split, P(), P(), split),
        out_specs=(split, split, P(), P()),
        check_vma=False,
    )
```

```python
import functools
import math

import jax
import jax.numpy as jnp
from jax import lax
from jax.experimental import pallas as pl
from jax.experimental.pallas import tpu as pltpu
from jax.sharding import Mesh
from jax.sharding import PartitionSpec as P

SPACE = ("xl", "y", "core")
DP = ("xh", "zh", "zl")
NEAR = ("xh", "xl", "y", "zl")
F32 = jnp.float32
BF16 = jnp.bfloat16

CH = 96
PG = 24
TAPS = 27
WIN = 9 * CH
LANES = 128
HALF = TAPS * CH // 2
PART = HALF // 3
LEFT, RIGHT = 224, PART - 224
F_PART = CH // 2
CHUNK = PART + LEFT + 2 * F_PART
PIECES = 32
PIECE = 72
ROWS = PIECES * PIECE


def dot(a, b):
    return lax.dot_general(a, b, (((1,), (0,)), ((), ())), preferred_element_type=F32)


def dot_nt(a, b):
    return lax.dot_general(a, b, (((1,), (1,)), ((), ())), preferred_element_type=F32)


def dot_tn(a, b):
    return lax.dot_general(a, b, (((0,), (0,)), ((), ())), preferred_element_type=F32)


def later(tile):
    lane = lax.broadcasted_iota(jnp.int32, tile.shape, 1)
    return jnp.where(lane == 0, 0.0, pltpu.roll(tile, 1, 1))


def earlier(tile):
    lane = lax.broadcasted_iota(jnp.int32, tile.shape, 1)
    return jnp.where(lane == LANES - 1, 0.0, pltpu.roll(tile, LANES - 1, 1))


def fill_windows(ref, tiles):
    zero = jnp.zeros((CH, LANES), BF16)
    for b in range(3):
        for c in range(3):
            rows = pl.ds((b * 3 + c) * CH, CH)
            for y in range(2):
                source = y + b - 1
                if source in (0, 1):
                    even, odd, odd_later, even_earlier = tiles[source]
                    pair = ((odd_later, even), (even, odd), (odd, even_earlier))[c]
                else:
                    pair = (zero, zero)
                for parity in range(2):
                    ref[rows, pl.ds((2 * y + parity) * LANES, LANES)] = pair[parity]


def ones_where(condition):
    return jnp.where(condition, 1.0, 0.0).astype(BF16)


def split_matrix():
    z = lax.broadcasted_iota(jnp.int32, (256, LANES), 0)
    k2 = 2 * lax.broadcasted_iota(jnp.int32, (256, LANES), 1)
    return jnp.concatenate([ones_where(z == k2 + off) for off in (0, 1, -1, 2)], axis=1)


def merge_matrix():
    lane = lax.broadcasted_iota(jnp.int32, (LANES, 256), 0)
    z = lax.broadcasted_iota(jnp.int32, (LANES, 256), 1)
    return jnp.concatenate([ones_where(z == 2 * lane + bit) for bit in (0, 1)], axis=0)


def quotient(value, divisor, bits):
    return (value * (2**bits // divisor + 1)) >> bits


def fold_matrix(rows):
    row = lax.broadcasted_iota(jnp.int32, (rows, WIN), 0)
    column = lax.broadcasted_iota(jnp.int32, (1, WIN), 1)
    target = quotient(column, CH, 16) * PG + column - PG * quotient(column, PG, 16)
    return ones_where(row == target)


def group_mask():
    row = lax.broadcasted_iota(jnp.int32, (CH, WIN), 0)
    column = lax.broadcasted_iota(jnp.int32, (1, WIN), 1)
    offset = row - PG * quotient(column - CH * quotient(column, CH, 16), PG, 16)
    return (offset >= 0) & (offset < PG)


def order_matrix():
    row = lax.broadcasted_iota(jnp.int32, (3 * 256, 6 * LANES), 0)
    column = lax.broadcasted_iota(jnp.int32, (1, 6 * LANES), 1)
    channel = quotient(column, TAPS, 16)
    tap = column - TAPS * channel
    plane = quotient(tap, 9, 16)
    target = plane * 256 + (8 - tap + 9 * plane) * PG + channel
    return ones_where((row == target) & (column < PG * TAPS))


def expand(narrow, fold, mask):
    return jnp.where(mask, dot(narrow, fold), 0.0).astype(BF16)


def prepare_kernel(fw_ref, w1_hbm, w1, sem):
    row = lax.broadcasted_iota(jnp.int32, (3 * 256, PG * TAPS), 0)
    column = lax.broadcasted_iota(jnp.int32, (1, PG * TAPS), 1)
    channel = quotient(column, TAPS, 16)
    tap = column - TAPS * channel
    plane = quotient(tap, 9, 16)
    order = ones_where(row == plane * 256 + (tap - 9 * plane) * PG + channel)
    narrow = dot_nt(fw_ref[...], order).astype(BF16)
    mask = group_mask()
    fold = fold_matrix(256)
    for a in range(3):
        w1[pl.ds(a * CH, CH), :] = expand(narrow[:, a * 256 : (a + 1) * 256], fold, mask)
    send = pltpu.make_async_copy(w1, w1_hbm, sem)
    send.start()
    send.wait()


def cotangent_of(slab):
    return jnp.concatenate([slab[4, :, :LANES], slab[4, :, LANES:]], axis=0)


def main_kernel(
    inner_ref, core_ref, far_hbm, own_hbm, twin_hbm, w1_hbm, w2_hbm,
    mine_hbm, other_hbm, wn_hbm, g_hbm,
    beside, own_ref, w2_ref, mine_ref, other_ref, wn_ref, g_ref,
    xs, w1, pre_ref, xc_ref, gs, order_ref, fg, sems,
):
    inner = inner_ref[0]
    core = core_ref[0]
    low_ref, high_ref = beside.at[0], beside.at[1]
    fetches = [
        pltpu.make_async_copy(own_hbm, own_ref, sems.at[0]),
        pltpu.make_async_copy(far_hbm, beside.at[core], sems.at[1]),
        pltpu.make_async_copy(twin_hbm, beside.at[1 - core], sems.at[2]),
        pltpu.make_async_copy(w1_hbm, w1, sems.at[3]),
        pltpu.make_async_copy(w2_hbm, w2_ref, sems.at[4]),
    ]
    for fetch in fetches:
        fetch.start()
    split = split_matrix()
    mask = group_mask()
    fetches[0].wait()
    for e in (2, 3, 0, 1, 4, 5):
        slab = (low_ref, own_ref, high_ref)[e // 2]
        if e == 0:
            fetches[1].wait()
            fetches[2].wait()
        tiles = []
        for y in range(2):
            parts = dot(slab[2 * (e % 2) + y], split).astype(BF16)
            tiles.append([parts[:, q * LANES : (q + 1) * LANES] for q in range(4)])
            if 1 <= e <= 4:
                xc_ref[e - 1, :, pl.ds(y * 256, 256)] = parts[:, :256]
        fill_windows(xs.at[e], tiles)
    fetches[3].wait()
    for e in range(6):
        first, last = max(0, e - 3), min(2, e)
        terms = dot(w1[pl.ds(first * CH, (last - first + 1) * CH), :], xs[e])
        for a in range(first, last + 1):
            term = terms[(a - first) * CH : (a - first + 1) * CH]
            j = e - a
            if a == 0:
                pre_ref[j] = term
            else:
                pre_ref[j] += term
    zero = jnp.zeros((CH, LANES), BF16)
    for a in range(3):
        for c in range(3):
            wn_ref[pl.ds((9 * a + c) * CH, CH), :] = zero
        for y in range(2):
            value = pre_ref[a, :, pl.ds(y * 256, 256)]
            hidden = value * jax.nn.sigmoid(value)
            if a == 0:
                hidden = hidden * inner
            even, odd = hidden[:, :LANES], hidden[:, LANES:]
            base = (9 * a + 3 * (y + 1)) * CH
            wn_ref[pl.ds(base, CH), :] = later(odd).astype(BF16)
            wn_ref[pl.ds(base + CH, CH), :] = even.astype(BF16)
            wn_ref[pl.ds(base + 2 * CH, CH), :] = odd.astype(BF16)
    send_wn = pltpu.make_async_copy(wn_ref, wn_hbm, sems.at[0])
    send_wn.start()
    cot = cotangent_of(own_ref)
    rest = cot[LANES:]
    none = jnp.zeros_like(rest)
    both = jnp.concatenate(
        [jnp.concatenate([rest, none], axis=1), jnp.concatenate([none, rest], axis=1)], axis=0
    )
    fill = jnp.zeros((LEFT - RIGHT, LANES), BF16)
    for out_ref, half in ((other_ref, 1 - core), (mine_ref, core)):
        for k in range(3):
            base = pl.multiple_of(half * HALF + k * PART, 16)
            wide = dot_nt(wn_ref[pl.ds(base, PART), :], cot[:LANES])
            out_ref[pl.ds(k * CHUNK, PART), :] = wide.astype(BF16)
            left = wn_ref[pl.ds(base, LEFT), :]
            right = jnp.concatenate([wn_ref[pl.ds(base + LEFT, RIGHT), :], fill], axis=0)
            pairs = jnp.concatenate([left, right], axis=1)
            out_ref[pl.ds(k * CHUNK + PART, LEFT), :] = dot_nt(pairs, both).astype(BF16)
    with_above = jnp.concatenate([cot, cotangent_of(high_ref)], axis=1)
    with_below = jnp.concatenate([cot, cotangent_of(low_ref)], axis=1)
    order_ref[...] = order_matrix()
    fetches[4].wait()
    spread = [
        dot(w2_ref[pl.ds((9 * a + 3) * CH, 6 * CH), :], with_below if a == 2 else with_above)
        for a in range(3)
    ]
    for j in range(4):
        sources = {0: ((0, 0), (2, 1)), 1: ((1, 0),), 2: ((2, 0), (0, 1)), 3: ((1, 1),)}[j]
        tiles = []
        for y in range(2):
            got = []
            for c in range(3):
                total = None
                for a, part in sources:
                    tile = spread[a][
                        (3 * y + c) * CH : (3 * y + c + 1) * CH, part * LANES : (part + 1) * LANES
                    ]
                    total = tile if total is None else total + tile
                got.append(total)
            even = got[1]
            odd = got[2] + earlier(got[0])
            value = pre_ref[j, :, pl.ds(y * 256, 256)]
            sigma = jax.nn.sigmoid(value)
            slope = sigma * (1.0 + value * (1.0 - sigma))
            if j == 0:
                slope = slope * inner
            even = even * slope[:, :LANES]
            odd = odd * slope[:, LANES:]
            tiles.append([t.astype(BF16) for t in (even, odd, later(odd), earlier(even))])
            for q in range(4):
                g_ref[j, :, pl.ds((4 * y + q) * LANES, LANES)] = tiles[y][q]
        if j in (1, 2):
            fill_windows(gs.at[j - 1], tiles)
    send_g = pltpu.make_async_copy(g_ref, g_hbm, sems.at[1])
    send_g.start()
    taps = None
    for j in (1, 2):
        planes = jnp.concatenate([xc_ref[j - 1], xc_ref[j], xc_ref[j + 1]], axis=0)
        term = dot_nt(planes, gs[j - 1])
        taps = term if taps is None else taps + term
    fold = fold_matrix(256)
    kept = [jnp.where(mask, taps[a * CH : (a + 1) * CH], 0.0).astype(BF16) for a in range(3)]
    narrow = dot_nt(jnp.concatenate(kept, axis=0), fold).astype(BF16)
    ordered = dot(
        jnp.concatenate([narrow[a * CH : (a + 1) * CH] for a in range(3)], axis=1), order_ref[...]
    )
    fg[...] = ordered.astype(BF16)
    for out_ref, half in ((other_ref, 1 - core), (mine_ref, core)):
        base = pl.multiple_of(half * F_PART, 16)
        for k in range(6):
            at = (k // 2) * CHUNK + PART + LEFT + (k % 2) * F_PART
            out_ref[pl.ds(at, F_PART), :] = fg[pl.ds(base, F_PART), pl.ds(k * LANES, LANES)]
        out_ref[pl.ds(3 * CHUNK, ROWS - 3 * CHUNK), :] = jnp.zeros((ROWS - 3 * CHUNK, LANES), BF16)
    send_other = pltpu.make_async_copy(other_ref, other_hbm, sems.at[2])
    send_mine = pltpu.make_async_copy(mine_ref, mine_hbm, sems.at[3])
    send_other.start()
    send_mine.start()
    send_wn.wait()
    send_g.wait()
    send_other.wait()
    send_mine.wait()


def tail_kernel(
    after_hbm, g_hbm, wn_hbm, w2_hbm, fw_ref, feat_ref, vg_ref,
    g_ref, wn_ref, w2_ref, gs, w1, acc, sems,
):
    fetches = [
        pltpu.make_async_copy(source, target, sems.at[i])
        for i, (source, target) in enumerate(
            ((g_hbm, g_ref), (wn_hbm, wn_ref), (w2_hbm, w2_ref))
        )
    ]
    for fetch in fetches:
        fetch.start()
    mask = group_mask()
    fold = fold_matrix(9 * PG)
    for a in range(3):
        w1[pl.ds(a * CH, CH), :] = expand(fw_ref[pl.ds(a * CH, CH), :], fold, mask)
    fetches[0].wait()
    for j in range(4):
        tiles = [
            [g_ref[j, :, pl.ds((4 * y + q) * LANES, LANES)] for q in range(4)] for y in range(2)
        ]
        fill_windows(gs.at[j], tiles)
    for j in range(4):
        first, last = max(0, j - 1), min(2, j)
        terms = dot(w1[pl.ds(first * CH, (last - first + 1) * CH), :], gs[j])
        for a in range(first, last + 1):
            term = terms[(a - first) * CH : (a - first + 1) * CH]
            out = j - a
            if a == 0:
                acc[out] = term
            else:
                acc[out] += term
    merge = merge_matrix()
    for out in range(2):
        for y in range(2):
            cut = pl.ds(y * 256, 256)
            vg_ref[out, :, cut] = dot(acc[out, :, cut].astype(BF16), merge).astype(BF16)
    fetches[1].wait()
    fetches[2].wait()
    feat_ref[...] = dot_tn(w2_ref[...], wn_ref[...]).astype(BF16)


def add_kernel(mine_hbm, got_hbm, out_hbm, mine_ref, got_ref, sems):
    fetches = [
        pltpu.make_async_copy(mine_hbm, mine_ref, sems.at[0]),
        pltpu.make_async_copy(got_hbm, got_ref, sems.at[1]),
    ]
    for fetch in fetches:
        fetch.start()
    for fetch in fetches:
        fetch.wait()
    got_ref[...] = (mine_ref[...].astype(F32) + got_ref[...].astype(F32)).astype(BF16)
    send = pltpu.make_async_copy(got_ref, out_hbm, sems.at[0])
    send.start()
    send.wait()


def finish_kernel(factor, half_ref, rows_hbm, *refs):
    strided_hbm, grouped_hbm, rows_ref, strided_ref, grouped_ref, fetch_sems, send_sems = refs[-7:]
    half = half_ref[0]
    fetches = [
        pltpu.make_async_copy(
            rows_hbm.at[pl.ds(k * CHUNK, CHUNK)], rows_ref.at[pl.ds(k * CHUNK, CHUNK)], fetch_sems.at[k]
        )
        for k in range(3)
    ]
    for fetch in fetches:
        fetch.start()
    sends = []
    for k in range(3):
        fetches[k].wait()
        at = k * CHUNK
        here = pl.ds(k * PART, PART)
        strided_ref[here, pl.ds(0, LANES)] = rows_ref[pl.ds(at, PART), :].astype(F32) * factor
        rest = rows_ref[pl.ds(at + PART, LEFT), :].astype(F32) * factor
        strided_ref[pl.ds(k * PART, LEFT), pl.ds(LANES, 64)] = rest[:, :64]
        strided_ref[pl.ds(k * PART + LEFT, RIGHT), pl.ds(LANES, 64)] = rest[:RIGHT, 64:]
        there = pl.ds(pl.multiple_of(half * HALF + k * PART, 8), PART)
        sends.append(
            pltpu.make_async_copy(strided_ref.at[here], strided_hbm.at[there], send_sems.at[k])
        )
        sends[-1].start()
        for i in range(2):
            tile = rows_ref[pl.ds(at + PART + LEFT + i * F_PART, F_PART), :]
            grouped_ref[:, pl.ds((2 * k + i) * LANES, LANES)] = tile.astype(F32) * factor
    there = pl.ds(pl.multiple_of(half * F_PART, 8), F_PART)
    sends.append(pltpu.make_async_copy(grouped_ref, grouped_hbm.at[there], send_sems.at[3]))
    sends[-1].start()
    for send in sends:
        send.wait()


VMEM = pl.BlockSpec(memory_space=pltpu.VMEM)
SMEM = pl.BlockSpec(memory_space=pltpu.SMEM)
ANY = pl.BlockSpec(memory_space=pl.ANY)
MIB = 1024 * 1024


def prepare_call(weight):
    return pl.pallas_call(
        prepare_kernel,
        out_shape=jax.ShapeDtypeStruct((3 * CH, WIN), BF16),
        in_specs=[VMEM],
        out_specs=ANY,
        scratch_shapes=[pltpu.VMEM((3 * CH, WIN), BF16), pltpu.SemaphoreType.DMA],
        compiler_params=pltpu.CompilerParams(vmem_limit_bytes=16 * MIB),
        name="prepare",
    )(weight)


def main_call(inner, core, far, own, twin, weight, w2):
    return pl.pallas_call(
        main_kernel,
        out_shape=(
            jax.ShapeDtypeStruct((ROWS, LANES), BF16),
            jax.ShapeDtypeStruct((ROWS, LANES), BF16),
            jax.ShapeDtypeStruct((TAPS * CH, LANES), BF16),
            jax.ShapeDtypeStruct((4, CH, 8 * LANES), BF16),
        ),
        in_specs=[SMEM, SMEM] + [ANY] * 5,
        out_specs=(ANY,) * 4,
        scratch_shapes=[
            pltpu.VMEM((2, 5, CH, 256), BF16),
            pltpu.VMEM((5, CH, 256), BF16),
            pltpu.VMEM((TAPS * CH, 192), BF16),
            pltpu.VMEM((ROWS, LANES), BF16),
            pltpu.VMEM((ROWS, LANES), BF16),
            pltpu.VMEM((TAPS * CH, LANES), BF16),
            pltpu.VMEM((4, CH, 8 * LANES), BF16),
            pltpu.VMEM((6, WIN, 512), BF16),
            pltpu.VMEM((3 * CH, WIN), BF16),
            pltpu.VMEM((4, CH, 512), F32),
            pltpu.VMEM((4, CH, 512), BF16),
            pltpu.VMEM((2, WIN, 512), BF16),
            pltpu.VMEM((768, 768), BF16),
            pltpu.VMEM((CH, 6 * LANES), BF16),
            pltpu.SemaphoreType.DMA((5,)),
        ],
        compiler_params=pltpu.CompilerParams(vmem_limit_bytes=40 * MIB),
        name="main",
    )(inner, core, far, own, twin, weight, w2)


def tail_call(after, grads, windows, w2, weight):
    return pl.pallas_call(
        tail_kernel,
        out_shape=(
            jax.ShapeDtypeStruct((192, LANES), BF16),
            jax.ShapeDtypeStruct((2, CH, 512), BF16),
        ),
        in_specs=[ANY, ANY, ANY, ANY, VMEM],
        out_specs=(VMEM,) * 2,
        scratch_shapes=[
            pltpu.VMEM((4, CH, 8 * LANES), BF16),
            pltpu.VMEM((TAPS * CH, LANES), BF16),
            pltpu.VMEM((TAPS * CH, 192), BF16),
            pltpu.VMEM((4, WIN, 512), BF16),
            pltpu.VMEM((3 * CH, WIN), BF16),
            pltpu.VMEM((2, CH, 512), F32),
            pltpu.SemaphoreType.DMA((3,)),
        ],
        compiler_params=pltpu.CompilerParams(vmem_limit_bytes=40 * MIB),
        cost_estimate=pl.CostEstimate(flops=10**9, bytes_accessed=4 * 10**6, transcendentals=0),
        name="tail",
    )(after, grads, windows, w2, weight)


def add_call(mine, got):
    return pl.pallas_call(
        add_kernel,
        out_shape=jax.ShapeDtypeStruct((ROWS, LANES), BF16),
        in_specs=[ANY, ANY],
        out_specs=ANY,
        scratch_shapes=[
            pltpu.VMEM((ROWS, LANES), BF16),
            pltpu.VMEM((ROWS, LANES), BF16),
            pltpu.SemaphoreType.DMA((2,)),
        ],
        compiler_params=pltpu.CompilerParams(vmem_limit_bytes=16 * MIB),
        name="add",
    )(mine, got)


def finish_call(factor, half, rows, before=()):
    return pl.pallas_call(
        functools.partial(finish_kernel, factor),
        out_shape=(
            jax.ShapeDtypeStruct((TAPS * CH, 192), F32),
            jax.ShapeDtypeStruct((CH, 6 * LANES), F32),
        ),
        in_specs=[SMEM, ANY] + [ANY] * len(before),
        out_specs=(ANY, ANY),
        scratch_shapes=[
            pltpu.VMEM((ROWS, LANES), BF16),
            pltpu.VMEM((HALF, 192), F32),
            pltpu.VMEM((F_PART, 6 * LANES), F32),
            pltpu.SemaphoreType.DMA((3,)),
            pltpu.SemaphoreType.DMA((4,)),
        ],
        input_output_aliases={2 + i: i for i in range(len(before))},
        compiler_params=pltpu.CompilerParams(vmem_limit_bytes=16 * MIB),
        name="finish",
    )(half, rows, *before)


def zero_kernel(after_hbm, out_ref):
    out_ref[0] = 0.0


def zero_call(after):
    return pl.pallas_call(
        zero_kernel,
        out_shape=jax.ShapeDtypeStruct((1,), F32),
        in_specs=[ANY],
        out_specs=SMEM,
        name="zero",
    )(after)


def sum_pieces(parts):
    return jnp.sum(parts.astype(F32), axis=0).astype(BF16)


def to_all(piece, axes, count):
    copies = jnp.broadcast_to(piece[None], (count,) + piece.shape)
    return lax.all_to_all(copies, axes, 0, 0, tiled=True)


def shards(volume, first_weight, second_weight, out_cotangent):
    count = lax.axis_size(SPACE)
    planes = volume[0].transpose(1, 2, 0, 3).reshape(4, CH, 256)
    cotangent = out_cotangent.reshape(2, CH, LANES).transpose(1, 0, 2).reshape(1, CH, 256)
    own = jnp.concatenate([planes, cotangent], axis=0)
    swap = [(0, 1), (1, 0)]
    twin = lax.ppermute(own, "core", swap)
    far = lax.ppermute(
        own,
        SPACE,
        [(i, i + 1) for i in range(1, count - 1, 2)] + [(i, i - 1) for i in range(2, count, 2)],
    )
    core = lax.axis_index("core").astype(jnp.int32).reshape(1)
    inner = jnp.where(lax.axis_index(SPACE) > 0, 1.0, 0.0).astype(F32).reshape(1)
    blocks = first_weight.reshape(3, 9, 4, PG, PG)
    forward_weight = prepare_call(first_weight.transpose(1, 3, 2, 0).reshape(CH, PG * TAPS))
    backward_weight = blocks[::-1, ::-1].transpose(0, 2, 3, 1, 4).reshape(3 * CH, 9 * PG)
    w2 = second_weight.reshape(TAPS * CH, 192)
    mine, other, windows, grads = main_call(inner, core, far, own, twin, forward_weight, w2)
    chip = add_call(mine, lax.ppermute(other, "core", swap))
    parts = lax.all_to_all(chip.reshape(PIECES, PIECE, LANES), NEAR, 0, 0, tiled=True)
    piece = sum_pieces(parts)
    feat, vgrad = tail_call(piece, grads, windows, w2, backward_weight)
    features = feat.reshape(out_cotangent.shape)
    volume_grad = vgrad.reshape(2, CH, 2, 256).transpose(1, 0, 2, 3)
    parts = to_all(piece, "zh", lax.axis_size("zh"))
    piece = lax.reduce(parts.astype(F32), zero_call(volume_grad)[0], lax.add, (0,)).astype(BF16)
    own_half = to_all(piece, NEAR, PIECES).reshape(ROWS, LANES)
    other_half = lax.ppermute(own_half, "core", swap)
    factor = 1.0 / math.sqrt(lax.axis_size(DP) * lax.axis_size(SPACE) * LANES)
    halves = finish_call(factor, core, own_half)
    second_grad, narrow = finish_call(factor, 1 - core, other_half, halves)
    first_grad = narrow[:, : TAPS * PG].reshape(4, PG, PG, TAPS).transpose(3, 0, 1, 2)
    return (features, volume_grad[None], first_grad, second_grad.reshape(second_weight.shape))


def solution(mesh):
    fine = Mesh(mesh.devices.reshape(2, 8, 2, 2, 4, 2), ("xh", "zh", "zl", "xl", "y", "core"))
    split = P(DP, None, SPACE, None, None)
    return jax.shard_map(
        shards,
        mesh=fine,
        in_specs=(split, P(), P(), split),
        out_specs=(split, split, P(), P()),
        check_vma=False,
    )
```

```python
import functools
import math

import jax
import jax.numpy as jnp
from jax import lax
from jax.experimental import pallas as pl
from jax.experimental.pallas import tpu as pltpu
from jax.sharding import Mesh
from jax.sharding import PartitionSpec as P

SPACE = ("xl", "y", "core")
DP = ("xh", "zh", "zl")
NEAR = ("xh", "xl", "y", "zl")
F32 = jnp.float32
BF16 = jnp.bfloat16

CH = 96
PG = 24
TAPS = 27
WIN = 9 * CH
LANES = 128
HALF = TAPS * CH // 2
PART = HALF // 3
LEFT, RIGHT = 224, PART - 224
F_PART = CH // 2
CHUNK = PART + LEFT + 2 * F_PART
PIECES = 32
PIECE = 72
ROWS = PIECES * PIECE


def dot(a, b):
    return lax.dot_general(a, b, (((1,), (0,)), ((), ())), preferred_element_type=F32)


def dot_nt(a, b):
    return lax.dot_general(a, b, (((1,), (1,)), ((), ())), preferred_element_type=F32)


def dot_tn(a, b):
    return lax.dot_general(a, b, (((0,), (0,)), ((), ())), preferred_element_type=F32)


def later(tile):
    lane = lax.broadcasted_iota(jnp.int32, tile.shape, 1)
    return jnp.where(lane == 0, 0.0, pltpu.roll(tile, 1, 1))


def earlier(tile):
    lane = lax.broadcasted_iota(jnp.int32, tile.shape, 1)
    return jnp.where(lane == LANES - 1, 0.0, pltpu.roll(tile, LANES - 1, 1))


def fill_windows(ref, tiles):
    zero = jnp.zeros((CH, LANES), BF16)
    for b in range(3):
        for c in range(3):
            rows = pl.ds((b * 3 + c) * CH, CH)
            for y in range(2):
                source = y + b - 1
                if source in (0, 1):
                    even, odd, odd_later, even_earlier = tiles[source]
                    pair = ((odd_later, even), (even, odd), (odd, even_earlier))[c]
                else:
                    pair = (zero, zero)
                for parity in range(2):
                    ref[rows, pl.ds((2 * y + parity) * LANES, LANES)] = pair[parity]


def ones_where(condition):
    return jnp.where(condition, 1.0, 0.0).astype(BF16)


def split_matrix():
    z = lax.broadcasted_iota(jnp.int32, (256, LANES), 0)
    k2 = 2 * lax.broadcasted_iota(jnp.int32, (256, LANES), 1)
    return jnp.concatenate([ones_where(z == k2 + off) for off in (0, 1, -1, 2)], axis=1)


def merge_matrix():
    lane = lax.broadcasted_iota(jnp.int32, (LANES, 256), 0)
    z = lax.broadcasted_iota(jnp.int32, (LANES, 256), 1)
    return jnp.concatenate([ones_where(z == 2 * lane + bit) for bit in (0, 1)], axis=0)


def quotient(value, divisor, bits):
    return (value * (2**bits // divisor + 1)) >> bits


def fold_matrix(rows):
    row = lax.broadcasted_iota(jnp.int32, (rows, WIN), 0)
    column = lax.broadcasted_iota(jnp.int32, (1, WIN), 1)
    target = quotient(column, CH, 16) * PG + column - PG * quotient(column, PG, 16)
    return ones_where(row == target)


def group_mask():
    row = lax.broadcasted_iota(jnp.int32, (CH, WIN), 0)
    column = lax.broadcasted_iota(jnp.int32, (1, WIN), 1)
    offset = row - PG * quotient(column - CH * quotient(column, CH, 16), PG, 16)
    return (offset >= 0) & (offset < PG)


def order_matrix():
    row = lax.broadcasted_iota(jnp.int32, (3 * 256, 6 * LANES), 0)
    column = lax.broadcasted_iota(jnp.int32, (1, 6 * LANES), 1)
    channel = quotient(column, TAPS, 16)
    tap = column - TAPS * channel
    plane = quotient(tap, 9, 16)
    target = plane * 256 + (8 - tap + 9 * plane) * PG + channel
    return ones_where((row == target) & (column < PG * TAPS))


def expand(narrow, fold, mask):
    return jnp.where(mask, dot(narrow, fold), 0.0).astype(BF16)


def fill_weights(w1, fw, flip):
    row = lax.broadcasted_iota(jnp.int32, (3 * 256, PG * TAPS), 0)
    column = lax.broadcasted_iota(jnp.int32, (1, PG * TAPS), 1)
    channel = quotient(column, TAPS, 16)
    tap = column - TAPS * channel
    if flip:
        tap = TAPS - 1 - tap
    plane = quotient(tap, 9, 16)
    order = ones_where(row == plane * 256 + (tap - 9 * plane) * PG + channel)
    narrow = dot_nt(fw, order).astype(BF16)
    mask = group_mask()
    fold = fold_matrix(256)
    for a in range(3):
        w1[pl.ds(a * CH, CH), :] = expand(narrow[:, a * 256 : (a + 1) * 256], fold, mask)


def prepare_kernel(own_hbm, fw_ref, w1_hbm, again_hbm, w1, sems):
    copy = pltpu.make_async_copy(own_hbm, again_hbm, sems.at[0])
    copy.start()
    fill_weights(w1, fw_ref[...], False)
    send = pltpu.make_async_copy(w1, w1_hbm, sems.at[1])
    send.start()
    copy.wait()
    send.wait()


def cotangent_of(slab):
    return jnp.concatenate([slab[4, :, :LANES], slab[4, :, LANES:]], axis=0)


def main_kernel(
    inner_ref, core_ref, far_hbm, own_hbm, twin_hbm, w1_hbm, w2_hbm,
    mine_hbm, other_hbm, wn_hbm, g_hbm,
    beside, own_ref, w2_ref, mine_ref, other_ref, wn_ref, g_ref,
    xs, w1, pre_ref, xc_ref, gs, order_ref, fg, sems,
):
    inner = inner_ref[0]
    core = core_ref[0]
    low_ref, high_ref = beside.at[0], beside.at[1]
    fetches = [
        pltpu.make_async_copy(own_hbm, own_ref, sems.at[0]),
        pltpu.make_async_copy(far_hbm, beside.at[core], sems.at[1]),
        pltpu.make_async_copy(twin_hbm, beside.at[1 - core], sems.at[2]),
        pltpu.make_async_copy(w1_hbm, w1, sems.at[3]),
        pltpu.make_async_copy(w2_hbm, w2_ref, sems.at[4]),
    ]
    for fetch in fetches:
        fetch.start()
    split = split_matrix()
    mask = group_mask()
    fetches[0].wait()
    for e in (2, 3, 0, 1, 4, 5):
        slab = (low_ref, own_ref, high_ref)[e // 2]
        if e == 0:
            fetches[1].wait()
            fetches[2].wait()
        tiles = []
        for y in range(2):
            parts = dot(slab[2 * (e % 2) + y], split).astype(BF16)
            tiles.append([parts[:, q * LANES : (q + 1) * LANES] for q in range(4)])
            if 1 <= e <= 4:
                xc_ref[e - 1, :, pl.ds(y * 256, 256)] = parts[:, :256]
        fill_windows(xs.at[e], tiles)
    fetches[3].wait()
    for e in range(6):
        first, last = max(0, e - 3), min(2, e)
        terms = dot(w1[pl.ds(first * CH, (last - first + 1) * CH), :], xs[e])
        for a in range(first, last + 1):
            term = terms[(a - first) * CH : (a - first + 1) * CH]
            j = e - a
            if a == 0:
                pre_ref[j] = term
            else:
                pre_ref[j] += term
    zero = jnp.zeros((CH, LANES), BF16)
    for a in range(3):
        for c in range(3):
            wn_ref[pl.ds((9 * a + c) * CH, CH), :] = zero
        for y in range(2):
            value = pre_ref[a, :, pl.ds(y * 256, 256)]
            hidden = value * jax.nn.sigmoid(value)
            if a == 0:
                hidden = hidden * inner
            even, odd = hidden[:, :LANES], hidden[:, LANES:]
            base = (9 * a + 3 * (y + 1)) * CH
            wn_ref[pl.ds(base, CH), :] = later(odd).astype(BF16)
            wn_ref[pl.ds(base + CH, CH), :] = even.astype(BF16)
            wn_ref[pl.ds(base + 2 * CH, CH), :] = odd.astype(BF16)
    send_wn = pltpu.make_async_copy(wn_ref, wn_hbm, sems.at[0])
    send_wn.start()
    cot = cotangent_of(own_ref)
    rest = cot[LANES:]
    none = jnp.zeros_like(rest)
    both = jnp.concatenate(
        [jnp.concatenate([rest, none], axis=1), jnp.concatenate([none, rest], axis=1)], axis=0
    )
    fill = jnp.zeros((LEFT - RIGHT, LANES), BF16)
    for out_ref, half in ((other_ref, 1 - core), (mine_ref, core)):
        for k in range(3):
            base = pl.multiple_of(half * HALF + k * PART, 16)
            wide = dot_nt(wn_ref[pl.ds(base, PART), :], cot[:LANES])
            out_ref[pl.ds(k * CHUNK, PART), :] = wide.astype(BF16)
            left = wn_ref[pl.ds(base, LEFT), :]
            right = jnp.concatenate([wn_ref[pl.ds(base + LEFT, RIGHT), :], fill], axis=0)
            pairs = jnp.concatenate([left, right], axis=1)
            out_ref[pl.ds(k * CHUNK + PART, LEFT), :] = dot_nt(pairs, both).astype(BF16)
    with_above = jnp.concatenate([cot, cotangent_of(high_ref)], axis=1)
    with_below = jnp.concatenate([cot, cotangent_of(low_ref)], axis=1)
    order_ref[...] = order_matrix()
    fetches[4].wait()
    spread = [
        dot(w2_ref[pl.ds((9 * a + 3) * CH, 6 * CH), :], with_below if a == 2 else with_above)
        for a in range(3)
    ]
    for j in range(4):
        sources = {0: ((0, 0), (2, 1)), 1: ((1, 0),), 2: ((2, 0), (0, 1)), 3: ((1, 1),)}[j]
        tiles = []
        for y in range(2):
            got = []
            for c in range(3):
                total = None
                for a, part in sources:
                    tile = spread[a][
                        (3 * y + c) * CH : (3 * y + c + 1) * CH, part * LANES : (part + 1) * LANES
                    ]
                    total = tile if total is None else total + tile
                got.append(total)
            even = got[1]
            odd = got[2] + earlier(got[0])
            value = pre_ref[j, :, pl.ds(y * 256, 256)]
            sigma = jax.nn.sigmoid(value)
            slope = sigma * (1.0 + value * (1.0 - sigma))
            if j == 0:
                slope = slope * inner
            even = even * slope[:, :LANES]
            odd = odd * slope[:, LANES:]
            tiles.append([t.astype(BF16) for t in (even, odd, later(odd), earlier(even))])
            for q in range(4):
                g_ref[j, :, pl.ds((4 * y + q) * LANES, LANES)] = tiles[y][q]
        if j in (1, 2):
            fill_windows(gs.at[j - 1], tiles)
    send_g = pltpu.make_async_copy(g_ref, g_hbm, sems.at[1])
    send_g.start()
    taps = None
    for j in (1, 2):
        planes = jnp.concatenate([xc_ref[j - 1], xc_ref[j], xc_ref[j + 1]], axis=0)
        term = dot_nt(planes, gs[j - 1])
        taps = term if taps is None else taps + term
    fold = fold_matrix(256)
    kept = [jnp.where(mask, taps[a * CH : (a + 1) * CH], 0.0).astype(BF16) for a in range(3)]
    narrow = dot_nt(jnp.concatenate(kept, axis=0), fold).astype(BF16)
    ordered = dot(
        jnp.concatenate([narrow[a * CH : (a + 1) * CH] for a in range(3)], axis=1), order_ref[...]
    )
    fg[...] = ordered.astype(BF16)
    for out_ref, half in ((other_ref, 1 - core), (mine_ref, core)):
        base = pl.multiple_of(half * F_PART, 16)
        for k in range(6):
            at = (k // 2) * CHUNK + PART + LEFT + (k % 2) * F_PART
            out_ref[pl.ds(at, F_PART), :] = fg[pl.ds(base, F_PART), pl.ds(k * LANES, LANES)]
        out_ref[pl.ds(3 * CHUNK, ROWS - 3 * CHUNK), :] = jnp.zeros((ROWS - 3 * CHUNK, LANES), BF16)
    send_other = pltpu.make_async_copy(other_ref, other_hbm, sems.at[2])
    send_mine = pltpu.make_async_copy(mine_ref, mine_hbm, sems.at[3])
    send_other.start()
    send_mine.start()
    send_wn.wait()
    send_g.wait()
    send_other.wait()
    send_mine.wait()


def tail_kernel(
    after_hbm, g_hbm, wn_hbm, w2_hbm, fw_ref, feat_ref, vg_ref,
    g_ref, wn_ref, w2_ref, gs, w1, acc, sems,
):
    fetches = [
        pltpu.make_async_copy(source, target, sems.at[i])
        for i, (source, target) in enumerate(
            ((g_hbm, g_ref), (wn_hbm, wn_ref), (w2_hbm, w2_ref))
        )
    ]
    for fetch in fetches:
        fetch.start()
    fill_weights(w1, fw_ref[...], True)
    fetches[0].wait()
    for j in range(4):
        tiles = [
            [g_ref[j, :, pl.ds((4 * y + q) * LANES, LANES)] for q in range(4)] for y in range(2)
        ]
        fill_windows(gs.at[j], tiles)
    for j in range(4):
        first, last = max(0, j - 1), min(2, j)
        terms = dot(w1[pl.ds(first * CH, (last - first + 1) * CH), :], gs[j])
        for a in range(first, last + 1):
            term = terms[(a - first) * CH : (a - first + 1) * CH]
            out = j - a
            if a == 0:
                acc[out] = term
            else:
                acc[out] += term
    merge = merge_matrix()
    for out in range(2):
        for y in range(2):
            cut = pl.ds(y * 256, 256)
            vg_ref[out, :, cut] = dot(acc[out, :, cut].astype(BF16), merge).astype(BF16)
    fetches[1].wait()
    fetches[2].wait()
    feat_ref[...] = dot_tn(w2_ref[...], wn_ref[...]).astype(BF16)


def add_kernel(mine_hbm, got_hbm, out_hbm, mine_ref, got_ref, sems):
    fetches = [
        pltpu.make_async_copy(mine_hbm, mine_ref, sems.at[0]),
        pltpu.make_async_copy(got_hbm, got_ref, sems.at[1]),
    ]
    for fetch in fetches:
        fetch.start()
    for fetch in fetches:
        fetch.wait()
    got_ref[...] = (mine_ref[...].astype(F32) + got_ref[...].astype(F32)).astype(BF16)
    send = pltpu.make_async_copy(got_ref, out_hbm, sems.at[0])
    send.start()
    send.wait()


def finish_kernel(factor, half_ref, rows_hbm, *refs):
    strided_hbm, grouped_hbm, rows_ref, strided_ref, grouped_ref, fetch_sems, send_sems = refs[-7:]
    half = half_ref[0]
    fetches = [
        pltpu.make_async_copy(
            rows_hbm.at[pl.ds(k * CHUNK, CHUNK)], rows_ref.at[pl.ds(k * CHUNK, CHUNK)], fetch_sems.at[k]
        )
        for k in range(3)
    ]
    for fetch in fetches:
        fetch.start()
    sends = []
    for k in range(3):
        fetches[k].wait()
        at = k * CHUNK
        here = pl.ds(k * PART, PART)
        strided_ref[here, pl.ds(0, LANES)] = rows_ref[pl.ds(at, PART), :].astype(F32) * factor
        rest = rows_ref[pl.ds(at + PART, LEFT), :].astype(F32) * factor
        strided_ref[pl.ds(k * PART, LEFT), pl.ds(LANES, 64)] = rest[:, :64]
        strided_ref[pl.ds(k * PART + LEFT, RIGHT), pl.ds(LANES, 64)] = rest[:RIGHT, 64:]
        there = pl.ds(pl.multiple_of(half * HALF + k * PART, 8), PART)
        sends.append(
            pltpu.make_async_copy(strided_ref.at[here], strided_hbm.at[there], send_sems.at[k])
        )
        sends[-1].start()
        for i in range(2):
            tile = rows_ref[pl.ds(at + PART + LEFT + i * F_PART, F_PART), :]
            grouped_ref[:, pl.ds((2 * k + i) * LANES, LANES)] = tile.astype(F32) * factor
    there = pl.ds(pl.multiple_of(half * F_PART, 8), F_PART)
    sends.append(pltpu.make_async_copy(grouped_ref, grouped_hbm.at[there], send_sems.at[3]))
    sends[-1].start()
    for send in sends:
        send.wait()


VMEM = pl.BlockSpec(memory_space=pltpu.VMEM)
SMEM = pl.BlockSpec(memory_space=pltpu.SMEM)
ANY = pl.BlockSpec(memory_space=pl.ANY)
MIB = 1024 * 1024


def prepare_call(own, weight):
    return pl.pallas_call(
        prepare_kernel,
        out_shape=(
            jax.ShapeDtypeStruct((3 * CH, WIN), BF16),
            jax.ShapeDtypeStruct(own.shape, BF16),
        ),
        in_specs=[ANY, VMEM],
        out_specs=(ANY, ANY),
        scratch_shapes=[pltpu.VMEM((3 * CH, WIN), BF16), pltpu.SemaphoreType.DMA((2,))],
        compiler_params=pltpu.CompilerParams(vmem_limit_bytes=16 * MIB),
        name="prepare",
    )(own, weight)


def main_call(inner, core, far, own, twin, weight, w2):
    return pl.pallas_call(
        main_kernel,
        out_shape=(
            jax.ShapeDtypeStruct((ROWS, LANES), BF16),
            jax.ShapeDtypeStruct((ROWS, LANES), BF16),
            jax.ShapeDtypeStruct((TAPS * CH, LANES), BF16),
            jax.ShapeDtypeStruct((4, CH, 8 * LANES), BF16),
        ),
        in_specs=[SMEM, SMEM] + [ANY] * 5,
        out_specs=(ANY,) * 4,
        scratch_shapes=[
            pltpu.VMEM((2, 5, CH, 256), BF16),
            pltpu.VMEM((5, CH, 256), BF16),
            pltpu.VMEM((TAPS * CH, 192), BF16),
            pltpu.VMEM((ROWS, LANES), BF16),
            pltpu.VMEM((ROWS, LANES), BF16),
            pltpu.VMEM((TAPS * CH, LANES), BF16),
            pltpu.VMEM((4, CH, 8 * LANES), BF16),
            pltpu.VMEM((6, WIN, 512), BF16),
            pltpu.VMEM((3 * CH, WIN), BF16),
            pltpu.VMEM((4, CH, 512), F32),
            pltpu.VMEM((4, CH, 512), BF16),
            pltpu.VMEM((2, WIN, 512), BF16),
            pltpu.VMEM((768, 768), BF16),
            pltpu.VMEM((CH, 6 * LANES), BF16),
            pltpu.SemaphoreType.DMA((5,)),
        ],
        compiler_params=pltpu.CompilerParams(vmem_limit_bytes=40 * MIB),
        name="main",
    )(inner, core, far, own, twin, weight, w2)


def tail_call(after, grads, windows, w2, weight):
    return pl.pallas_call(
        tail_kernel,
        out_shape=(
            jax.ShapeDtypeStruct((192, LANES), BF16),
            jax.ShapeDtypeStruct((2, CH, 512), BF16),
        ),
        in_specs=[ANY, ANY, ANY, ANY, VMEM],
        out_specs=(VMEM,) * 2,
        scratch_shapes=[
            pltpu.VMEM((4, CH, 8 * LANES), BF16),
            pltpu.VMEM((TAPS * CH, LANES), BF16),
            pltpu.VMEM((TAPS * CH, 192), BF16),
            pltpu.VMEM((4, WIN, 512), BF16),
            pltpu.VMEM((3 * CH, WIN), BF16),
            pltpu.VMEM((2, CH, 512), F32),
            pltpu.SemaphoreType.DMA((3,)),
        ],
        compiler_params=pltpu.CompilerParams(vmem_limit_bytes=40 * MIB),
        cost_estimate=pl.CostEstimate(flops=10**9, bytes_accessed=4 * 10**6, transcendentals=0),
        name="tail",
    )(after, grads, windows, w2, weight)


def add_call(mine, got):
    return pl.pallas_call(
        add_kernel,
        out_shape=jax.ShapeDtypeStruct((ROWS, LANES), BF16),
        in_specs=[ANY, ANY],
        out_specs=ANY,
        scratch_shapes=[
            pltpu.VMEM((ROWS, LANES), BF16),
            pltpu.VMEM((ROWS, LANES), BF16),
            pltpu.SemaphoreType.DMA((2,)),
        ],
        compiler_params=pltpu.CompilerParams(vmem_limit_bytes=16 * MIB),
        name="add",
    )(mine, got)


def finish_call(factor, half, rows, before=()):
    return pl.pallas_call(
        functools.partial(finish_kernel, factor),
        out_shape=(
            jax.ShapeDtypeStruct((TAPS * CH, 192), F32),
            jax.ShapeDtypeStruct((CH, 6 * LANES), F32),
        ),
        in_specs=[SMEM, ANY] + [ANY] * len(before),
        out_specs=(ANY, ANY),
        scratch_shapes=[
            pltpu.VMEM((ROWS, LANES), BF16),
            pltpu.VMEM((HALF, 192), F32),
            pltpu.VMEM((F_PART, 6 * LANES), F32),
            pltpu.SemaphoreType.DMA((3,)),
            pltpu.SemaphoreType.DMA((4,)),
        ],
        input_output_aliases={2 + i: i for i in range(len(before))},
        compiler_params=pltpu.CompilerParams(vmem_limit_bytes=16 * MIB),
        name="finish",
    )(half, rows, *before)


def zero_kernel(after_hbm, out_ref):
    out_ref[0] = 0.0


def zero_call(after):
    return pl.pallas_call(
        zero_kernel,
        out_shape=jax.ShapeDtypeStruct((1,), F32),
        in_specs=[ANY],
        out_specs=SMEM,
        name="zero",
    )(after)


def sum_pieces(parts):
    return jnp.sum(parts.astype(F32), axis=0).astype(BF16)


def to_all(piece, axes, count):
    copies = jnp.broadcast_to(piece[None], (count,) + piece.shape)
    return lax.all_to_all(copies, axes, 0, 0, tiled=True)


def shards(volume, first_weight, second_weight, out_cotangent):
    count = lax.axis_size(SPACE)
    planes = volume[0].transpose(1, 2, 0, 3).reshape(4, CH, 256)
    cotangent = out_cotangent.reshape(2, CH, LANES).transpose(1, 0, 2).reshape(1, CH, 256)
    own = jnp.concatenate([planes, cotangent], axis=0)
    swap = [(0, 1), (1, 0)]
    far = lax.ppermute(
        own,
        SPACE,
        [(i, i + 1) for i in range(1, count - 1, 2)] + [(i, i - 1) for i in range(2, count, 2)],
    )
    core = lax.axis_index("core").astype(jnp.int32).reshape(1)
    inner = jnp.where(lax.axis_index(SPACE) > 0, 1.0, 0.0).astype(F32).reshape(1)
    forward_weight = first_weight.transpose(1, 3, 2, 0).reshape(CH, PG * TAPS)
    forward_weight, again = prepare_call(own, forward_weight)
    twin = lax.ppermute(again, "core", swap)
    backward_weight = first_weight.transpose(1, 2, 3, 0).reshape(CH, PG * TAPS)
    w2 = second_weight.reshape(TAPS * CH, 192)
    mine, other, windows, grads = main_call(inner, core, far, own, twin, forward_weight, w2)
    chip = add_call(mine, lax.ppermute(other, "core", swap))
    parts = lax.all_to_all(chip.reshape(PIECES, PIECE, LANES), NEAR, 0, 0, tiled=True)
    piece = sum_pieces(parts)
    feat, vgrad = tail_call(piece, grads, windows, w2, backward_weight)
    features = feat.reshape(out_cotangent.shape)
    volume_grad = vgrad.reshape(2, CH, 2, 256).transpose(1, 0, 2, 3)
    parts = to_all(piece, "zh", lax.axis_size("zh"))
    piece = lax.reduce(parts.astype(F32), zero_call(volume_grad)[0], lax.add, (0,)).astype(BF16)
    own_half = to_all(piece, NEAR, PIECES).reshape(ROWS, LANES)
    other_half = lax.ppermute(own_half, "core", swap)
    factor = 1.0 / math.sqrt(lax.axis_size(DP) * lax.axis_size(SPACE) * LANES)
    halves = finish_call(factor, core, own_half)
    second_grad, narrow = finish_call(factor, 1 - core, other_half, halves)
    first_grad = narrow[:, : TAPS * PG].reshape(4, PG, PG, TAPS).transpose(3, 0, 1, 2)
    return (features, volume_grad[None], first_grad, second_grad.reshape(second_weight.shape))


def solution(mesh):
    fine = Mesh(mesh.devices.reshape(2, 8, 2, 2, 4, 2), ("xh", "zh", "zl", "xl", "y", "core"))
    split = P(DP, None, SPACE, None, None)
    return jax.shard_map(
        shards,
        mesh=fine,
        in_specs=(split, P(), P(), split),
        out_specs=(split, split, P(), P()),
        check_vma=False,
    )
```

```python
import functools
import math

import jax
import jax.numpy as jnp
from jax import lax
from jax.experimental import pallas as pl
from jax.experimental.pallas import tpu as pltpu
from jax.sharding import Mesh
from jax.sharding import PartitionSpec as P

SPACE = ("xl", "y", "core")
DP = ("xh", "zh", "zl")
NEAR = ("xh", "xl", "y", "zl")
F32 = jnp.float32
BF16 = jnp.bfloat16

CH = 96
PG = 24
TAPS = 27
WIN = 9 * CH
LANES = 128
HALF = TAPS * CH // 2
PART = HALF // 3
LEFT, RIGHT = 224, PART - 224
F_PART = CH // 2
CHUNK = PART + LEFT + 2 * F_PART
PIECES = 32
PIECE = 72
ROWS = PIECES * PIECE


def dot(a, b):
    return lax.dot_general(a, b, (((1,), (0,)), ((), ())), preferred_element_type=F32)


def dot_nt(a, b):
    return lax.dot_general(a, b, (((1,), (1,)), ((), ())), preferred_element_type=F32)


def dot_tn(a, b):
    return lax.dot_general(a, b, (((0,), (0,)), ((), ())), preferred_element_type=F32)


def later(tile):
    lane = lax.broadcasted_iota(jnp.int32, tile.shape, 1)
    return jnp.where(lane == 0, 0.0, pltpu.roll(tile, 1, 1))


def earlier(tile):
    lane = lax.broadcasted_iota(jnp.int32, tile.shape, 1)
    return jnp.where(lane == LANES - 1, 0.0, pltpu.roll(tile, LANES - 1, 1))


def fill_windows(ref, tiles):
    zero = jnp.zeros((CH, LANES), BF16)
    for b in range(3):
        for c in range(3):
            rows = pl.ds((b * 3 + c) * CH, CH)
            for y in range(2):
                source = y + b - 1
                if source in (0, 1):
                    even, odd, odd_later, even_earlier = tiles[source]
                    pair = ((odd_later, even), (even, odd), (odd, even_earlier))[c]
                else:
                    pair = (zero, zero)
                for parity in range(2):
                    ref[rows, pl.ds((2 * y + parity) * LANES, LANES)] = pair[parity]


def ones_where(condition):
    return jnp.where(condition, 1.0, 0.0).astype(BF16)


def split_matrix():
    z = lax.broadcasted_iota(jnp.int32, (256, LANES), 0)
    k2 = 2 * lax.broadcasted_iota(jnp.int32, (256, LANES), 1)
    return jnp.concatenate([ones_where(z == k2 + off) for off in (0, 1, -1, 2)], axis=1)


def merge_matrix():
    lane = lax.broadcasted_iota(jnp.int32, (LANES, 256), 0)
    z = lax.broadcasted_iota(jnp.int32, (LANES, 256), 1)
    return jnp.concatenate([ones_where(z == 2 * lane + bit) for bit in (0, 1)], axis=0)


def quotient(value, divisor, bits):
    return (value * (2**bits // divisor + 1)) >> bits


def fold_matrix(rows):
    row = lax.broadcasted_iota(jnp.int32, (rows, WIN), 0)
    column = lax.broadcasted_iota(jnp.int32, (1, WIN), 1)
    target = quotient(column, CH, 16) * PG + column - PG * quotient(column, PG, 16)
    return ones_where(row == target)


def group_mask():
    row = lax.broadcasted_iota(jnp.int32, (CH, WIN), 0)
    column = lax.broadcasted_iota(jnp.int32, (1, WIN), 1)
    offset = row - PG * quotient(column - CH * quotient(column, CH, 16), PG, 16)
    return (offset >= 0) & (offset < PG)


def order_matrix():
    row = lax.broadcasted_iota(jnp.int32, (3 * 256, 6 * LANES), 0)
    column = lax.broadcasted_iota(jnp.int32, (1, 6 * LANES), 1)
    channel = quotient(column, TAPS, 16)
    tap = column - TAPS * channel
    plane = quotient(tap, 9, 16)
    target = plane * 256 + (8 - tap + 9 * plane) * PG + channel
    return ones_where((row == target) & (column < PG * TAPS))


def expand(narrow, fold, mask):
    return jnp.where(mask, dot(narrow, fold), 0.0).astype(BF16)


def fill_weights(w1, fw, flip):
    row = lax.broadcasted_iota(jnp.int32, (3 * 256, PG * TAPS), 0)
    column = lax.broadcasted_iota(jnp.int32, (1, PG * TAPS), 1)
    channel = quotient(column, TAPS, 16)
    tap = column - TAPS * channel
    if flip:
        tap = TAPS - 1 - tap
    plane = quotient(tap, 9, 16)
    order = ones_where(row == plane * 256 + (tap - 9 * plane) * PG + channel)
    narrow = dot_nt(fw, order).astype(BF16)
    mask = group_mask()
    fold = fold_matrix(256)
    for a in range(3):
        w1[pl.ds(a * CH, CH), :] = expand(narrow[:, a * 256 : (a + 1) * 256], fold, mask)


def again_kernel(own_hbm, after_hbm, again_hbm, sem):
    copy = pltpu.make_async_copy(own_hbm, again_hbm, sem)
    copy.start()
    copy.wait()


def prepare_kernel(fw_ref, w1_hbm, w1, sem):
    fill_weights(w1, fw_ref[...], False)
    send = pltpu.make_async_copy(w1, w1_hbm, sem)
    send.start()
    send.wait()


def cotangent_of(slab):
    return jnp.concatenate([slab[4, :, :LANES], slab[4, :, LANES:]], axis=0)


def main_kernel(
    inner_ref, core_ref, far_hbm, own_hbm, twin_hbm, w1_hbm, w2_hbm,
    mine_hbm, other_hbm, wn_hbm, g_hbm,
    beside, own_ref, w2_ref, mine_ref, other_ref, wn_ref, g_ref,
    xs, w1, pre_ref, xc_ref, gs, order_ref, fg, sems,
):
    inner = inner_ref[0]
    core = core_ref[0]
    low_ref, high_ref = beside.at[0], beside.at[1]
    fetches = [
        pltpu.make_async_copy(own_hbm, own_ref, sems.at[0]),
        pltpu.make_async_copy(far_hbm, beside.at[core], sems.at[1]),
        pltpu.make_async_copy(twin_hbm, beside.at[1 - core], sems.at[2]),
        pltpu.make_async_copy(w1_hbm, w1, sems.at[3]),
        pltpu.make_async_copy(w2_hbm, w2_ref, sems.at[4]),
    ]
    for fetch in fetches:
        fetch.start()
    split = split_matrix()
    mask = group_mask()
    fetches[0].wait()
    for e in (2, 3, 0, 1, 4, 5):
        slab = (low_ref, own_ref, high_ref)[e // 2]
        if e == 0:
            fetches[1].wait()
            fetches[2].wait()
        tiles = []
        for y in range(2):
            parts = dot(slab[2 * (e % 2) + y], split).astype(BF16)
            tiles.append([parts[:, q * LANES : (q + 1) * LANES] for q in range(4)])
            if 1 <= e <= 4:
                xc_ref[e - 1, :, pl.ds(y * 256, 256)] = parts[:, :256]
        fill_windows(xs.at[e], tiles)
    fetches[3].wait()
    for e in range(6):
        first, last = max(0, e - 3), min(2, e)
        terms = dot(w1[pl.ds(first * CH, (last - first + 1) * CH), :], xs[e])
        for a in range(first, last + 1):
            term = terms[(a - first) * CH : (a - first + 1) * CH]
            j = e - a
            if a == 0:
                pre_ref[j] = term
            else:
                pre_ref[j] += term
    zero = jnp.zeros((CH, LANES), BF16)
    for a in range(3):
        for c in range(3):
            wn_ref[pl.ds((9 * a + c) * CH, CH), :] = zero
        for y in range(2):
            value = pre_ref[a, :, pl.ds(y * 256, 256)]
            hidden = value * jax.nn.sigmoid(value)
            if a == 0:
                hidden = hidden * inner
            even, odd = hidden[:, :LANES], hidden[:, LANES:]
            base = (9 * a + 3 * (y + 1)) * CH
            wn_ref[pl.ds(base, CH), :] = later(odd).astype(BF16)
            wn_ref[pl.ds(base + CH, CH), :] = even.astype(BF16)
            wn_ref[pl.ds(base + 2 * CH, CH), :] = odd.astype(BF16)
    send_wn = pltpu.make_async_copy(wn_ref, wn_hbm, sems.at[0])
    send_wn.start()
    cot = cotangent_of(own_ref)
    rest = cot[LANES:]
    none = jnp.zeros_like(rest)
    both = jnp.concatenate(
        [jnp.concatenate([rest, none], axis=1), jnp.concatenate([none, rest], axis=1)], axis=0
    )
    fill = jnp.zeros((LEFT - RIGHT, LANES), BF16)
    for out_ref, half in ((other_ref, 1 - core), (mine_ref, core)):
        for k in range(3):
            base = pl.multiple_of(half * HALF + k * PART, 16)
            wide = dot_nt(wn_ref[pl.ds(base, PART), :], cot[:LANES])
            out_ref[pl.ds(k * CHUNK, PART), :] = wide.astype(BF16)
            left = wn_ref[pl.ds(base, LEFT), :]
            right = jnp.concatenate([wn_ref[pl.ds(base + LEFT, RIGHT), :], fill], axis=0)
            pairs = jnp.concatenate([left, right], axis=1)
            out_ref[pl.ds(k * CHUNK + PART, LEFT), :] = dot_nt(pairs, both).astype(BF16)
    with_above = jnp.concatenate([cot, cotangent_of(high_ref)], axis=1)
    with_below = jnp.concatenate([cot, cotangent_of(low_ref)], axis=1)
    order_ref[...] = order_matrix()
    fetches[4].wait()
    spread = [
        dot(w2_ref[pl.ds((9 * a + 3) * CH, 6 * CH), :], with_below if a == 2 else with_above)
        for a in range(3)
    ]
    for j in range(4):
        sources = {0: ((0, 0), (2, 1)), 1: ((1, 0),), 2: ((2, 0), (0, 1)), 3: ((1, 1),)}[j]
        tiles = []
        for y in range(2):
            got = []
            for c in range(3):
                total = None
                for a, part in sources:
                    tile = spread[a][
                        (3 * y + c) * CH : (3 * y + c + 1) * CH, part * LANES : (part + 1) * LANES
                    ]
                    total = tile if total is None else total + tile
                got.append(total)
            even = got[1]
            odd = got[2] + earlier(got[0])
            value = pre_ref[j, :, pl.ds(y * 256, 256)]
            sigma = jax.nn.sigmoid(value)
            slope = sigma * (1.0 + value * (1.0 - sigma))
            if j == 0:
                slope = slope * inner
            even = even * slope[:, :LANES]
            odd = odd * slope[:, LANES:]
            tiles.append([t.astype(BF16) for t in (even, odd, later(odd), earlier(even))])
            for q in range(4):
                g_ref[j, :, pl.ds((4 * y + q) * LANES, LANES)] = tiles[y][q]
        if j in (1, 2):
            fill_windows(gs.at[j - 1], tiles)
    send_g = pltpu.make_async_copy(g_ref, g_hbm, sems.at[1])
    send_g.start()
    taps = None
    for j in (1, 2):
        planes = jnp.concatenate([xc_ref[j - 1], xc_ref[j], xc_ref[j + 1]], axis=0)
        term = dot_nt(planes, gs[j - 1])
        taps = term if taps is None else taps + term
    fold = fold_matrix(256)
    kept = [jnp.where(mask, taps[a * CH : (a + 1) * CH], 0.0).astype(BF16) for a in range(3)]
    narrow = dot_nt(jnp.concatenate(kept, axis=0), fold).astype(BF16)
    ordered = dot(
        jnp.concatenate([narrow[a * CH : (a + 1) * CH] for a in range(3)], axis=1), order_ref[...]
    )
    fg[...] = ordered.astype(BF16)
    for out_ref, half in ((other_ref, 1 - core), (mine_ref, core)):
        base = pl.multiple_of(half * F_PART, 16)
        for k in range(6):
            at = (k // 2) * CHUNK + PART + LEFT + (k % 2) * F_PART
            out_ref[pl.ds(at, F_PART), :] = fg[pl.ds(base, F_PART), pl.ds(k * LANES, LANES)]
        out_ref[pl.ds(3 * CHUNK, ROWS - 3 * CHUNK), :] = jnp.zeros((ROWS - 3 * CHUNK, LANES), BF16)
    send_other = pltpu.make_async_copy(other_ref, other_hbm, sems.at[2])
    send_mine = pltpu.make_async_copy(mine_ref, mine_hbm, sems.at[3])
    send_other.start()
    send_mine.start()
    send_wn.wait()
    send_g.wait()
    send_other.wait()
    send_mine.wait()


def tail_kernel(
    after_hbm, g_hbm, wn_hbm, w2_hbm, fw_ref, feat_ref, vg_ref,
    g_ref, wn_ref, w2_ref, gs, w1, acc, sems,
):
    fetches = [
        pltpu.make_async_copy(source, target, sems.at[i])
        for i, (source, target) in enumerate(
            ((g_hbm, g_ref), (wn_hbm, wn_ref), (w2_hbm, w2_ref))
        )
    ]
    for fetch in fetches:
        fetch.start()
    fill_weights(w1, fw_ref[...], True)
    fetches[0].wait()
    for j in range(4):
        tiles = [
            [g_ref[j, :, pl.ds((4 * y + q) * LANES, LANES)] for q in range(4)] for y in range(2)
        ]
        fill_windows(gs.at[j], tiles)
    for j in range(4):
        first, last = max(0, j - 1), min(2, j)
        terms = dot(w1[pl.ds(first * CH, (last - first + 1) * CH), :], gs[j])
        for a in range(first, last + 1):
            term = terms[(a - first) * CH : (a - first + 1) * CH]
            out = j - a
            if a == 0:
                acc[out] = term
            else:
                acc[out] += term
    merge = merge_matrix()
    for out in range(2):
        for y in range(2):
            cut = pl.ds(y * 256, 256)
            vg_ref[out, :, cut] = dot(acc[out, :, cut].astype(BF16), merge).astype(BF16)
    fetches[1].wait()
    fetches[2].wait()
    feat_ref[...] = dot_tn(w2_ref[...], wn_ref[...]).astype(BF16)


def add_kernel(mine_hbm, got_hbm, out_hbm, mine_ref, got_ref, sems):
    fetches = [
        pltpu.make_async_copy(mine_hbm, mine_ref, sems.at[0]),
        pltpu.make_async_copy(got_hbm, got_ref, sems.at[1]),
    ]
    for fetch in fetches:
        fetch.start()
    for fetch in fetches:
        fetch.wait()
    got_ref[...] = (mine_ref[...].astype(F32) + got_ref[...].astype(F32)).astype(BF16)
    send = pltpu.make_async_copy(got_ref, out_hbm, sems.at[0])
    send.start()
    send.wait()


def finish_kernel(factor, half_ref, rows_hbm, *refs):
    strided_hbm, grouped_hbm, rows_ref, strided_ref, grouped_ref, fetch_sems, send_sems = refs[-7:]
    half = half_ref[0]
    fetches = [
        pltpu.make_async_copy(
            rows_hbm.at[pl.ds(k * CHUNK, CHUNK)], rows_ref.at[pl.ds(k * CHUNK, CHUNK)], fetch_sems.at[k]
        )
        for k in range(3)
    ]
    for fetch in fetches:
        fetch.start()
    sends = []
    for k in range(3):
        fetches[k].wait()
        at = k * CHUNK
        here = pl.ds(k * PART, PART)
        strided_ref[here, pl.ds(0, LANES)] = rows_ref[pl.ds(at, PART), :].astype(F32) * factor
        rest = rows_ref[pl.ds(at + PART, LEFT), :].astype(F32) * factor
        strided_ref[pl.ds(k * PART, LEFT), pl.ds(LANES, 64)] = rest[:, :64]
        strided_ref[pl.ds(k * PART + LEFT, RIGHT), pl.ds(LANES, 64)] = rest[:RIGHT, 64:]
        there = pl.ds(pl.multiple_of(half * HALF + k * PART, 8), PART)
        sends.append(
            pltpu.make_async_copy(strided_ref.at[here], strided_hbm.at[there], send_sems.at[k])
        )
        sends[-1].start()
        for i in range(2):
            tile = rows_ref[pl.ds(at + PART + LEFT + i * F_PART, F_PART), :]
            grouped_ref[:, pl.ds((2 * k + i) * LANES, LANES)] = tile.astype(F32) * factor
    there = pl.ds(pl.multiple_of(half * F_PART, 8), F_PART)
    sends.append(pltpu.make_async_copy(grouped_ref, grouped_hbm.at[there], send_sems.at[3]))
    sends[-1].start()
    for send in sends:
        send.wait()


VMEM = pl.BlockSpec(memory_space=pltpu.VMEM)
SMEM = pl.BlockSpec(memory_space=pltpu.SMEM)
ANY = pl.BlockSpec(memory_space=pl.ANY)
MIB = 1024 * 1024


def again_call(own, after):
    return pl.pallas_call(
        again_kernel,
        out_shape=jax.ShapeDtypeStruct(own.shape, BF16),
        in_specs=[ANY, ANY],
        out_specs=ANY,
        scratch_shapes=[pltpu.SemaphoreType.DMA],
        compiler_params=pltpu.CompilerParams(vmem_limit_bytes=MIB),
        name="again",
    )(own, after)


def prepare_call(weight):
    return pl.pallas_call(
        prepare_kernel,
        out_shape=jax.ShapeDtypeStruct((3 * CH, WIN), BF16),
        in_specs=[VMEM],
        out_specs=ANY,
        scratch_shapes=[pltpu.VMEM((3 * CH, WIN), BF16), pltpu.SemaphoreType.DMA],
        compiler_params=pltpu.CompilerParams(vmem_limit_bytes=6 * MIB),
        name="prepare",
    )(weight)


def main_call(inner, core, far, own, twin, weight, w2):
    return pl.pallas_call(
        main_kernel,
        out_shape=(
            jax.ShapeDtypeStruct((ROWS, LANES), BF16),
            jax.ShapeDtypeStruct((ROWS, LANES), BF16),
            jax.ShapeDtypeStruct((TAPS * CH, LANES), BF16),
            jax.ShapeDtypeStruct((4, CH, 8 * LANES), BF16),
        ),
        in_specs=[SMEM, SMEM] + [ANY] * 5,
        out_specs=(ANY,) * 4,
        scratch_shapes=[
            pltpu.VMEM((2, 5, CH, 256), BF16),
            pltpu.VMEM((5, CH, 256), BF16),
            pltpu.VMEM((TAPS * CH, 192), BF16),
            pltpu.VMEM((ROWS, LANES), BF16),
            pltpu.VMEM((ROWS, LANES), BF16),
            pltpu.VMEM((TAPS * CH, LANES), BF16),
            pltpu.VMEM((4, CH, 8 * LANES), BF16),
            pltpu.VMEM((6, WIN, 512), BF16),
            pltpu.VMEM((3 * CH, WIN), BF16),
            pltpu.VMEM((4, CH, 512), F32),
            pltpu.VMEM((4, CH, 512), BF16),
            pltpu.VMEM((2, WIN, 512), BF16),
            pltpu.VMEM((768, 768), BF16),
            pltpu.VMEM((CH, 6 * LANES), BF16),
            pltpu.SemaphoreType.DMA((5,)),
        ],
        compiler_params=pltpu.CompilerParams(vmem_limit_bytes=24 * MIB),
        name="main",
    )(inner, core, far, own, twin, weight, w2)


def tail_call(after, grads, windows, w2, weight):
    return pl.pallas_call(
        tail_kernel,
        out_shape=(
            jax.ShapeDtypeStruct((192, LANES), BF16),
            jax.ShapeDtypeStruct((2, CH, 512), BF16),
        ),
        in_specs=[ANY, ANY, ANY, ANY, VMEM],
        out_specs=(VMEM,) * 2,
        scratch_shapes=[
            pltpu.VMEM((4, CH, 8 * LANES), BF16),
            pltpu.VMEM((TAPS * CH, LANES), BF16),
            pltpu.VMEM((TAPS * CH, 192), BF16),
            pltpu.VMEM((4, WIN, 512), BF16),
            pltpu.VMEM((3 * CH, WIN), BF16),
            pltpu.VMEM((2, CH, 512), F32),
            pltpu.SemaphoreType.DMA((3,)),
        ],
        compiler_params=pltpu.CompilerParams(vmem_limit_bytes=12 * MIB),
        cost_estimate=pl.CostEstimate(flops=10**9, bytes_accessed=4 * 10**6, transcendentals=0),
        name="tail",
    )(after, grads, windows, w2, weight)


def add_call(mine, got):
    return pl.pallas_call(
        add_kernel,
        out_shape=jax.ShapeDtypeStruct((ROWS, LANES), BF16),
        in_specs=[ANY, ANY],
        out_specs=ANY,
        scratch_shapes=[
            pltpu.VMEM((ROWS, LANES), BF16),
            pltpu.VMEM((ROWS, LANES), BF16),
            pltpu.SemaphoreType.DMA((2,)),
        ],
        compiler_params=pltpu.CompilerParams(vmem_limit_bytes=4 * MIB),
        name="add",
    )(mine, got)


def finish_call(factor, half, rows, before=()):
    return pl.pallas_call(
        functools.partial(finish_kernel, factor),
        out_shape=(
            jax.ShapeDtypeStruct((TAPS * CH, 192), F32),
            jax.ShapeDtypeStruct((CH, 6 * LANES), F32),
        ),
        in_specs=[SMEM, ANY] + [ANY] * len(before),
        out_specs=(ANY, ANY),
        scratch_shapes=[
            pltpu.VMEM((ROWS, LANES), BF16),
            pltpu.VMEM((HALF, 192), F32),
            pltpu.VMEM((F_PART, 6 * LANES), F32),
            pltpu.SemaphoreType.DMA((3,)),
            pltpu.SemaphoreType.DMA((4,)),
        ],
        input_output_aliases={2 + i: i for i in range(len(before))},
        compiler_params=pltpu.CompilerParams(vmem_limit_bytes=6 * MIB),
        name="finish",
    )(half, rows, *before)


def zero_kernel(after_hbm, out_ref):
    out_ref[0] = 0.0


def zero_call(after):
    return pl.pallas_call(
        zero_kernel,
        out_shape=jax.ShapeDtypeStruct((1,), F32),
        in_specs=[ANY],
        out_specs=SMEM,
        compiler_params=pltpu.CompilerParams(vmem_limit_bytes=MIB),
        name="zero",
    )(after)


def sum_pieces(parts):
    return jnp.sum(parts.astype(F32), axis=0).astype(BF16)


def to_all(piece, axes, count):
    copies = jnp.broadcast_to(piece[None], (count,) + piece.shape)
    return lax.all_to_all(copies, axes, 0, 0, tiled=True)


def shards(volume, first_weight, second_weight, out_cotangent):
    count = lax.axis_size(SPACE)
    planes = volume[0].transpose(1, 2, 0, 3).reshape(4, CH, 256)
    cotangent = out_cotangent.reshape(2, CH, LANES).transpose(1, 0, 2).reshape(1, CH, 256)
    own = jnp.concatenate([planes, cotangent], axis=0)
    swap = [(0, 1), (1, 0)]
    far = lax.ppermute(
        own,
        SPACE,
        [(i, i + 1) for i in range(1, count - 1, 2)] + [(i, i - 1) for i in range(2, count, 2)],
    )
    core = lax.axis_index("core").astype(jnp.int32).reshape(1)
    inner = jnp.where(lax.axis_index(SPACE) > 0, 1.0, 0.0).astype(F32).reshape(1)
    forward_weight = first_weight.transpose(1, 3, 2, 0).reshape(CH, PG * TAPS)
    twin = lax.ppermute(again_call(own, forward_weight), "core", swap)
    forward_weight = prepare_call(forward_weight)
    backward_weight = first_weight.transpose(1, 2, 3, 0).reshape(CH, PG * TAPS)
    w2 = second_weight.reshape(TAPS * CH, 192)
    mine, other, windows, grads = main_call(inner, core, far, own, twin, forward_weight, w2)
    chip = add_call(mine, lax.ppermute(other, "core", swap))
    parts = lax.all_to_all(chip.reshape(PIECES, PIECE, LANES), NEAR, 0, 0, tiled=True)
    feat, vgrad = tail_call(chip, grads, windows, w2, backward_weight)
    features = feat.reshape(out_cotangent.shape)
    volume_grad = vgrad.reshape(2, CH, 2, 256).transpose(1, 0, 2, 3)
    piece = lax.reduce(parts.astype(F32), zero_call(volume_grad)[0], lax.add, (0,)).astype(BF16)
    piece = sum_pieces(to_all(piece, "zh", lax.axis_size("zh")))
    own_half = to_all(piece, NEAR, PIECES).reshape(ROWS, LANES)
    other_half = lax.ppermute(own_half, "core", swap)
    factor = 1.0 / math.sqrt(lax.axis_size(DP) * lax.axis_size(SPACE) * LANES)
    halves = finish_call(factor, core, own_half)
    second_grad, narrow = finish_call(factor, 1 - core, other_half, halves)
    first_grad = narrow[:, : TAPS * PG].reshape(4, PG, PG, TAPS).transpose(3, 0, 1, 2)
    return (features, volume_grad[None], first_grad, second_grad.reshape(second_weight.shape))


def solution(mesh):
    fine = Mesh(mesh.devices.reshape(2, 8, 2, 2, 4, 2), ("xh", "zh", "zl", "xl", "y", "core"))
    split = P(DP, None, SPACE, None, None)
    return jax.shard_map(
        shards,
        mesh=fine,
        in_specs=(split, P(), P(), split),
        out_specs=(split, split, P(), P()),
        check_vma=False,
    )
```

```python
import functools
import math

import jax
import jax.numpy as jnp
from jax import lax
from jax.experimental import pallas as pl
from jax.experimental.pallas import tpu as pltpu
from jax.sharding import Mesh
from jax.sharding import PartitionSpec as P

SPACE = ("xl", "y", "core")
DP = ("xh", "zh", "zl")
NEAR = ("xh", "xl", "y", "zl")
F32 = jnp.float32
BF16 = jnp.bfloat16

CH = 96
PG = 24
TAPS = 27
WIN = 9 * CH
LANES = 128
HALF = TAPS * CH // 2
PART = HALF // 3
LEFT, RIGHT = 224, PART - 224
F_PART = CH // 2
CHUNK = PART + LEFT + 2 * F_PART
PIECES = 32
PIECE = 72
ROWS = PIECES * PIECE


def dot(a, b):
    return lax.dot_general(a, b, (((1,), (0,)), ((), ())), preferred_element_type=F32)


def dot_nt(a, b):
    return lax.dot_general(a, b, (((1,), (1,)), ((), ())), preferred_element_type=F32)


def dot_tn(a, b):
    return lax.dot_general(a, b, (((0,), (0,)), ((), ())), preferred_element_type=F32)


def later(tile):
    lane = lax.broadcasted_iota(jnp.int32, tile.shape, 1)
    return jnp.where(lane == 0, 0.0, pltpu.roll(tile, 1, 1))


def earlier(tile):
    lane = lax.broadcasted_iota(jnp.int32, tile.shape, 1)
    return jnp.where(lane == LANES - 1, 0.0, pltpu.roll(tile, LANES - 1, 1))


def fill_windows(ref, tiles):
    zero = jnp.zeros((CH, LANES), BF16)
    for b in range(3):
        for c in range(3):
            rows = pl.ds((b * 3 + c) * CH, CH)
            for y in range(2):
                source = y + b - 1
                if source in (0, 1):
                    even, odd, odd_later, even_earlier = tiles[source]
                    pair = ((odd_later, even), (even, odd), (odd, even_earlier))[c]
                else:
                    pair = (zero, zero)
                for parity in range(2):
                    ref[rows, pl.ds((2 * y + parity) * LANES, LANES)] = pair[parity]


def ones_where(condition):
    return jnp.where(condition, 1.0, 0.0).astype(BF16)


def split_matrix():
    z = lax.broadcasted_iota(jnp.int32, (256, LANES), 0)
    k2 = 2 * lax.broadcasted_iota(jnp.int32, (256, LANES), 1)
    return jnp.concatenate([ones_where(z == k2 + off) for off in (0, 1, -1, 2)], axis=1)


def merge_matrix():
    lane = lax.broadcasted_iota(jnp.int32, (LANES, 256), 0)
    z = lax.broadcasted_iota(jnp.int32, (LANES, 256), 1)
    return jnp.concatenate([ones_where(z == 2 * lane + bit) for bit in (0, 1)], axis=0)


def quotient(value, divisor, bits):
    return (value * (2**bits // divisor + 1)) >> bits


def fold_matrix(rows):
    row = lax.broadcasted_iota(jnp.int32, (rows, WIN), 0)
    column = lax.broadcasted_iota(jnp.int32, (1, WIN), 1)
    target = quotient(column, CH, 16) * PG + column - PG * quotient(column, PG, 16)
    return ones_where(row == target)


def group_mask():
    row = lax.broadcasted_iota(jnp.int32, (CH, WIN), 0)
    column = lax.broadcasted_iota(jnp.int32, (1, WIN), 1)
    offset = row - PG * quotient(column - CH * quotient(column, CH, 16), PG, 16)
    return (offset >= 0) & (offset < PG)


def order_matrix():
    row = lax.broadcasted_iota(jnp.int32, (3 * 256, 6 * LANES), 0)
    column = lax.broadcasted_iota(jnp.int32, (1, 6 * LANES), 1)
    channel = quotient(column, TAPS, 16)
    tap = column - TAPS * channel
    plane = quotient(tap, 9, 16)
    target = plane * 256 + (8 - tap + 9 * plane) * PG + channel
    return ones_where((row == target) & (column < PG * TAPS))


def expand(narrow, fold, mask):
    return jnp.where(mask, dot(narrow, fold), 0.0).astype(BF16)


def fill_weights(w1, fw, flip):
    row = lax.broadcasted_iota(jnp.int32, (3 * 256, PG * TAPS), 0)
    column = lax.broadcasted_iota(jnp.int32, (1, PG * TAPS), 1)
    channel = quotient(column, TAPS, 16)
    tap = column - TAPS * channel
    if flip:
        tap = TAPS - 1 - tap
    plane = quotient(tap, 9, 16)
    order = ones_where(row == plane * 256 + (tap - 9 * plane) * PG + channel)
    narrow = dot_nt(fw, order).astype(BF16)
    mask = group_mask()
    fold = fold_matrix(256)
    for a in range(3):
        w1[pl.ds(a * CH, CH), :] = expand(narrow[:, a * 256 : (a + 1) * 256], fold, mask)


def again_kernel(own_hbm, after_hbm, again_hbm, sem):
    copy = pltpu.make_async_copy(own_hbm, again_hbm, sem)
    copy.start()
    copy.wait()


def cotangent_of(slab):
    return jnp.concatenate([slab[4, :, :LANES], slab[4, :, LANES:]], axis=0)


def main_kernel(
    inner_ref, core_ref, far_hbm, own_hbm, twin_hbm, fw_hbm, w2_hbm,
    mine_hbm, other_hbm, wn_hbm, g_hbm,
    beside, own_ref, fw_ref, w2_ref, mine_ref, other_ref, wn_ref, g_ref,
    xs, w1, pre_ref, xc_ref, gs, order_ref, fg, sems,
):
    inner = inner_ref[0]
    core = core_ref[0]
    low_ref, high_ref = beside.at[0], beside.at[1]
    fetches = [
        pltpu.make_async_copy(fw_hbm, fw_ref, sems.at[3]),
        pltpu.make_async_copy(own_hbm, own_ref, sems.at[0]),
        pltpu.make_async_copy(far_hbm, beside.at[core], sems.at[1]),
        pltpu.make_async_copy(twin_hbm, beside.at[1 - core], sems.at[2]),
        pltpu.make_async_copy(w2_hbm, w2_ref, sems.at[4]),
    ]
    for fetch in fetches:
        fetch.start()
    split = split_matrix()
    mask = group_mask()
    fetches[0].wait()
    fill_weights(w1, fw_ref[...], False)
    fetches[1].wait()
    for e in (2, 3, 0, 1, 4, 5):
        slab = (low_ref, own_ref, high_ref)[e // 2]
        if e == 0:
            fetches[2].wait()
            fetches[3].wait()
        tiles = []
        for y in range(2):
            parts = dot(slab[2 * (e % 2) + y], split).astype(BF16)
            tiles.append([parts[:, q * LANES : (q + 1) * LANES] for q in range(4)])
            if 1 <= e <= 4:
                xc_ref[e - 1, :, pl.ds(y * 256, 256)] = parts[:, :256]
        fill_windows(xs.at[e], tiles)
    for e in range(6):
        first, last = max(0, e - 3), min(2, e)
        terms = dot(w1[pl.ds(first * CH, (last - first + 1) * CH), :], xs[e])
        for a in range(first, last + 1):
            term = terms[(a - first) * CH : (a - first + 1) * CH]
            j = e - a
            if a == 0:
                pre_ref[j] = term
            else:
                pre_ref[j] += term
    zero = jnp.zeros((CH, LANES), BF16)
    for a in range(3):
        for c in range(3):
            wn_ref[pl.ds((9 * a + c) * CH, CH), :] = zero
        for y in range(2):
            value = pre_ref[a, :, pl.ds(y * 256, 256)]
            hidden = value * jax.nn.sigmoid(value)
            if a == 0:
                hidden = hidden * inner
            even, odd = hidden[:, :LANES], hidden[:, LANES:]
            base = (9 * a + 3 * (y + 1)) * CH
            wn_ref[pl.ds(base, CH), :] = later(odd).astype(BF16)
            wn_ref[pl.ds(base + CH, CH), :] = even.astype(BF16)
            wn_ref[pl.ds(base + 2 * CH, CH), :] = odd.astype(BF16)
    send_wn = pltpu.make_async_copy(wn_ref, wn_hbm, sems.at[0])
    send_wn.start()
    cot = cotangent_of(own_ref)
    rest = cot[LANES:]
    none = jnp.zeros_like(rest)
    both = jnp.concatenate(
        [jnp.concatenate([rest, none], axis=1), jnp.concatenate([none, rest], axis=1)], axis=0
    )
    fill = jnp.zeros((LEFT - RIGHT, LANES), BF16)
    for out_ref, half in ((other_ref, 1 - core), (mine_ref, core)):
        for k in range(3):
            base = pl.multiple_of(half * HALF + k * PART, 16)
            wide = dot_nt(wn_ref[pl.ds(base, PART), :], cot[:LANES])
            out_ref[pl.ds(k * CHUNK, PART), :] = wide.astype(BF16)
            left = wn_ref[pl.ds(base, LEFT), :]
            right = jnp.concatenate([wn_ref[pl.ds(base + LEFT, RIGHT), :], fill], axis=0)
            pairs = jnp.concatenate([left, right], axis=1)
            out_ref[pl.ds(k * CHUNK + PART, LEFT), :] = dot_nt(pairs, both).astype(BF16)
    with_above = jnp.concatenate([cot, cotangent_of(high_ref)], axis=1)
    with_below = jnp.concatenate([cot, cotangent_of(low_ref)], axis=1)
    order_ref[...] = order_matrix()
    fetches[4].wait()
    spread = [
        dot(w2_ref[pl.ds((9 * a + 3) * CH, 6 * CH), :], with_below if a == 2 else with_above)
        for a in range(3)
    ]
    for j in range(4):
        sources = {0: ((0, 0), (2, 1)), 1: ((1, 0),), 2: ((2, 0), (0, 1)), 3: ((1, 1),)}[j]
        tiles = []
        for y in range(2):
            got = []
            for c in range(3):
                total = None
                for a, part in sources:
                    tile = spread[a][
                        (3 * y + c) * CH : (3 * y + c + 1) * CH, part * LANES : (part + 1) * LANES
                    ]
                    total = tile if total is None else total + tile
                got.append(total)
            even = got[1]
            odd = got[2] + earlier(got[0])
            value = pre_ref[j, :, pl.ds(y * 256, 256)]
            sigma = jax.nn.sigmoid(value)
            slope = sigma * (1.0 + value * (1.0 - sigma))
            if j == 0:
                slope = slope * inner
            even = even * slope[:, :LANES]
            odd = odd * slope[:, LANES:]
            tiles.append([t.astype(BF16) for t in (even, odd, later(odd), earlier(even))])
            for q in range(4):
                g_ref[j, :, pl.ds((4 * y + q) * LANES, LANES)] = tiles[y][q]
        if j in (1, 2):
            fill_windows(gs.at[j - 1], tiles)
    send_g = pltpu.make_async_copy(g_ref, g_hbm, sems.at[1])
    send_g.start()
    taps = None
    for j in (1, 2):
        planes = jnp.concatenate([xc_ref[j - 1], xc_ref[j], xc_ref[j + 1]], axis=0)
        term = dot_nt(planes, gs[j - 1])
        taps = term if taps is None else taps + term
    fold = fold_matrix(256)
    kept = [jnp.where(mask, taps[a * CH : (a + 1) * CH], 0.0).astype(BF16) for a in range(3)]
    narrow = dot_nt(jnp.concatenate(kept, axis=0), fold).astype(BF16)
    ordered = dot(
        jnp.concatenate([narrow[a * CH : (a + 1) * CH] for a in range(3)], axis=1), order_ref[...]
    )
    fg[...] = ordered.astype(BF16)
    for out_ref, half in ((other_ref, 1 - core), (mine_ref, core)):
        base = pl.multiple_of(half * F_PART, 16)
        for k in range(6):
            at = (k // 2) * CHUNK + PART + LEFT + (k % 2) * F_PART
            out_ref[pl.ds(at, F_PART), :] = fg[pl.ds(base, F_PART), pl.ds(k * LANES, LANES)]
        out_ref[pl.ds(3 * CHUNK, ROWS - 3 * CHUNK), :] = jnp.zeros((ROWS - 3 * CHUNK, LANES), BF16)
    send_other = pltpu.make_async_copy(other_ref, other_hbm, sems.at[2])
    send_mine = pltpu.make_async_copy(mine_ref, mine_hbm, sems.at[3])
    send_other.start()
    send_mine.start()
    send_wn.wait()
    send_g.wait()
    send_other.wait()
    send_mine.wait()


def tail_kernel(
    after_hbm, g_hbm, wn_hbm, w2_hbm, fw_ref, feat_ref, vg_ref,
    g_ref, wn_ref, w2_ref, gs, w1, acc, sems,
):
    fetches = [
        pltpu.make_async_copy(source, target, sems.at[i])
        for i, (source, target) in enumerate(
            ((g_hbm, g_ref), (wn_hbm, wn_ref), (w2_hbm, w2_ref))
        )
    ]
    for fetch in fetches:
        fetch.start()
    fill_weights(w1, fw_ref[...], True)
    fetches[0].wait()
    for j in range(4):
        tiles = [
            [g_ref[j, :, pl.ds((4 * y + q) * LANES, LANES)] for q in range(4)] for y in range(2)
        ]
        fill_windows(gs.at[j], tiles)
    for j in range(4):
        first, last = max(0, j - 1), min(2, j)
        terms = dot(w1[pl.ds(first * CH, (last - first + 1) * CH), :], gs[j])
        for a in range(first, last + 1):
            term = terms[(a - first) * CH : (a - first + 1) * CH]
            out = j - a
            if a == 0:
                acc[out] = term
            else:
                acc[out] += term
    merge = merge_matrix()
    for out in range(2):
        for y in range(2):
            cut = pl.ds(y * 256, 256)
            vg_ref[out, :, cut] = dot(acc[out, :, cut].astype(BF16), merge).astype(BF16)
    fetches[1].wait()
    fetches[2].wait()
    feat_ref[...] = dot_tn(w2_ref[...], wn_ref[...]).astype(BF16)


def add_kernel(mine_hbm, got_hbm, out_hbm, mine_ref, got_ref, sems):
    fetches = [
        pltpu.make_async_copy(mine_hbm, mine_ref, sems.at[0]),
        pltpu.make_async_copy(got_hbm, got_ref, sems.at[1]),
    ]
    for fetch in fetches:
        fetch.start()
    for fetch in fetches:
        fetch.wait()
    got_ref[...] = (mine_ref[...].astype(F32) + got_ref[...].astype(F32)).astype(BF16)
    send = pltpu.make_async_copy(got_ref, out_hbm, sems.at[0])
    send.start()
    send.wait()


def finish_kernel(factor, half_ref, rows_hbm, *refs):
    strided_hbm, grouped_hbm, rows_ref, strided_ref, grouped_ref, fetch_sems, send_sems = refs[-7:]
    half = half_ref[0]
    fetches = [
        pltpu.make_async_copy(
            rows_hbm.at[pl.ds(k * CHUNK, CHUNK)], rows_ref.at[pl.ds(k * CHUNK, CHUNK)], fetch_sems.at[k]
        )
        for k in range(3)
    ]
    for fetch in fetches:
        fetch.start()
    sends = []
    for k in range(3):
        fetches[k].wait()
        at = k * CHUNK
        here = pl.ds(k * PART, PART)
        strided_ref[here, pl.ds(0, LANES)] = rows_ref[pl.ds(at, PART), :].astype(F32) * factor
        rest = rows_ref[pl.ds(at + PART, LEFT), :].astype(F32) * factor
        strided_ref[pl.ds(k * PART, LEFT), pl.ds(LANES, 64)] = rest[:, :64]
        strided_ref[pl.ds(k * PART + LEFT, RIGHT), pl.ds(LANES, 64)] = rest[:RIGHT, 64:]
        there = pl.ds(pl.multiple_of(half * HALF + k * PART, 8), PART)
        sends.append(
            pltpu.make_async_copy(strided_ref.at[here], strided_hbm.at[there], send_sems.at[k])
        )
        sends[-1].start()
        for i in range(2):
            tile = rows_ref[pl.ds(at + PART + LEFT + i * F_PART, F_PART), :]
            grouped_ref[:, pl.ds((2 * k + i) * LANES, LANES)] = tile.astype(F32) * factor
    there = pl.ds(pl.multiple_of(half * F_PART, 8), F_PART)
    sends.append(pltpu.make_async_copy(grouped_ref, grouped_hbm.at[there], send_sems.at[3]))
    sends[-1].start()
    for send in sends:
        send.wait()


VMEM = pl.BlockSpec(memory_space=pltpu.VMEM)
SMEM = pl.BlockSpec(memory_space=pltpu.SMEM)
ANY = pl.BlockSpec(memory_space=pl.ANY)
MIB = 1024 * 1024


def again_call(own, after):
    return pl.pallas_call(
        again_kernel,
        out_shape=jax.ShapeDtypeStruct(own.shape, BF16),
        in_specs=[ANY, ANY],
        out_specs=ANY,
        scratch_shapes=[pltpu.SemaphoreType.DMA],
        compiler_params=pltpu.CompilerParams(vmem_limit_bytes=MIB),
        name="again",
    )(own, after)


def main_call(inner, core, far, own, twin, weight, w2):
    return pl.pallas_call(
        main_kernel,
        out_shape=(
            jax.ShapeDtypeStruct((ROWS, LANES), BF16),
            jax.ShapeDtypeStruct((ROWS, LANES), BF16),
            jax.ShapeDtypeStruct((TAPS * CH, LANES), BF16),
            jax.ShapeDtypeStruct((4, CH, 8 * LANES), BF16),
        ),
        in_specs=[SMEM, SMEM] + [ANY] * 5,
        out_specs=(ANY,) * 4,
        scratch_shapes=[
            pltpu.VMEM((2, 5, CH, 256), BF16),
            pltpu.VMEM((5, CH, 256), BF16),
            pltpu.VMEM((CH, PG * TAPS), BF16),
            pltpu.VMEM((TAPS * CH, 192), BF16),
            pltpu.VMEM((ROWS, LANES), BF16),
            pltpu.VMEM((ROWS, LANES), BF16),
            pltpu.VMEM((TAPS * CH, LANES), BF16),
            pltpu.VMEM((4, CH, 8 * LANES), BF16),
            pltpu.VMEM((6, WIN, 512), BF16),
            pltpu.VMEM((3 * CH, WIN), BF16),
            pltpu.VMEM((4, CH, 512), F32),
            pltpu.VMEM((4, CH, 512), BF16),
            pltpu.VMEM((2, WIN, 512), BF16),
            pltpu.VMEM((768, 768), BF16),
            pltpu.VMEM((CH, 6 * LANES), BF16),
            pltpu.SemaphoreType.DMA((5,)),
        ],
        compiler_params=pltpu.CompilerParams(vmem_limit_bytes=24 * MIB),
        name="main",
    )(inner, core, far, own, twin, weight, w2)


def tail_call(after, grads, windows, w2, weight):
    return pl.pallas_call(
        tail_kernel,
        out_shape=(
            jax.ShapeDtypeStruct((192, LANES), BF16),
            jax.ShapeDtypeStruct((2, CH, 512), BF16),
        ),
        in_specs=[ANY, ANY, ANY, ANY, VMEM],
        out_specs=(VMEM,) * 2,
        scratch_shapes=[
            pltpu.VMEM((4, CH, 8 * LANES), BF16),
            pltpu.VMEM((TAPS * CH, LANES), BF16),
            pltpu.VMEM((TAPS * CH, 192), BF16),
            pltpu.VMEM((4, WIN, 512), BF16),
            pltpu.VMEM((3 * CH, WIN), BF16),
            pltpu.VMEM((2, CH, 512), F32),
            pltpu.SemaphoreType.DMA((3,)),
        ],
        compiler_params=pltpu.CompilerParams(vmem_limit_bytes=12 * MIB),
        cost_estimate=pl.CostEstimate(flops=10**9, bytes_accessed=4 * 10**6, transcendentals=0),
        name="tail",
    )(after, grads, windows, w2, weight)


def add_call(mine, got):
    return pl.pallas_call(
        add_kernel,
        out_shape=jax.ShapeDtypeStruct((ROWS, LANES), BF16),
        in_specs=[ANY, ANY],
        out_specs=ANY,
        scratch_shapes=[
            pltpu.VMEM((ROWS, LANES), BF16),
            pltpu.VMEM((ROWS, LANES), BF16),
            pltpu.SemaphoreType.DMA((2,)),
        ],
        compiler_params=pltpu.CompilerParams(vmem_limit_bytes=4 * MIB),
        name="add",
    )(mine, got)


def finish_call(factor, half, rows, before=()):
    return pl.pallas_call(
        functools.partial(finish_kernel, factor),
        out_shape=(
            jax.ShapeDtypeStruct((TAPS * CH, 192), F32),
            jax.ShapeDtypeStruct((CH, 6 * LANES), F32),
        ),
        in_specs=[SMEM, ANY] + [ANY] * len(before),
        out_specs=(ANY, ANY),
        scratch_shapes=[
            pltpu.VMEM((ROWS, LANES), BF16),
            pltpu.VMEM((HALF, 192), F32),
            pltpu.VMEM((F_PART, 6 * LANES), F32),
            pltpu.SemaphoreType.DMA((3,)),
            pltpu.SemaphoreType.DMA((4,)),
        ],
        input_output_aliases={2 + i: i for i in range(len(before))},
        compiler_params=pltpu.CompilerParams(vmem_limit_bytes=6 * MIB),
        name="finish",
    )(half, rows, *before)


def zero_kernel(after_hbm, out_ref):
    out_ref[0] = 0.0


def zero_call(after):
    return pl.pallas_call(
        zero_kernel,
        out_shape=jax.ShapeDtypeStruct((1,), F32),
        in_specs=[ANY],
        out_specs=SMEM,
        compiler_params=pltpu.CompilerParams(vmem_limit_bytes=MIB),
        name="zero",
    )(after)


def sum_pieces(parts):
    return jnp.sum(parts.astype(F32), axis=0).astype(BF16)


def to_all(piece, axes, count):
    copies = jnp.broadcast_to(piece[None], (count,) + piece.shape)
    return lax.all_to_all(copies, axes, 0, 0, tiled=True)


def shards(volume, first_weight, second_weight, out_cotangent):
    count = lax.axis_size(SPACE)
    planes = volume[0].transpose(1, 2, 0, 3).reshape(4, CH, 256)
    cotangent = out_cotangent.reshape(2, CH, LANES).transpose(1, 0, 2).reshape(1, CH, 256)
    own = jnp.concatenate([planes, cotangent], axis=0)
    swap = [(0, 1), (1, 0)]
    far = lax.ppermute(
        own,
        SPACE,
        [(i, i + 1) for i in range(1, count - 1, 2)] + [(i, i - 1) for i in range(2, count, 2)],
    )
    core = lax.axis_index("core").astype(jnp.int32).reshape(1)
    inner = jnp.where(lax.axis_index(SPACE) > 0, 1.0, 0.0).astype(F32).reshape(1)
    forward_weight = first_weight.transpose(1, 3, 2, 0).reshape(CH, PG * TAPS)
    twin = lax.ppermute(again_call(own, forward_weight), "core", swap)
    backward_weight = first_weight.transpose(1, 2, 3, 0).reshape(CH, PG * TAPS)
    w2 = second_weight.reshape(TAPS * CH, 192)
    mine, other, windows, grads = main_call(inner, core, far, own, twin, forward_weight, w2)
    chip = add_call(mine, lax.ppermute(other, "core", swap))
    parts = lax.all_to_all(chip.reshape(PIECES, PIECE, LANES), NEAR, 0, 0, tiled=True)
    piece = sum_pieces(parts)
    feat, vgrad = tail_call(piece, grads, windows, w2, backward_weight)
    features = feat.reshape(out_cotangent.shape)
    volume_grad = vgrad.reshape(2, CH, 2, 256).transpose(1, 0, 2, 3)
    parts = to_all(piece, "zh", lax.axis_size("zh"))
    piece = lax.reduce(parts.astype(F32), zero_call(volume_grad)[0], lax.add, (0,)).astype(BF16)
    own_half = to_all(piece, NEAR, PIECES).reshape(ROWS, LANES)
    other_half = lax.ppermute(own_half, "core", swap)
    factor = 1.0 / math.sqrt(lax.axis_size(DP) * lax.axis_size(SPACE) * LANES)
    halves = finish_call(factor, core, own_half)
    second_grad, narrow = finish_call(factor, 1 - core, other_half, halves)
    first_grad = narrow[:, : TAPS * PG].reshape(4, PG, PG, TAPS).transpose(3, 0, 1, 2)
    return (features, volume_grad[None], first_grad, second_grad.reshape(second_weight.shape))


def solution(mesh):
    fine = Mesh(mesh.devices.reshape(2, 8, 2, 2, 4, 2), ("xh", "zh", "zl", "xl", "y", "core"))
    split = P(DP, None, SPACE, None, None)
    return jax.shard_map(
        shards,
        mesh=fine,
        in_specs=(split, P(), P(), split),
        out_specs=(split, split, P(), P()),
        check_vma=False,
    )
```

```python
import functools
import math

import jax
import jax.numpy as jnp
from jax import lax
from jax.experimental import pallas as pl
from jax.experimental.pallas import tpu as pltpu
from jax.sharding import Mesh
from jax.sharding import PartitionSpec as P

SPACE = ("xl", "y", "core")
DP = ("xh", "zh", "zl")
NEAR = ("xh", "xl", "y", "zl")
F32 = jnp.float32
BF16 = jnp.bfloat16

CH = 96
PG = 24
TAPS = 27
WIN = 9 * CH
LANES = 128
HALF = TAPS * CH // 2
PART = HALF // 3
LEFT, RIGHT = 224, PART - 224
F_PART = CH // 2
CHUNK = PART + LEFT + 2 * F_PART
PIECES = 32
PIECE = 72
ROWS = PIECES * PIECE


def dot(a, b):
    return lax.dot_general(a, b, (((1,), (0,)), ((), ())), preferred_element_type=F32)


def dot_nt(a, b):
    return lax.dot_general(a, b, (((1,), (1,)), ((), ())), preferred_element_type=F32)


def dot_tn(a, b):
    return lax.dot_general(a, b, (((0,), (0,)), ((), ())), preferred_element_type=F32)


def later(tile):
    lane = lax.broadcasted_iota(jnp.int32, tile.shape, 1)
    return jnp.where(lane == 0, 0.0, pltpu.roll(tile, 1, 1))


def earlier(tile):
    lane = lax.broadcasted_iota(jnp.int32, tile.shape, 1)
    return jnp.where(lane == LANES - 1, 0.0, pltpu.roll(tile, LANES - 1, 1))


def fill_windows(ref, tiles):
    zero = jnp.zeros((CH, LANES), BF16)
    for b in range(3):
        for c in range(3):
            rows = pl.ds((b * 3 + c) * CH, CH)
            for y in range(2):
                source = y + b - 1
                if source in (0, 1):
                    even, odd, odd_later, even_earlier = tiles[source]
                    pair = ((odd_later, even), (even, odd), (odd, even_earlier))[c]
                else:
                    pair = (zero, zero)
                for parity in range(2):
                    ref[rows, pl.ds((2 * y + parity) * LANES, LANES)] = pair[parity]


def ones_where(condition):
    return jnp.where(condition, 1.0, 0.0).astype(BF16)


def split_matrix():
    z = lax.broadcasted_iota(jnp.int32, (256, LANES), 0)
    k2 = 2 * lax.broadcasted_iota(jnp.int32, (256, LANES), 1)
    return jnp.concatenate([ones_where(z == k2 + off) for off in (0, 1, -1, 2)], axis=1)


def merge_matrix():
    lane = lax.broadcasted_iota(jnp.int32, (LANES, 256), 0)
    z = lax.broadcasted_iota(jnp.int32, (LANES, 256), 1)
    return jnp.concatenate([ones_where(z == 2 * lane + bit) for bit in (0, 1)], axis=0)


def quotient(value, divisor, bits):
    return (value * (2**bits // divisor + 1)) >> bits


def fold_matrix(rows):
    row = lax.broadcasted_iota(jnp.int32, (rows, WIN), 0)
    column = lax.broadcasted_iota(jnp.int32, (1, WIN), 1)
    target = quotient(column, CH, 16) * PG + column - PG * quotient(column, PG, 16)
    return ones_where(row == target)


def group_mask():
    row = lax.broadcasted_iota(jnp.int32, (CH, WIN), 0)
    column = lax.broadcasted_iota(jnp.int32, (1, WIN), 1)
    offset = row - PG * quotient(column - CH * quotient(column, CH, 16), PG, 16)
    return (offset >= 0) & (offset < PG)


def order_matrix():
    row = lax.broadcasted_iota(jnp.int32, (3 * 256, 6 * LANES), 0)
    column = lax.broadcasted_iota(jnp.int32, (1, 6 * LANES), 1)
    channel = quotient(column, TAPS, 16)
    tap = column - TAPS * channel
    plane = quotient(tap, 9, 16)
    target = plane * 256 + (8 - tap + 9 * plane) * PG + channel
    return ones_where((row == target) & (column < PG * TAPS))


def expand(narrow, fold, mask):
    return jnp.where(mask, dot(narrow, fold), 0.0).astype(BF16)


def fill_weights(w1, fw, flip):
    row = lax.broadcasted_iota(jnp.int32, (3 * 256, PG * TAPS), 0)
    column = lax.broadcasted_iota(jnp.int32, (1, PG * TAPS), 1)
    channel = quotient(column, TAPS, 16)
    tap = column - TAPS * channel
    if flip:
        tap = TAPS - 1 - tap
    plane = quotient(tap, 9, 16)
    order = ones_where(row == plane * 256 + (tap - 9 * plane) * PG + channel)
    narrow = dot_nt(fw, order).astype(BF16)
    mask = group_mask()
    fold = fold_matrix(256)
    for a in range(3):
        w1[pl.ds(a * CH, CH), :] = expand(narrow[:, a * 256 : (a + 1) * 256], fold, mask)


def again_kernel(own_hbm, after_hbm, again_hbm, sem):
    copy = pltpu.make_async_copy(own_hbm, again_hbm, sem)
    copy.start()
    copy.wait()


def prepare_kernel(fw_ref, w1_hbm, w1, sem):
    fill_weights(w1, fw_ref[...], False)
    send = pltpu.make_async_copy(w1, w1_hbm, sem)
    send.start()
    send.wait()


def cotangent_of(slab):
    return jnp.concatenate([slab[4, :, :LANES], slab[4, :, LANES:]], axis=0)


def main_kernel(
    inner_ref, core_ref, far_hbm, own_hbm, twin_hbm, w1_hbm, w2_hbm,
    mine_hbm, other_hbm, wn_hbm, g_hbm,
    beside, own_ref, w2_ref, mine_ref, other_ref, wn_ref, g_ref,
    xs, w1, pre_ref, xc_ref, gs, order_ref, fg, sems,
):
    inner = inner_ref[0]
    core = core_ref[0]
    low_ref, high_ref = beside.at[0], beside.at[1]
    fetches = [
        pltpu.make_async_copy(own_hbm, own_ref, sems.at[0]),
        pltpu.make_async_copy(far_hbm, beside.at[core], sems.at[1]),
        pltpu.make_async_copy(twin_hbm, beside.at[1 - core], sems.at[2]),
        pltpu.make_async_copy(w1_hbm, w1, sems.at[3]),
        pltpu.make_async_copy(w2_hbm, w2_ref, sems.at[4]),
    ]
    for fetch in fetches:
        fetch.start()
    split = split_matrix()
    mask = group_mask()
    fetches[0].wait()
    for e in (2, 3, 0, 1, 4, 5):
        slab = (low_ref, own_ref, high_ref)[e // 2]
        if e == 0:
            fetches[1].wait()
            fetches[2].wait()
        tiles = []
        for y in range(2):
            parts = dot(slab[2 * (e % 2) + y], split).astype(BF16)
            tiles.append([parts[:, q * LANES : (q + 1) * LANES] for q in range(4)])
            if 1 <= e <= 4:
                xc_ref[e - 1, :, pl.ds(y * 256, 256)] = parts[:, :256]
        fill_windows(xs.at[e], tiles)
    fetches[3].wait()
    for e in range(6):
        first, last = max(0, e - 3), min(2, e)
        terms = dot(w1[pl.ds(first * CH, (last - first + 1) * CH), :], xs[e])
        for a in range(first, last + 1):
            term = terms[(a - first) * CH : (a - first + 1) * CH]
            j = e - a
            if a == 0:
                pre_ref[j] = term
            else:
                pre_ref[j] += term
    zero = jnp.zeros((CH, LANES), BF16)
    for a in range(3):
        for c in range(3):
            wn_ref[pl.ds((9 * a + c) * CH, CH), :] = zero
        for y in range(2):
            value = pre_ref[a, :, pl.ds(y * 256, 256)]
            hidden = value * jax.nn.sigmoid(value)
            if a == 0:
                hidden = hidden * inner
            even, odd = hidden[:, :LANES], hidden[:, LANES:]
            base = (9 * a + 3 * (y + 1)) * CH
            wn_ref[pl.ds(base, CH), :] = later(odd).astype(BF16)
            wn_ref[pl.ds(base + CH, CH), :] = even.astype(BF16)
            wn_ref[pl.ds(base + 2 * CH, CH), :] = odd.astype(BF16)
    send_wn = pltpu.make_async_copy(wn_ref, wn_hbm, sems.at[0])
    send_wn.start()
    cot = cotangent_of(own_ref)
    rest = cot[LANES:]
    none = jnp.zeros_like(rest)
    both = jnp.concatenate(
        [jnp.concatenate([rest, none], axis=1), jnp.concatenate([none, rest], axis=1)], axis=0
    )
    fill = jnp.zeros((LEFT - RIGHT, LANES), BF16)
    for out_ref, half in ((other_ref, 1 - core), (mine_ref, core)):
        for k in range(3):
            base = pl.multiple_of(half * HALF + k * PART, 16)
            wide = dot_nt(wn_ref[pl.ds(base, PART), :], cot[:LANES])
            out_ref[pl.ds(k * CHUNK, PART), :] = wide.astype(BF16)
            left = wn_ref[pl.ds(base, LEFT), :]
            right = jnp.concatenate([wn_ref[pl.ds(base + LEFT, RIGHT), :], fill], axis=0)
            pairs = jnp.concatenate([left, right], axis=1)
            out_ref[pl.ds(k * CHUNK + PART, LEFT), :] = dot_nt(pairs, both).astype(BF16)
    with_above = jnp.concatenate([cot, cotangent_of(high_ref)], axis=1)
    with_below = jnp.concatenate([cot, cotangent_of(low_ref)], axis=1)
    order_ref[...] = order_matrix()
    fetches[4].wait()
    spread = [
        dot(w2_ref[pl.ds((9 * a + 3) * CH, 6 * CH), :], with_below if a == 2 else with_above)
        for a in range(3)
    ]
    for j in range(4):
        sources = {0: ((0, 0), (2, 1)), 1: ((1, 0),), 2: ((2, 0), (0, 1)), 3: ((1, 1),)}[j]
        tiles = []
        for y in range(2):
            got = []
            for c in range(3):
                total = None
                for a, part in sources:
                    tile = spread[a][
                        (3 * y + c) * CH : (3 * y + c + 1) * CH, part * LANES : (part + 1) * LANES
                    ]
                    total = tile if total is None else total + tile
                got.append(total)
            even = got[1]
            odd = got[2] + earlier(got[0])
            value = pre_ref[j, :, pl.ds(y * 256, 256)]
            sigma = jax.nn.sigmoid(value)
            slope = sigma * (1.0 + value * (1.0 - sigma))
            if j == 0:
                slope = slope * inner
            even = even * slope[:, :LANES]
            odd = odd * slope[:, LANES:]
            tiles.append([t.astype(BF16) for t in (even, odd, later(odd), earlier(even))])
            for q in range(4):
                g_ref[j, :, pl.ds((4 * y + q) * LANES, LANES)] = tiles[y][q]
        if j in (1, 2):
            fill_windows(gs.at[j - 1], tiles)
    send_g = pltpu.make_async_copy(g_ref, g_hbm, sems.at[1])
    send_g.start()
    taps = None
    for j in (1, 2):
        planes = jnp.concatenate([xc_ref[j - 1], xc_ref[j], xc_ref[j + 1]], axis=0)
        term = dot_nt(planes, gs[j - 1])
        taps = term if taps is None else taps + term
    fold = fold_matrix(256)
    kept = [jnp.where(mask, taps[a * CH : (a + 1) * CH], 0.0).astype(BF16) for a in range(3)]
    narrow = dot_nt(jnp.concatenate(kept, axis=0), fold).astype(BF16)
    ordered = dot(
        jnp.concatenate([narrow[a * CH : (a + 1) * CH] for a in range(3)], axis=1), order_ref[...]
    )
    fg[...] = ordered.astype(BF16)
    for out_ref, half in ((other_ref, 1 - core), (mine_ref, core)):
        base = pl.multiple_of(half * F_PART, 16)
        for k in range(6):
            at = (k // 2) * CHUNK + PART + LEFT + (k % 2) * F_PART
            out_ref[pl.ds(at, F_PART), :] = fg[pl.ds(base, F_PART), pl.ds(k * LANES, LANES)]
        out_ref[pl.ds(3 * CHUNK, ROWS - 3 * CHUNK), :] = jnp.zeros((ROWS - 3 * CHUNK, LANES), BF16)
    send_other = pltpu.make_async_copy(other_ref, other_hbm, sems.at[2])
    send_mine = pltpu.make_async_copy(mine_ref, mine_hbm, sems.at[3])
    send_other.start()
    send_mine.start()
    send_wn.wait()
    send_g.wait()
    send_other.wait()
    send_mine.wait()


def tail_kernel(
    after_hbm, g_hbm, wn_hbm, w2_hbm, fw_ref, feat_ref, vg_ref,
    g_ref, wn_ref, w2_ref, gs, w1, acc, sems,
):
    fetches = [
        pltpu.make_async_copy(source, target, sems.at[i])
        for i, (source, target) in enumerate(
            ((g_hbm, g_ref), (wn_hbm, wn_ref), (w2_hbm, w2_ref))
        )
    ]
    for fetch in fetches:
        fetch.start()
    fill_weights(w1, fw_ref[...], True)
    fetches[0].wait()
    for j in range(4):
        tiles = [
            [g_ref[j, :, pl.ds((4 * y + q) * LANES, LANES)] for q in range(4)] for y in range(2)
        ]
        fill_windows(gs.at[j], tiles)
    for j in range(4):
        first, last = max(0, j - 1), min(2, j)
        terms = dot(w1[pl.ds(first * CH, (last - first + 1) * CH), :], gs[j])
        for a in range(first, last + 1):
            term = terms[(a - first) * CH : (a - first + 1) * CH]
            out = j - a
            if a == 0:
                acc[out] = term
            else:
                acc[out] += term
    merge = merge_matrix()
    for out in range(2):
        for y in range(2):
            cut = pl.ds(y * 256, 256)
            vg_ref[out, :, cut] = dot(acc[out, :, cut].astype(BF16), merge).astype(BF16)
    fetches[1].wait()
    fetches[2].wait()
    feat_ref[...] = dot_tn(w2_ref[...], wn_ref[...]).astype(BF16)


def add_kernel(mine_hbm, got_hbm, out_hbm, mine_ref, got_ref, sems):
    fetches = [
        pltpu.make_async_copy(mine_hbm, mine_ref, sems.at[0]),
        pltpu.make_async_copy(got_hbm, got_ref, sems.at[1]),
    ]
    for fetch in fetches:
        fetch.start()
    for fetch in fetches:
        fetch.wait()
    got_ref[...] = (mine_ref[...].astype(F32) + got_ref[...].astype(F32)).astype(BF16)
    send = pltpu.make_async_copy(got_ref, out_hbm, sems.at[0])
    send.start()
    send.wait()


def finish_kernel(factor, half_ref, rows_hbm, *refs):
    strided_hbm, grouped_hbm, rows_ref, strided_ref, grouped_ref, fetch_sems, send_sems = refs[-7:]
    half = half_ref[0]
    fetches = [
        pltpu.make_async_copy(
            rows_hbm.at[pl.ds(k * CHUNK, CHUNK)], rows_ref.at[pl.ds(k * CHUNK, CHUNK)], fetch_sems.at[k]
        )
        for k in range(3)
    ]
    for fetch in fetches:
        fetch.start()
    sends = []
    for k in range(3):
        fetches[k].wait()
        at = k * CHUNK
        here = pl.ds(k * PART, PART)
        strided_ref[here, pl.ds(0, LANES)] = rows_ref[pl.ds(at, PART), :].astype(F32) * factor
        rest = rows_ref[pl.ds(at + PART, LEFT), :].astype(F32) * factor
        strided_ref[pl.ds(k * PART, LEFT), pl.ds(LANES, 64)] = rest[:, :64]
        strided_ref[pl.ds(k * PART + LEFT, RIGHT), pl.ds(LANES, 64)] = rest[:RIGHT, 64:]
        there = pl.ds(pl.multiple_of(half * HALF + k * PART, 8), PART)
        sends.append(
            pltpu.make_async_copy(strided_ref.at[here], strided_hbm.at[there], send_sems.at[k])
        )
        sends[-1].start()
        for i in range(2):
            tile = rows_ref[pl.ds(at + PART + LEFT + i * F_PART, F_PART), :]
            grouped_ref[:, pl.ds((2 * k + i) * LANES, LANES)] = tile.astype(F32) * factor
    there = pl.ds(pl.multiple_of(half * F_PART, 8), F_PART)
    sends.append(pltpu.make_async_copy(grouped_ref, grouped_hbm.at[there], send_sems.at[3]))
    sends[-1].start()
    for send in sends:
        send.wait()


VMEM = pl.BlockSpec(memory_space=pltpu.VMEM)
SMEM = pl.BlockSpec(memory_space=pltpu.SMEM)
ANY = pl.BlockSpec(memory_space=pl.ANY)
MIB = 1024 * 1024


def again_call(own, after):
    return pl.pallas_call(
        again_kernel,
        out_shape=jax.ShapeDtypeStruct(own.shape, BF16),
        in_specs=[ANY, ANY],
        out_specs=ANY,
        scratch_shapes=[pltpu.SemaphoreType.DMA],
        compiler_params=pltpu.CompilerParams(vmem_limit_bytes=MIB),
        name="again",
    )(own, after)


def prepare_call(weight):
    return pl.pallas_call(
        prepare_kernel,
        out_shape=jax.ShapeDtypeStruct((3 * CH, WIN), BF16),
        in_specs=[VMEM],
        out_specs=ANY,
        scratch_shapes=[pltpu.VMEM((3 * CH, WIN), BF16), pltpu.SemaphoreType.DMA],
        compiler_params=pltpu.CompilerParams(vmem_limit_bytes=6 * MIB),
        name="prepare",
    )(weight)


def main_call(inner, core, far, own, twin, weight, w2):
    return pl.pallas_call(
        main_kernel,
        out_shape=(
            jax.ShapeDtypeStruct((ROWS, LANES), BF16),
            jax.ShapeDtypeStruct((ROWS, LANES), BF16),
            jax.ShapeDtypeStruct((TAPS * CH, LANES), BF16),
            jax.ShapeDtypeStruct((4, CH, 8 * LANES), BF16),
        ),
        in_specs=[SMEM, SMEM] + [ANY] * 5,
        out_specs=(ANY,) * 4,
        scratch_shapes=[
            pltpu.VMEM((2, 5, CH, 256), BF16),
            pltpu.VMEM((5, CH, 256), BF16),
            pltpu.VMEM((TAPS * CH, 192), BF16),
            pltpu.VMEM((ROWS, LANES), BF16),
            pltpu.VMEM((ROWS, LANES), BF16),
            pltpu.VMEM((TAPS * CH, LANES), BF16),
            pltpu.VMEM((4, CH, 8 * LANES), BF16),
            pltpu.VMEM((6, WIN, 512), BF16),
            pltpu.VMEM((3 * CH, WIN), BF16),
            pltpu.VMEM((4, CH, 512), F32),
            pltpu.VMEM((4, CH, 512), BF16),
            pltpu.VMEM((2, WIN, 512), BF16),
            pltpu.VMEM((768, 768), BF16),
            pltpu.VMEM((CH, 6 * LANES), BF16),
            pltpu.SemaphoreType.DMA((5,)),
        ],
        compiler_params=pltpu.CompilerParams(vmem_limit_bytes=24 * MIB),
        name="main",
    )(inner, core, far, own, twin, weight, w2)


def tail_call(after, grads, windows, w2, weight):
    return pl.pallas_call(
        tail_kernel,
        out_shape=(
            jax.ShapeDtypeStruct((192, LANES), BF16),
            jax.ShapeDtypeStruct((2, CH, 512), BF16),
        ),
        in_specs=[ANY, ANY, ANY, ANY, VMEM],
        out_specs=(VMEM,) * 2,
        scratch_shapes=[
            pltpu.VMEM((4, CH, 8 * LANES), BF16),
            pltpu.VMEM((TAPS * CH, LANES), BF16),
            pltpu.VMEM((TAPS * CH, 192), BF16),
            pltpu.VMEM((4, WIN, 512), BF16),
            pltpu.VMEM((3 * CH, WIN), BF16),
            pltpu.VMEM((2, CH, 512), F32),
            pltpu.SemaphoreType.DMA((3,)),
        ],
        compiler_params=pltpu.CompilerParams(vmem_limit_bytes=52 * MIB),
        cost_estimate=pl.CostEstimate(flops=10**9, bytes_accessed=4 * 10**6, transcendentals=0),
        name="tail",
    )(after, grads, windows, w2, weight)


def add_call(mine, got):
    return pl.pallas_call(
        add_kernel,
        out_shape=jax.ShapeDtypeStruct((ROWS, LANES), BF16),
        in_specs=[ANY, ANY],
        out_specs=ANY,
        scratch_shapes=[
            pltpu.VMEM((ROWS, LANES), BF16),
            pltpu.VMEM((ROWS, LANES), BF16),
            pltpu.SemaphoreType.DMA((2,)),
        ],
        compiler_params=pltpu.CompilerParams(vmem_limit_bytes=4 * MIB),
        name="add",
    )(mine, got)


def finish_call(factor, half, rows, before=()):
    return pl.pallas_call(
        functools.partial(finish_kernel, factor),
        out_shape=(
            jax.ShapeDtypeStruct((TAPS * CH, 192), F32),
            jax.ShapeDtypeStruct((CH, 6 * LANES), F32),
        ),
        in_specs=[SMEM, ANY] + [ANY] * len(before),
        out_specs=(ANY, ANY),
        scratch_shapes=[
            pltpu.VMEM((ROWS, LANES), BF16),
            pltpu.VMEM((HALF, 192), F32),
            pltpu.VMEM((F_PART, 6 * LANES), F32),
            pltpu.SemaphoreType.DMA((3,)),
            pltpu.SemaphoreType.DMA((4,)),
        ],
        input_output_aliases={2 + i: i for i in range(len(before))},
        compiler_params=pltpu.CompilerParams(vmem_limit_bytes=6 * MIB),
        name="finish",
    )(half, rows, *before)


def zero_kernel(after_hbm, out_ref):
    out_ref[0] = 0.0


def zero_call(after):
    return pl.pallas_call(
        zero_kernel,
        out_shape=jax.ShapeDtypeStruct((1,), F32),
        in_specs=[ANY],
        out_specs=SMEM,
        compiler_params=pltpu.CompilerParams(vmem_limit_bytes=MIB),
        name="zero",
    )(after)


def sum_pieces(parts):
    return jnp.sum(parts.astype(F32), axis=0).astype(BF16)


def to_all(piece, axes, count):
    copies = jnp.broadcast_to(piece[None], (count,) + piece.shape)
    return lax.all_to_all(copies, axes, 0, 0, tiled=True)


def shards(volume, first_weight, second_weight, out_cotangent):
    count = lax.axis_size(SPACE)
    planes = volume[0].transpose(1, 2, 0, 3).reshape(4, CH, 256)
    cotangent = out_cotangent.reshape(2, CH, LANES).transpose(1, 0, 2).reshape(1, CH, 256)
    own = jnp.concatenate([planes, cotangent], axis=0)
    swap = [(0, 1), (1, 0)]
    far = lax.ppermute(
        own,
        SPACE,
        [(i, i + 1) for i in range(1, count - 1, 2)] + [(i, i - 1) for i in range(2, count, 2)],
    )
    core = lax.axis_index("core").astype(jnp.int32).reshape(1)
    inner = jnp.where(lax.axis_index(SPACE) > 0, 1.0, 0.0).astype(F32).reshape(1)
    forward_weight = first_weight.transpose(1, 3, 2, 0).reshape(CH, PG * TAPS)
    twin = lax.ppermute(again_call(own, forward_weight), "core", swap)
    forward_weight = prepare_call(forward_weight)
    backward_weight = first_weight.transpose(1, 2, 3, 0).reshape(CH, PG * TAPS)
    w2 = second_weight.reshape(TAPS * CH, 192)
    mine, other, windows, grads = main_call(inner, core, far, own, twin, forward_weight, w2)
    chip = add_call(mine, lax.ppermute(other, "core", swap))
    parts = lax.all_to_all(chip.reshape(PIECES, PIECE, LANES), NEAR, 0, 0, tiled=True)
    piece = sum_pieces(parts)
    feat, vgrad = tail_call(piece, grads, windows, w2, backward_weight)
    features = feat.reshape(out_cotangent.shape)
    volume_grad = vgrad.reshape(2, CH, 2, 256).transpose(1, 0, 2, 3)
    parts = to_all(piece, "zh", lax.axis_size("zh"))
    piece = lax.reduce(parts.astype(F32), zero_call(volume_grad)[0], lax.add, (0,)).astype(BF16)
    own_half = to_all(piece, NEAR, PIECES).reshape(ROWS, LANES)
    other_half = lax.ppermute(own_half, "core", swap)
    factor = 1.0 / math.sqrt(lax.axis_size(DP) * lax.axis_size(SPACE) * LANES)
    halves = finish_call(factor, core, own_half)
    second_grad, narrow = finish_call(factor, 1 - core, other_half, halves)
    first_grad = narrow[:, : TAPS * PG].reshape(4, PG, PG, TAPS).transpose(3, 0, 1, 2)
    return (features, volume_grad[None], first_grad, second_grad.reshape(second_weight.shape))


def solution(mesh):
    fine = Mesh(mesh.devices.reshape(2, 8, 2, 2, 4, 2), ("xh", "zh", "zl", "xl", "y", "core"))
    split = P(DP, None, SPACE, None, None)
    return jax.shard_map(
        shards,
        mesh=fine,
        in_specs=(split, P(), P(), split),
        out_specs=(split, split, P(), P()),
        check_vma=False,
    )
```

```python
import functools
import math

import jax
import jax.numpy as jnp
from jax import lax
from jax.experimental import pallas as pl
from jax.experimental.pallas import tpu as pltpu
from jax.sharding import Mesh
from jax.sharding import PartitionSpec as P

SPACE = ("xl", "y", "core")
DP = ("xh", "zh", "zl")
NEAR = ("xh", "xl", "y", "zl")
F32 = jnp.float32
BF16 = jnp.bfloat16

CH = 96
PG = 24
TAPS = 27
WIN = 9 * CH
PAIR = CH // 2
WIN2 = 9 * PAIR
LANES = 128
HALF = TAPS * CH // 2
PART = HALF // 3
LEFT, RIGHT = 224, PART - 224
F_PART = CH // 2
CHUNK = PART + LEFT + 2 * F_PART
PIECES = 32
PIECE = 72
ROWS = PIECES * PIECE


def dot(a, b):
    return lax.dot_general(a, b, (((1,), (0,)), ((), ())), preferred_element_type=F32)


def dot_nt(a, b):
    return lax.dot_general(a, b, (((1,), (1,)), ((), ())), preferred_element_type=F32)


def dot_tn(a, b):
    return lax.dot_general(a, b, (((0,), (0,)), ((), ())), preferred_element_type=F32)


def later(tile):
    lane = lax.broadcasted_iota(jnp.int32, tile.shape, 1)
    return jnp.where(lane == 0, 0.0, pltpu.roll(tile, 1, 1))


def earlier(tile):
    lane = lax.broadcasted_iota(jnp.int32, tile.shape, 1)
    return jnp.where(lane == LANES - 1, 0.0, pltpu.roll(tile, LANES - 1, 1))


def fill_windows(ref, tiles):
    zero = jnp.zeros((CH, LANES), BF16)
    for b in range(3):
        for c in range(3):
            for y in range(2):
                source = y + b - 1
                if source in (0, 1):
                    even, odd, odd_later, even_earlier = tiles[source]
                    pair = ((odd_later, even), (even, odd), (odd, even_earlier))[c]
                else:
                    pair = (zero, zero)
                for h in range(2):
                    rows = pl.ds(h * WIN2 + (b * 3 + c) * PAIR, PAIR)
                    for parity in range(2):
                        ref[rows, pl.ds((2 * y + parity) * LANES, LANES)] = pair[parity][
                            h * PAIR : (h + 1) * PAIR
                        ]


def ones_where(condition):
    return jnp.where(condition, 1.0, 0.0).astype(BF16)


def split_matrix():
    z = lax.broadcasted_iota(jnp.int32, (256, LANES), 0)
    k2 = 2 * lax.broadcasted_iota(jnp.int32, (256, LANES), 1)
    return jnp.concatenate([ones_where(z == k2 + off) for off in (0, 1, -1, 2)], axis=1)


def merge_matrix():
    lane = lax.broadcasted_iota(jnp.int32, (LANES, 256), 0)
    z = lax.broadcasted_iota(jnp.int32, (LANES, 256), 1)
    return jnp.concatenate([ones_where(z == 2 * lane + bit) for bit in (0, 1)], axis=0)


def quotient(value, divisor, bits):
    return (value * (2**bits // divisor + 1)) >> bits


def fold_matrix():
    row = lax.broadcasted_iota(jnp.int32, (256, WIN2), 0)
    column = lax.broadcasted_iota(jnp.int32, (1, WIN2), 1)
    target = quotient(column, PAIR, 16) * PG + column - PG * quotient(column, PG, 16)
    return ones_where(row == target)


def group_mask():
    row = lax.broadcasted_iota(jnp.int32, (PAIR, WIN2), 0)
    column = lax.broadcasted_iota(jnp.int32, (1, WIN2), 1)
    offset = row - PG * quotient(column - PAIR * quotient(column, PAIR, 16), PG, 16)
    return (offset >= 0) & (offset < PG)


def order_matrix():
    row = lax.broadcasted_iota(jnp.int32, (3 * 256, 6 * LANES), 0)
    column = lax.broadcasted_iota(jnp.int32, (1, 6 * LANES), 1)
    channel = quotient(column, TAPS, 16)
    tap = column - TAPS * channel
    plane = quotient(tap, 9, 16)
    target = plane * 256 + (8 - tap + 9 * plane) * PG + channel
    return ones_where((row == target) & (column < PG * TAPS))


def fill_weights(w1, fw, flip):
    row = lax.broadcasted_iota(jnp.int32, (3 * 256, PG * TAPS), 0)
    column = lax.broadcasted_iota(jnp.int32, (1, PG * TAPS), 1)
    channel = quotient(column, TAPS, 16)
    tap = column - TAPS * channel
    if flip:
        tap = TAPS - 1 - tap
    plane = quotient(tap, 9, 16)
    order = ones_where(row == plane * 256 + (tap - 9 * plane) * PG + channel)
    narrow = dot_nt(fw, order).astype(BF16)
    mask = group_mask()
    fold = fold_matrix()
    for h in range(2):
        for a in range(3):
            block = dot(narrow[h * PAIR : (h + 1) * PAIR, a * 256 : (a + 1) * 256], fold)
            w1[h, pl.ds(a * PAIR, PAIR), :] = jnp.where(mask, block, 0.0).astype(BF16)


def again_kernel(own_hbm, after_hbm, again_hbm, sem):
    copy = pltpu.make_async_copy(own_hbm, again_hbm, sem)
    copy.start()
    copy.wait()


def prepare_kernel(fw_ref, w1_hbm, w1, sem):
    fill_weights(w1, fw_ref[...], False)
    send = pltpu.make_async_copy(w1, w1_hbm, sem)
    send.start()
    send.wait()


def cotangent_of(slab):
    return jnp.concatenate([slab[4, :, :LANES], slab[4, :, LANES:]], axis=0)


def main_kernel(
    inner_ref, core_ref, far_hbm, own_hbm, twin_hbm, w1_hbm, w2_hbm,
    mine_hbm, other_hbm, wn_hbm, g_hbm,
    beside, own_ref, w2_ref, mine_ref, other_ref, wn_ref, g_ref,
    xs, w1, pre_ref, xc_ref, gs, order_ref, fg, sems,
):
    inner = inner_ref[0]
    core = core_ref[0]
    low_ref, high_ref = beside.at[0], beside.at[1]
    fetches = [
        pltpu.make_async_copy(own_hbm, own_ref, sems.at[0]),
        pltpu.make_async_copy(far_hbm, beside.at[core], sems.at[1]),
        pltpu.make_async_copy(twin_hbm, beside.at[1 - core], sems.at[2]),
        pltpu.make_async_copy(w1_hbm, w1, sems.at[3]),
        pltpu.make_async_copy(w2_hbm, w2_ref, sems.at[4]),
    ]
    for fetch in fetches:
        fetch.start()
    split = split_matrix()
    mask = group_mask()
    fetches[0].wait()
    for e in (2, 3, 0, 1, 4, 5):
        slab = (low_ref, own_ref, high_ref)[e // 2]
        if e == 0:
            fetches[1].wait()
            fetches[2].wait()
        tiles = []
        for y in range(2):
            parts = dot(slab[2 * (e % 2) + y], split).astype(BF16)
            tiles.append([parts[:, q * LANES : (q + 1) * LANES] for q in range(4)])
            if 1 <= e <= 4:
                xc_ref[e - 1, :, pl.ds(y * 256, 256)] = parts[:, :256]
        fill_windows(xs.at[e], tiles)
    fetches[3].wait()
    for e in range(6):
        first, last = max(0, e - 3), min(2, e)
        for h in range(2):
            here = pl.ds(h * PAIR, PAIR)
            terms = dot(
                w1[h, pl.ds(first * PAIR, (last - first + 1) * PAIR), :],
                xs[e, pl.ds(h * WIN2, WIN2), :],
            )
            for a in range(first, last + 1):
                term = terms[(a - first) * PAIR : (a - first + 1) * PAIR]
                j = e - a
                if a == 0:
                    pre_ref[j, here, :] = term
                else:
                    pre_ref[j, here, :] += term
    zero = jnp.zeros((CH, LANES), BF16)
    for a in range(3):
        for c in range(3):
            wn_ref[pl.ds((9 * a + c) * CH, CH), :] = zero
        for y in range(2):
            value = pre_ref[a, :, pl.ds(y * 256, 256)]
            hidden = value * jax.nn.sigmoid(value)
            if a == 0:
                hidden = hidden * inner
            even, odd = hidden[:, :LANES], hidden[:, LANES:]
            base = (9 * a + 3 * (y + 1)) * CH
            wn_ref[pl.ds(base, CH), :] = later(odd).astype(BF16)
            wn_ref[pl.ds(base + CH, CH), :] = even.astype(BF16)
            wn_ref[pl.ds(base + 2 * CH, CH), :] = odd.astype(BF16)
    send_wn = pltpu.make_async_copy(wn_ref, wn_hbm, sems.at[0])
    send_wn.start()
    cot = cotangent_of(own_ref)
    rest = cot[LANES:]
    none = jnp.zeros_like(rest)
    both = jnp.concatenate(
        [jnp.concatenate([rest, none], axis=1), jnp.concatenate([none, rest], axis=1)], axis=0
    )
    fill = jnp.zeros((LEFT - RIGHT, LANES), BF16)
    for out_ref, half in ((other_ref, 1 - core), (mine_ref, core)):
        for k in range(3):
            base = pl.multiple_of(half * HALF + k * PART, 16)
            wide = dot_nt(wn_ref[pl.ds(base, PART), :], cot[:LANES])
            out_ref[pl.ds(k * CHUNK, PART), :] = wide.astype(BF16)
            left = wn_ref[pl.ds(base, LEFT), :]
            right = jnp.concatenate([wn_ref[pl.ds(base + LEFT, RIGHT), :], fill], axis=0)
            pairs = jnp.concatenate([left, right], axis=1)
            out_ref[pl.ds(k * CHUNK + PART, LEFT), :] = dot_nt(pairs, both).astype(BF16)
    with_above = jnp.concatenate([cot, cotangent_of(high_ref)], axis=1)
    with_below = jnp.concatenate([cot, cotangent_of(low_ref)], axis=1)
    order_ref[...] = order_matrix()
    fetches[4].wait()
    spread = [
        dot(w2_ref[pl.ds((9 * a + 3) * CH, 6 * CH), :], with_below if a == 2 else with_above)
        for a in range(3)
    ]
    for j in range(4):
        sources = {0: ((0, 0), (2, 1)), 1: ((1, 0),), 2: ((2, 0), (0, 1)), 3: ((1, 1),)}[j]
        tiles = []
        for y in range(2):
            got = []
            for c in range(3):
                total = None
                for a, part in sources:
                    tile = spread[a][
                        (3 * y + c) * CH : (3 * y + c + 1) * CH, part * LANES : (part + 1) * LANES
                    ]
                    total = tile if total is None else total + tile
                got.append(total)
            even = got[1]
            odd = got[2] + earlier(got[0])
            value = pre_ref[j, :, pl.ds(y * 256, 256)]
            sigma = jax.nn.sigmoid(value)
            slope = sigma * (1.0 + value * (1.0 - sigma))
            if j == 0:
                slope = slope * inner
            even = even * slope[:, :LANES]
            odd = odd * slope[:, LANES:]
            tiles.append([t.astype(BF16) for t in (even, odd, later(odd), earlier(even))])
            for q in range(4):
                g_ref[j, :, pl.ds((4 * y + q) * LANES, LANES)] = tiles[y][q]
        if j in (1, 2):
            fill_windows(gs.at[j - 1], tiles)
    send_g = pltpu.make_async_copy(g_ref, g_hbm, sems.at[1])
    send_g.start()
    fold = fold_matrix()
    narrow = []
    for h in range(2):
        here = pl.ds(h * PAIR, PAIR)
        taps = None
        for j in (1, 2):
            planes = jnp.concatenate([xc_ref[j + a, here, :] for a in (-1, 0, 1)], axis=0)
            term = dot_nt(planes, gs[j - 1, pl.ds(h * WIN2, WIN2), :])
            taps = term if taps is None else taps + term
        kept = [
            jnp.where(mask, taps[a * PAIR : (a + 1) * PAIR], 0.0).astype(BF16) for a in range(3)
        ]
        narrow.append(dot_nt(jnp.concatenate(kept, axis=0), fold).astype(BF16))
    ordered = dot(
        jnp.concatenate(
            [
                jnp.concatenate([part[a * PAIR : (a + 1) * PAIR] for part in narrow], axis=0)
                for a in range(3)
            ],
            axis=1,
        ),
        order_ref[...],
    )
    fg[...] = ordered.astype(BF16)
    for out_ref, half in ((other_ref, 1 - core), (mine_ref, core)):
        base = pl.multiple_of(half * F_PART, 16)
        for k in range(6):
            at = (k // 2) * CHUNK + PART + LEFT + (k % 2) * F_PART
            out_ref[pl.ds(at, F_PART), :] = fg[pl.ds(base, F_PART), pl.ds(k * LANES, LANES)]
        out_ref[pl.ds(3 * CHUNK, ROWS - 3 * CHUNK), :] = jnp.zeros((ROWS - 3 * CHUNK, LANES), BF16)
    send_other = pltpu.make_async_copy(other_ref, other_hbm, sems.at[2])
    send_mine = pltpu.make_async_copy(mine_ref, mine_hbm, sems.at[3])
    send_other.start()
    send_mine.start()
    send_wn.wait()
    send_g.wait()
    send_other.wait()
    send_mine.wait()


def tail_kernel(
    after_hbm, g_hbm, wn_hbm, w2_hbm, fw_ref, feat_ref, vg_ref,
    g_ref, wn_ref, w2_ref, gs, w1, acc, sems,
):
    fetches = [
        pltpu.make_async_copy(source, target, sems.at[i])
        for i, (source, target) in enumerate(
            ((g_hbm, g_ref), (wn_hbm, wn_ref), (w2_hbm, w2_ref))
        )
    ]
    for fetch in fetches:
        fetch.start()
    fill_weights(w1, fw_ref[...], True)
    fetches[0].wait()
    for j in range(4):
        tiles = [
            [g_ref[j, :, pl.ds((4 * y + q) * LANES, LANES)] for q in range(4)] for y in range(2)
        ]
        fill_windows(gs.at[j], tiles)
    for j in range(4):
        first, last = max(0, j - 1), min(2, j)
        for h in range(2):
            here = pl.ds(h * PAIR, PAIR)
            terms = dot(
                w1[h, pl.ds(first * PAIR, (last - first + 1) * PAIR), :],
                gs[j, pl.ds(h * WIN2, WIN2), :],
            )
            for a in range(first, last + 1):
                term = terms[(a - first) * PAIR : (a - first + 1) * PAIR]
                out = j - a
                if a == 0:
                    acc[out, here, :] = term
                else:
                    acc[out, here, :] += term
    merge = merge_matrix()
    for out in range(2):
        for y in range(2):
            cut = pl.ds(y * 256, 256)
            vg_ref[out, :, cut] = dot(acc[out, :, cut].astype(BF16), merge).astype(BF16)
    fetches[1].wait()
    fetches[2].wait()
    feat_ref[...] = dot_tn(w2_ref[...], wn_ref[...]).astype(BF16)


def add_kernel(mine_hbm, got_hbm, out_hbm, mine_ref, got_ref, sems):
    fetches = [
        pltpu.make_async_copy(mine_hbm, mine_ref, sems.at[0]),
        pltpu.make_async_copy(got_hbm, got_ref, sems.at[1]),
    ]
    for fetch in fetches:
        fetch.start()
    for fetch in fetches:
        fetch.wait()
    got_ref[...] = (mine_ref[...].astype(F32) + got_ref[...].astype(F32)).astype(BF16)
    send = pltpu.make_async_copy(got_ref, out_hbm, sems.at[0])
    send.start()
    send.wait()


def finish_kernel(factor, half_ref, rows_hbm, *refs):
    strided_hbm, grouped_hbm, rows_ref, strided_ref, grouped_ref, fetch_sem, send_sems = refs[-7:]
    half = half_ref[0]
    fetch = pltpu.make_async_copy(rows_hbm, rows_ref, fetch_sem)
    fetch.start()
    fetch.wait()
    sends = []
    for k in range(3):
        at = k * CHUNK
        here = pl.ds(k * PART, PART)
        strided_ref[here, pl.ds(0, LANES)] = rows_ref[pl.ds(at, PART), :].astype(F32) * factor
        rest = rows_ref[pl.ds(at + PART, LEFT), :].astype(F32) * factor
        strided_ref[pl.ds(k * PART, LEFT), pl.ds(LANES, 64)] = rest[:, :64]
        strided_ref[pl.ds(k * PART + LEFT, RIGHT), pl.ds(LANES, 64)] = rest[:RIGHT, 64:]
        there = pl.ds(pl.multiple_of(half * HALF + k * PART, 8), PART)
        sends.append(
            pltpu.make_async_copy(strided_ref.at[here], strided_hbm.at[there], send_sems.at[k])
        )
        sends[-1].start()
        for i in range(2):
            tile = rows_ref[pl.ds(at + PART + LEFT + i * F_PART, F_PART), :]
            grouped_ref[:, pl.ds((2 * k + i) * LANES, LANES)] = tile.astype(F32) * factor
    there = pl.ds(pl.multiple_of(half * F_PART, 8), F_PART)
    sends.append(pltpu.make_async_copy(grouped_ref, grouped_hbm.at[there], send_sems.at[3]))
    sends[-1].start()
    for send in sends:
        send.wait()


VMEM = pl.BlockSpec(memory_space=pltpu.VMEM)
SMEM = pl.BlockSpec(memory_space=pltpu.SMEM)
ANY = pl.BlockSpec(memory_space=pl.ANY)
MIB = 1024 * 1024


def again_call(own, after):
    return pl.pallas_call(
        again_kernel,
        out_shape=jax.ShapeDtypeStruct(own.shape, BF16),
        in_specs=[ANY, ANY],
        out_specs=ANY,
        scratch_shapes=[pltpu.SemaphoreType.DMA],
        compiler_params=pltpu.CompilerParams(vmem_limit_bytes=MIB),
        name="again",
    )(own, after)


def prepare_call(weight):
    return pl.pallas_call(
        prepare_kernel,
        out_shape=jax.ShapeDtypeStruct((2, 3 * PAIR, WIN2), BF16),
        in_specs=[VMEM],
        out_specs=ANY,
        scratch_shapes=[pltpu.VMEM((2, 3 * PAIR, WIN2), BF16), pltpu.SemaphoreType.DMA],
        compiler_params=pltpu.CompilerParams(vmem_limit_bytes=6 * MIB),
        name="prepare",
    )(weight)


def main_call(inner, core, far, own, twin, weight, w2):
    return pl.pallas_call(
        main_kernel,
        out_shape=(
            jax.ShapeDtypeStruct((ROWS, LANES), BF16),
            jax.ShapeDtypeStruct((ROWS, LANES), BF16),
            jax.ShapeDtypeStruct((TAPS * CH, LANES), BF16),
            jax.ShapeDtypeStruct((4, CH, 8 * LANES), BF16),
        ),
        in_specs=[SMEM, SMEM] + [ANY] * 5,
        out_specs=(ANY,) * 4,
        scratch_shapes=[
            pltpu.VMEM((2, 5, CH, 256), BF16),
            pltpu.VMEM((5, CH, 256), BF16),
            pltpu.VMEM((TAPS * CH, 192), BF16),
            pltpu.VMEM((ROWS, LANES), BF16),
            pltpu.VMEM((ROWS, LANES), BF16),
            pltpu.VMEM((TAPS * CH, LANES), BF16),
            pltpu.VMEM((4, CH, 8 * LANES), BF16),
            pltpu.VMEM((6, WIN, 512), BF16),
            pltpu.VMEM((2, 3 * PAIR, WIN2), BF16),
            pltpu.VMEM((4, CH, 512), F32),
            pltpu.VMEM((4, CH, 512), BF16),
            pltpu.VMEM((2, WIN, 512), BF16),
            pltpu.VMEM((768, 768), BF16),
            pltpu.VMEM((CH, 6 * LANES), BF16),
            pltpu.SemaphoreType.DMA((5,)),
        ],
        compiler_params=pltpu.CompilerParams(vmem_limit_bytes=24 * MIB),
        name="main",
    )(inner, core, far, own, twin, weight, w2)


def tail_call(after, grads, windows, w2, weight):
    return pl.pallas_call(
        tail_kernel,
        out_shape=(
            jax.ShapeDtypeStruct((192, LANES), BF16),
            jax.ShapeDtypeStruct((2, CH, 512), BF16),
        ),
        in_specs=[ANY, ANY, ANY, ANY, VMEM],
        out_specs=(VMEM,) * 2,
        scratch_shapes=[
            pltpu.VMEM((4, CH, 8 * LANES), BF16),
            pltpu.VMEM((TAPS * CH, LANES), BF16),
            pltpu.VMEM((TAPS * CH, 192), BF16),
            pltpu.VMEM((4, WIN, 512), BF16),
            pltpu.VMEM((2, 3 * PAIR, WIN2), BF16),
            pltpu.VMEM((2, CH, 512), F32),
            pltpu.SemaphoreType.DMA((3,)),
        ],
        compiler_params=pltpu.CompilerParams(vmem_limit_bytes=52 * MIB),
        cost_estimate=pl.CostEstimate(flops=10**9, bytes_accessed=4 * 10**6, transcendentals=0),
        name="tail",
    )(after, grads, windows, w2, weight)


def add_call(mine, got):
    return pl.pallas_call(
        add_kernel,
        out_shape=jax.ShapeDtypeStruct((ROWS, LANES), BF16),
        in_specs=[ANY, ANY],
        out_specs=ANY,
        scratch_shapes=[
            pltpu.VMEM((ROWS, LANES), BF16),
            pltpu.VMEM((ROWS, LANES), BF16),
            pltpu.SemaphoreType.DMA((2,)),
        ],
        compiler_params=pltpu.CompilerParams(vmem_limit_bytes=4 * MIB),
        name="add",
    )(mine, got)


def finish_call(factor, half, rows, before=()):
    return pl.pallas_call(
        functools.partial(finish_kernel, factor),
        out_shape=(
            jax.ShapeDtypeStruct((TAPS * CH, 192), F32),
            jax.ShapeDtypeStruct((CH, 6 * LANES), F32),
        ),
        in_specs=[SMEM, ANY] + [ANY] * len(before),
        out_specs=(ANY, ANY),
        scratch_shapes=[
            pltpu.VMEM((ROWS, LANES), BF16),
            pltpu.VMEM((HALF, 192), F32),
            pltpu.VMEM((F_PART, 6 * LANES), F32),
            pltpu.SemaphoreType.DMA,
            pltpu.SemaphoreType.DMA((4,)),
        ],
        input_output_aliases={2 + i: i for i in range(len(before))},
        compiler_params=pltpu.CompilerParams(vmem_limit_bytes=6 * MIB),
        name="finish",
    )(half, rows, *before)


def zero_kernel(after_hbm, out_ref):
    out_ref[0] = 0.0


def zero_call(after):
    return pl.pallas_call(
        zero_kernel,
        out_shape=jax.ShapeDtypeStruct((1,), F32),
        in_specs=[ANY],
        out_specs=SMEM,
        compiler_params=pltpu.CompilerParams(vmem_limit_bytes=MIB),
        name="zero",
    )(after)


def sum_pieces(parts):
    return jnp.sum(parts.astype(F32), axis=0).astype(BF16)


def to_all(piece, axes, count):
    copies = jnp.broadcast_to(piece[None], (count,) + piece.shape)
    return lax.all_to_all(copies, axes, 0, 0, tiled=True)


def shards(volume, first_weight, second_weight, out_cotangent):
    count = lax.axis_size(SPACE)
    planes = volume[0].transpose(1, 2, 0, 3).reshape(4, CH, 256)
    cotangent = out_cotangent.reshape(2, CH, LANES).transpose(1, 0, 2).reshape(1, CH, 256)
    own = jnp.concatenate([planes, cotangent], axis=0)
    swap = [(0, 1), (1, 0)]
    far = lax.ppermute(
        own,
        SPACE,
        [(i, i + 1) for i in range(1, count - 1, 2)] + [(i, i - 1) for i in range(2, count, 2)],
    )
    core = lax.axis_index("core").astype(jnp.int32).reshape(1)
    inner = jnp.where(lax.axis_index(SPACE) > 0, 1.0, 0.0).astype(F32).reshape(1)
    forward_weight = first_weight.transpose(1, 3, 2, 0).reshape(CH, PG * TAPS)
    twin = lax.ppermute(again_call(own, forward_weight), "core", swap)
    forward_weight = prepare_call(forward_weight)
    backward_weight = first_weight.transpose(1, 2, 3, 0).reshape(CH, PG * TAPS)
    w2 = second_weight.reshape(TAPS * CH, 192)
    mine, other, windows, grads = main_call(inner, core, far, own, twin, forward_weight, w2)
    chip = add_call(mine, lax.ppermute(other, "core", swap))
    parts = lax.all_to_all(chip.reshape(PIECES, PIECE, LANES), NEAR, 0, 0, tiled=True)
    piece = sum_pieces(parts)
    feat, vgrad = tail_call(piece, grads, windows, w2, backward_weight)
    features = feat.reshape(out_cotangent.shape)
    volume_grad = vgrad.reshape(2, CH, 2, 256).transpose(1, 0, 2, 3)
    parts = to_all(piece, "zh", lax.axis_size("zh"))
    piece = lax.reduce(parts.astype(F32), zero_call(volume_grad)[0], lax.add, (0,)).astype(BF16)
    own_half = to_all(piece, NEAR, PIECES).reshape(ROWS, LANES)
    other_half = lax.ppermute(own_half, "core", swap)
    factor = 1.0 / math.sqrt(lax.axis_size(DP) * lax.axis_size(SPACE) * LANES)
    halves = finish_call(factor, core, own_half)
    second_grad, narrow = finish_call(factor, 1 - core, other_half, halves)
    first_grad = narrow[:, : TAPS * PG].reshape(4, PG, PG, TAPS).transpose(3, 0, 1, 2)
    return (features, volume_grad[None], first_grad, second_grad.reshape(second_weight.shape))


def solution(mesh):
    fine = Mesh(mesh.devices.reshape(2, 8, 2, 2, 4, 2), ("xh", "zh", "zl", "xl", "y", "core"))
    split = P(DP, None, SPACE, None, None)
    return jax.shard_map(
        shards,
        mesh=fine,
        in_specs=(split, P(), P(), split),
        out_specs=(split, split, P(), P()),
        check_vma=False,
    )
```

```python
import functools
import math

import jax
import jax.numpy as jnp
from jax import lax
from jax.experimental import pallas as pl
from jax.experimental.pallas import tpu as pltpu
from jax.sharding import Mesh
from jax.sharding import PartitionSpec as P

SPACE = ("xl", "y", "core")
DP = ("xh", "zh", "zl")
NEAR = ("zl", "y", "xh", "xl")
F32 = jnp.float32
BF16 = jnp.bfloat16

CH = 96
PG = 24
TAPS = 27
WIN = 9 * CH
PAIR = CH // 2
WIN2 = 9 * PAIR
LANES = 128
HALF = TAPS * CH // 2
PART = HALF // 3
LEFT, RIGHT = 224, PART - 224
F_PART = CH // 2
CHUNK = PART + LEFT + 2 * F_PART
PIECES = 32
PIECE = 72
ROWS = PIECES * PIECE


def dot(a, b):
    return lax.dot_general(a, b, (((1,), (0,)), ((), ())), preferred_element_type=F32)


def dot_nt(a, b):
    return lax.dot_general(a, b, (((1,), (1,)), ((), ())), preferred_element_type=F32)


def dot_tn(a, b):
    return lax.dot_general(a, b, (((0,), (0,)), ((), ())), preferred_element_type=F32)


def later(tile):
    lane = lax.broadcasted_iota(jnp.int32, tile.shape, 1)
    return jnp.where(lane == 0, 0.0, pltpu.roll(tile, 1, 1))


def earlier(tile):
    lane = lax.broadcasted_iota(jnp.int32, tile.shape, 1)
    return jnp.where(lane == LANES - 1, 0.0, pltpu.roll(tile, LANES - 1, 1))


def fill_windows(ref, tiles):
    zero = jnp.zeros((CH, LANES), BF16)
    for b in range(3):
        for c in range(3):
            for y in range(2):
                source = y + b - 1
                if source in (0, 1):
                    even, odd, odd_later, even_earlier = tiles[source]
                    pair = ((odd_later, even), (even, odd), (odd, even_earlier))[c]
                else:
                    pair = (zero, zero)
                for h in range(2):
                    rows = pl.ds(h * WIN2 + (b * 3 + c) * PAIR, PAIR)
                    for parity in range(2):
                        ref[rows, pl.ds((2 * y + parity) * LANES, LANES)] = pair[parity][
                            h * PAIR : (h + 1) * PAIR
                        ]


def ones_where(condition):
    return jnp.where(condition, 1.0, 0.0).astype(BF16)


def split_matrix():
    z = lax.broadcasted_iota(jnp.int32, (256, LANES), 0)
    k2 = 2 * lax.broadcasted_iota(jnp.int32, (256, LANES), 1)
    return jnp.concatenate([ones_where(z == k2 + off) for off in (0, 1, -1, 2)], axis=1)


def merge_matrix():
    lane = lax.broadcasted_iota(jnp.int32, (LANES, 256), 0)
    z = lax.broadcasted_iota(jnp.int32, (LANES, 256), 1)
    return jnp.concatenate([ones_where(z == 2 * lane + bit) for bit in (0, 1)], axis=0)


def quotient(value, divisor, bits):
    return (value * (2**bits // divisor + 1)) >> bits


def fold_matrix():
    row = lax.broadcasted_iota(jnp.int32, (256, WIN2), 0)
    column = lax.broadcasted_iota(jnp.int32, (1, WIN2), 1)
    target = quotient(column, PAIR, 16) * PG + column - PG * quotient(column, PG, 16)
    return ones_where(row == target)


def group_mask():
    row = lax.broadcasted_iota(jnp.int32, (PAIR, WIN2), 0)
    column = lax.broadcasted_iota(jnp.int32, (1, WIN2), 1)
    offset = row - PG * quotient(column - PAIR * quotient(column, PAIR, 16), PG, 16)
    return (offset >= 0) & (offset < PG)


def order_matrix():
    row = lax.broadcasted_iota(jnp.int32, (3 * 256, 6 * LANES), 0)
    column = lax.broadcasted_iota(jnp.int32, (1, 6 * LANES), 1)
    channel = quotient(column, TAPS, 16)
    tap = column - TAPS * channel
    plane = quotient(tap, 9, 16)
    target = plane * 256 + (8 - tap + 9 * plane) * PG + channel
    return ones_where((row == target) & (column < PG * TAPS))


def fill_weights(w1, fw, flip):
    row = lax.broadcasted_iota(jnp.int32, (3 * 256, PG * TAPS), 0)
    column = lax.broadcasted_iota(jnp.int32, (1, PG * TAPS), 1)
    channel = quotient(column, TAPS, 16)
    tap = column - TAPS * channel
    if flip:
        tap = TAPS - 1 - tap
    plane = quotient(tap, 9, 16)
    order = ones_where(row == plane * 256 + (tap - 9 * plane) * PG + channel)
    narrow = dot_nt(fw, order).astype(BF16)
    mask = group_mask()
    fold = fold_matrix()
    for h in range(2):
        for a in range(3):
            block = dot(narrow[h * PAIR : (h + 1) * PAIR, a * 256 : (a + 1) * 256], fold)
            w1[h, pl.ds(a * PAIR, PAIR), :] = jnp.where(mask, block, 0.0).astype(BF16)


def again_kernel(own_hbm, after_hbm, again_hbm, sem):
    copy = pltpu.make_async_copy(own_hbm, again_hbm, sem)
    copy.start()
    copy.wait()


def prepare_kernel(fw_ref, w1_hbm, w1, sem):
    fill_weights(w1, fw_ref[...], False)
    send = pltpu.make_async_copy(w1, w1_hbm, sem)
    send.start()
    send.wait()


def cotangent_of(slab):
    return jnp.concatenate([slab[4, :, :LANES], slab[4, :, LANES:]], axis=0)


def main_kernel(
    inner_ref, core_ref, far_hbm, own_hbm, twin_hbm, w1_hbm, w2_hbm,
    mine_hbm, other_hbm, wn_hbm, g_hbm,
    beside, own_ref, w2_ref, mine_ref, other_ref, wn_ref, g_ref,
    xs, w1, pre_ref, xc_ref, gs, order_ref, fg, sems,
):
    inner = inner_ref[0]
    core = core_ref[0]
    low_ref, high_ref = beside.at[0], beside.at[1]
    fetches = [
        pltpu.make_async_copy(own_hbm, own_ref, sems.at[0]),
        pltpu.make_async_copy(far_hbm, beside.at[core], sems.at[1]),
        pltpu.make_async_copy(twin_hbm, beside.at[1 - core], sems.at[2]),
        pltpu.make_async_copy(w1_hbm, w1, sems.at[3]),
        pltpu.make_async_copy(w2_hbm, w2_ref, sems.at[4]),
    ]
    for fetch in fetches:
        fetch.start()
    split = split_matrix()
    mask = group_mask()
    fetches[0].wait()
    for e in (2, 3, 0, 1, 4, 5):
        slab = (low_ref, own_ref, high_ref)[e // 2]
        if e == 0:
            fetches[1].wait()
            fetches[2].wait()
        tiles = []
        for y in range(2):
            parts = dot(slab[2 * (e % 2) + y], split).astype(BF16)
            tiles.append([parts[:, q * LANES : (q + 1) * LANES] for q in range(4)])
            if 1 <= e <= 4:
                xc_ref[e - 1, :, pl.ds(y * 256, 256)] = parts[:, :256]
        fill_windows(xs.at[e], tiles)
    fetches[3].wait()
    for e in range(6):
        first, last = max(0, e - 3), min(2, e)
        for h in range(2):
            here = pl.ds(h * PAIR, PAIR)
            terms = dot(
                w1[h, pl.ds(first * PAIR, (last - first + 1) * PAIR), :],
                xs[e, pl.ds(h * WIN2, WIN2), :],
            )
            for a in range(first, last + 1):
                term = terms[(a - first) * PAIR : (a - first + 1) * PAIR]
                j = e - a
                if a == 0:
                    pre_ref[j, here, :] = term
                else:
                    pre_ref[j, here, :] += term
    zero = jnp.zeros((CH, LANES), BF16)
    for a in range(3):
        for c in range(3):
            wn_ref[pl.ds((9 * a + c) * CH, CH), :] = zero
        for y in range(2):
            value = pre_ref[a, :, pl.ds(y * 256, 256)]
            hidden = value * jax.nn.sigmoid(value)
            if a == 0:
                hidden = hidden * inner
            even, odd = hidden[:, :LANES], hidden[:, LANES:]
            base = (9 * a + 3 * (y + 1)) * CH
            wn_ref[pl.ds(base, CH), :] = later(odd).astype(BF16)
            wn_ref[pl.ds(base + CH, CH), :] = even.astype(BF16)
            wn_ref[pl.ds(base + 2 * CH, CH), :] = odd.astype(BF16)
    send_wn = pltpu.make_async_copy(wn_ref, wn_hbm, sems.at[0])
    send_wn.start()
    cot = cotangent_of(own_ref)
    rest = cot[LANES:]
    none = jnp.zeros_like(rest)
    both = jnp.concatenate(
        [jnp.concatenate([rest, none], axis=1), jnp.concatenate([none, rest], axis=1)], axis=0
    )
    fill = jnp.zeros((LEFT - RIGHT, LANES), BF16)
    for out_ref, half in ((other_ref, 1 - core), (mine_ref, core)):
        for k in range(3):
            base = pl.multiple_of(half * HALF + k * PART, 16)
            wide = dot_nt(wn_ref[pl.ds(base, PART), :], cot[:LANES])
            out_ref[pl.ds(k * CHUNK, PART), :] = wide.astype(BF16)
            left = wn_ref[pl.ds(base, LEFT), :]
            right = jnp.concatenate([wn_ref[pl.ds(base + LEFT, RIGHT), :], fill], axis=0)
            pairs = jnp.concatenate([left, right], axis=1)
            out_ref[pl.ds(k * CHUNK + PART, LEFT), :] = dot_nt(pairs, both).astype(BF16)
    with_above = jnp.concatenate([cot, cotangent_of(high_ref)], axis=1)
    with_below = jnp.concatenate([cot, cotangent_of(low_ref)], axis=1)
    order_ref[...] = order_matrix()
    fetches[4].wait()
    spread = [
        dot(w2_ref[pl.ds((9 * a + 3) * CH, 6 * CH), :], with_below if a == 2 else with_above)
        for a in range(3)
    ]
    for j in range(4):
        sources = {0: ((0, 0), (2, 1)), 1: ((1, 0),), 2: ((2, 0), (0, 1)), 3: ((1, 1),)}[j]
        tiles = []
        for y in range(2):
            got = []
            for c in range(3):
                total = None
                for a, part in sources:
                    tile = spread[a][
                        (3 * y + c) * CH : (3 * y + c + 1) * CH, part * LANES : (part + 1) * LANES
                    ]
                    total = tile if total is None else total + tile
                got.append(total)
            even = got[1]
            odd = got[2] + earlier(got[0])
            value = pre_ref[j, :, pl.ds(y * 256, 256)]
            sigma = jax.nn.sigmoid(value)
            slope = sigma * (1.0 + value * (1.0 - sigma))
            if j == 0:
                slope = slope * inner
            even = even * slope[:, :LANES]
            odd = odd * slope[:, LANES:]
            tiles.append([t.astype(BF16) for t in (even, odd, later(odd), earlier(even))])
            for q in range(4):
                g_ref[j, :, pl.ds((4 * y + q) * LANES, LANES)] = tiles[y][q]
        if j in (1, 2):
            fill_windows(gs.at[j - 1], tiles)
    send_g = pltpu.make_async_copy(g_ref, g_hbm, sems.at[1])
    send_g.start()
    fold = fold_matrix()
    narrow = []
    for h in range(2):
        here = pl.ds(h * PAIR, PAIR)
        taps = None
        for j in (1, 2):
            planes = jnp.concatenate([xc_ref[j + a, here, :] for a in (-1, 0, 1)], axis=0)
            term = dot_nt(planes, gs[j - 1, pl.ds(h * WIN2, WIN2), :])
            taps = term if taps is None else taps + term
        kept = [
            jnp.where(mask, taps[a * PAIR : (a + 1) * PAIR], 0.0).astype(BF16) for a in range(3)
        ]
        narrow.append(dot_nt(jnp.concatenate(kept, axis=0), fold).astype(BF16))
    ordered = dot(
        jnp.concatenate(
            [
                jnp.concatenate([part[a * PAIR : (a + 1) * PAIR] for part in narrow], axis=0)
                for a in range(3)
            ],
            axis=1,
        ),
        order_ref[...],
    )
    fg[...] = ordered.astype(BF16)
    for out_ref, half in ((other_ref, 1 - core), (mine_ref, core)):
        base = pl.multiple_of(half * F_PART, 16)
        for k in range(6):
            at = (k // 2) * CHUNK + PART + LEFT + (k % 2) * F_PART
            out_ref[pl.ds(at, F_PART), :] = fg[pl.ds(base, F_PART), pl.ds(k * LANES, LANES)]
        out_ref[pl.ds(3 * CHUNK, ROWS - 3 * CHUNK), :] = jnp.zeros((ROWS - 3 * CHUNK, LANES), BF16)
    send_other = pltpu.make_async_copy(other_ref, other_hbm, sems.at[2])
    send_mine = pltpu.make_async_copy(mine_ref, mine_hbm, sems.at[3])
    send_other.start()
    send_mine.start()
    send_wn.wait()
    send_g.wait()
    send_other.wait()
    send_mine.wait()


def tail_kernel(
    after_hbm, g_hbm, wn_hbm, w2_hbm, fw_ref, feat_ref, vg_ref,
    g_ref, wn_ref, w2_ref, gs, w1, acc, sems,
):
    fetches = [
        pltpu.make_async_copy(source, target, sems.at[i])
        for i, (source, target) in enumerate(
            ((g_hbm, g_ref), (wn_hbm, wn_ref), (w2_hbm, w2_ref))
        )
    ]
    for fetch in fetches:
        fetch.start()
    fill_weights(w1, fw_ref[...], True)
    fetches[0].wait()
    for j in range(4):
        tiles = [
            [g_ref[j, :, pl.ds((4 * y + q) * LANES, LANES)] for q in range(4)] for y in range(2)
        ]
        fill_windows(gs.at[j], tiles)
    for j in range(4):
        first, last = max(0, j - 1), min(2, j)
        for h in range(2):
            here = pl.ds(h * PAIR, PAIR)
            terms = dot(
                w1[h, pl.ds(first * PAIR, (last - first + 1) * PAIR), :],
                gs[j, pl.ds(h * WIN2, WIN2), :],
            )
            for a in range(first, last + 1):
                term = terms[(a - first) * PAIR : (a - first + 1) * PAIR]
                out = j - a
                if a == 0:
                    acc[out, here, :] = term
                else:
                    acc[out, here, :] += term
    merge = merge_matrix()
    for out in range(2):
        for y in range(2):
            cut = pl.ds(y * 256, 256)
            vg_ref[out, :, cut] = dot(acc[out, :, cut].astype(BF16), merge).astype(BF16)
    fetches[1].wait()
    fetches[2].wait()
    feat_ref[...] = dot_tn(w2_ref[...], wn_ref[...]).astype(BF16)


def add_kernel(mine_hbm, got_hbm, out_hbm, mine_ref, got_ref, sems):
    fetches = [
        pltpu.make_async_copy(mine_hbm, mine_ref, sems.at[0]),
        pltpu.make_async_copy(got_hbm, got_ref, sems.at[1]),
    ]
    for fetch in fetches:
        fetch.start()
    for fetch in fetches:
        fetch.wait()
    got_ref[...] = (mine_ref[...].astype(F32) + got_ref[...].astype(F32)).astype(BF16)
    send = pltpu.make_async_copy(got_ref, out_hbm, sems.at[0])
    send.start()
    send.wait()


def finish_kernel(factor, half_ref, rows_hbm, *refs):
    strided_hbm, grouped_hbm, rows_ref, strided_ref, grouped_ref, fetch_sem, send_sems = refs[-7:]
    half = half_ref[0]
    fetch = pltpu.make_async_copy(rows_hbm, rows_ref, fetch_sem)
    fetch.start()
    fetch.wait()
    sends = []
    for k in range(3):
        at = k * CHUNK
        here = pl.ds(k * PART, PART)
        strided_ref[here, pl.ds(0, LANES)] = rows_ref[pl.ds(at, PART), :].astype(F32) * factor
        rest = rows_ref[pl.ds(at + PART, LEFT), :].astype(F32) * factor
        strided_ref[pl.ds(k * PART, LEFT), pl.ds(LANES, 64)] = rest[:, :64]
        strided_ref[pl.ds(k * PART + LEFT, RIGHT), pl.ds(LANES, 64)] = rest[:RIGHT, 64:]
        there = pl.ds(pl.multiple_of(half * HALF + k * PART, 8), PART)
        sends.append(
            pltpu.make_async_copy(strided_ref.at[here], strided_hbm.at[there], send_sems.at[k])
        )
        sends[-1].start()
        for i in range(2):
            tile = rows_ref[pl.ds(at + PART + LEFT + i * F_PART, F_PART), :]
            grouped_ref[:, pl.ds((2 * k + i) * LANES, LANES)] = tile.astype(F32) * factor
    there = pl.ds(pl.multiple_of(half * F_PART, 8), F_PART)
    sends.append(pltpu.make_async_copy(grouped_ref, grouped_hbm.at[there], send_sems.at[3]))
    sends[-1].start()
    for send in sends:
        send.wait()


VMEM = pl.BlockSpec(memory_space=pltpu.VMEM)
SMEM = pl.BlockSpec(memory_space=pltpu.SMEM)
ANY = pl.BlockSpec(memory_space=pl.ANY)
MIB = 1024 * 1024


def again_call(own, after):
    return pl.pallas_call(
        again_kernel,
        out_shape=jax.ShapeDtypeStruct(own.shape, BF16),
        in_specs=[ANY, ANY],
        out_specs=ANY,
        scratch_shapes=[pltpu.SemaphoreType.DMA],
        compiler_params=pltpu.CompilerParams(vmem_limit_bytes=MIB),
        name="again",
    )(own, after)


def prepare_call(weight):
    return pl.pallas_call(
        prepare_kernel,
        out_shape=jax.ShapeDtypeStruct((2, 3 * PAIR, WIN2), BF16),
        in_specs=[VMEM],
        out_specs=ANY,
        scratch_shapes=[pltpu.VMEM((2, 3 * PAIR, WIN2), BF16), pltpu.SemaphoreType.DMA],
        compiler_params=pltpu.CompilerParams(vmem_limit_bytes=6 * MIB),
        name="prepare",
    )(weight)


def main_call(inner, core, far, own, twin, weight, w2):
    return pl.pallas_call(
        main_kernel,
        out_shape=(
            jax.ShapeDtypeStruct((ROWS, LANES), BF16),
            jax.ShapeDtypeStruct((ROWS, LANES), BF16),
            jax.ShapeDtypeStruct((TAPS * CH, LANES), BF16),
            jax.ShapeDtypeStruct((4, CH, 8 * LANES), BF16),
        ),
        in_specs=[SMEM, SMEM] + [ANY] * 5,
        out_specs=(ANY,) * 4,
        scratch_shapes=[
            pltpu.VMEM((2, 5, CH, 256), BF16),
            pltpu.VMEM((5, CH, 256), BF16),
            pltpu.VMEM((TAPS * CH, 192), BF16),
            pltpu.VMEM((ROWS, LANES), BF16),
            pltpu.VMEM((ROWS, LANES), BF16),
            pltpu.VMEM((TAPS * CH, LANES), BF16),
            pltpu.VMEM((4, CH, 8 * LANES), BF16),
            pltpu.VMEM((6, WIN, 512), BF16),
            pltpu.VMEM((2, 3 * PAIR, WIN2), BF16),
            pltpu.VMEM((4, CH, 512), F32),
            pltpu.VMEM((4, CH, 512), BF16),
            pltpu.VMEM((2, WIN, 512), BF16),
            pltpu.VMEM((768, 768), BF16),
            pltpu.VMEM((CH, 6 * LANES), BF16),
            pltpu.SemaphoreType.DMA((5,)),
        ],
        compiler_params=pltpu.CompilerParams(vmem_limit_bytes=24 * MIB),
        name="main",
    )(inner, core, far, own, twin, weight, w2)


def tail_call(after, grads, windows, w2, weight):
    return pl.pallas_call(
        tail_kernel,
        out_shape=(
            jax.ShapeDtypeStruct((192, LANES), BF16),
            jax.ShapeDtypeStruct((2, CH, 512), BF16),
        ),
        in_specs=[ANY, ANY, ANY, ANY, VMEM],
        out_specs=(VMEM,) * 2,
        scratch_shapes=[
            pltpu.VMEM((4, CH, 8 * LANES), BF16),
            pltpu.VMEM((TAPS * CH, LANES), BF16),
            pltpu.VMEM((TAPS * CH, 192), BF16),
            pltpu.VMEM((4, WIN, 512), BF16),
            pltpu.VMEM((2, 3 * PAIR, WIN2), BF16),
            pltpu.VMEM((2, CH, 512), F32),
            pltpu.SemaphoreType.DMA((3,)),
        ],
        compiler_params=pltpu.CompilerParams(vmem_limit_bytes=52 * MIB),
        cost_estimate=pl.CostEstimate(flops=10**9, bytes_accessed=4 * 10**6, transcendentals=0),
        name="tail",
    )(after, grads, windows, w2, weight)


def add_call(mine, got):
    return pl.pallas_call(
        add_kernel,
        out_shape=jax.ShapeDtypeStruct((ROWS, LANES), BF16),
        in_specs=[ANY, ANY],
        out_specs=ANY,
        scratch_shapes=[
            pltpu.VMEM((ROWS, LANES), BF16),
            pltpu.VMEM((ROWS, LANES), BF16),
            pltpu.SemaphoreType.DMA((2,)),
        ],
        compiler_params=pltpu.CompilerParams(vmem_limit_bytes=4 * MIB),
        name="add",
    )(mine, got)


def finish_call(factor, half, rows, before=()):
    return pl.pallas_call(
        functools.partial(finish_kernel, factor),
        out_shape=(
            jax.ShapeDtypeStruct((TAPS * CH, 192), F32),
            jax.ShapeDtypeStruct((CH, 6 * LANES), F32),
        ),
        in_specs=[SMEM, ANY] + [ANY] * len(before),
        out_specs=(ANY, ANY),
        scratch_shapes=[
            pltpu.VMEM((ROWS, LANES), BF16),
            pltpu.VMEM((HALF, 192), F32),
            pltpu.VMEM((F_PART, 6 * LANES), F32),
            pltpu.SemaphoreType.DMA,
            pltpu.SemaphoreType.DMA((4,)),
        ],
        input_output_aliases={2 + i: i for i in range(len(before))},
        compiler_params=pltpu.CompilerParams(vmem_limit_bytes=6 * MIB),
        name="finish",
    )(half, rows, *before)


def zero_kernel(after_hbm, out_ref):
    out_ref[0] = 0.0


def zero_call(after):
    return pl.pallas_call(
        zero_kernel,
        out_shape=jax.ShapeDtypeStruct((1,), F32),
        in_specs=[ANY],
        out_specs=SMEM,
        compiler_params=pltpu.CompilerParams(vmem_limit_bytes=MIB),
        name="zero",
    )(after)


def sum_pieces(parts):
    return jnp.sum(parts.astype(F32), axis=0).astype(BF16)


def to_all(piece, axes, count):
    copies = jnp.broadcast_to(piece[None], (count,) + piece.shape)
    return lax.all_to_all(copies, axes, 0, 0, tiled=True)


def shards(volume, first_weight, second_weight, out_cotangent):
    count = lax.axis_size(SPACE)
    planes = volume[0].transpose(1, 2, 0, 3).reshape(4, CH, 256)
    cotangent = out_cotangent.reshape(2, CH, LANES).transpose(1, 0, 2).reshape(1, CH, 256)
    own = jnp.concatenate([planes, cotangent], axis=0)
    swap = [(0, 1), (1, 0)]
    far = lax.ppermute(
        own,
        SPACE,
        [(i, i + 1) for i in range(1, count - 1, 2)] + [(i, i - 1) for i in range(2, count, 2)],
    )
    core = lax.axis_index("core").astype(jnp.int32).reshape(1)
    inner = jnp.where(lax.axis_index(SPACE) > 0, 1.0, 0.0).astype(F32).reshape(1)
    forward_weight = first_weight.transpose(1, 3, 2, 0).reshape(CH, PG * TAPS)
    twin = lax.ppermute(again_call(own, forward_weight), "core", swap)
    forward_weight = prepare_call(forward_weight)
    backward_weight = first_weight.transpose(1, 2, 3, 0).reshape(CH, PG * TAPS)
    w2 = second_weight.reshape(TAPS * CH, 192)
    mine, other, windows, grads = main_call(inner, core, far, own, twin, forward_weight, w2)
    chip = add_call(mine, lax.ppermute(other, "core", swap))
    parts = lax.all_to_all(chip.reshape(PIECES, PIECE, LANES), NEAR, 0, 0, tiled=True)
    piece = sum_pieces(parts)
    feat, vgrad = tail_call(piece, grads, windows, w2, backward_weight)
    features = feat.reshape(out_cotangent.shape)
    volume_grad = vgrad.reshape(2, CH, 2, 256).transpose(1, 0, 2, 3)
    parts = to_all(piece, "zh", lax.axis_size("zh"))
    piece = lax.reduce(parts.astype(F32), zero_call(volume_grad)[0], lax.add, (0,)).astype(BF16)
    own_half = to_all(piece, NEAR, PIECES).reshape(ROWS, LANES)
    other_half = lax.ppermute(own_half, "core", swap)
    factor = 1.0 / math.sqrt(lax.axis_size(DP) * lax.axis_size(SPACE) * LANES)
    halves = finish_call(factor, core, own_half)
    second_grad, narrow = finish_call(factor, 1 - core, other_half, halves)
    first_grad = narrow[:, : TAPS * PG].reshape(4, PG, PG, TAPS).transpose(3, 0, 1, 2)
    return (features, volume_grad[None], first_grad, second_grad.reshape(second_weight.shape))


def solution(mesh):
    fine = Mesh(mesh.devices.reshape(2, 8, 2, 2, 4, 2), ("xh", "zh", "zl", "xl", "y", "core"))
    split = P(DP, None, SPACE, None, None)
    return jax.shard_map(
        shards,
        mesh=fine,
        in_specs=(split, P(), P(), split),
        out_specs=(split, split, P(), P()),
        check_vma=False,
    )
```
